32 devices in a mesh: vol: 4 (over z), win: 8 (over y, x, core).
Axes of the slice: x: 2, y: 2, z: 4, core: 2. Of those that a mesh axis runs over, the one named last changes fastest.
Arguments:
- tokens: bfloat16 [16, 32, 343, 96], P(None, ('vol', 'win')), may hold values from -6 to 6
- cotangent: bfloat16 [16, 32, 343, 96], P(None, ('vol', 'win')), may hold values from -6 to 6
- position_bias: bfloat16 [2, 6, 343, 343], replicated, may hold values from -4 to 4
- window_volume: int32 [16, 32], P(None, ('vol', 'win')), may hold values from 0 to 7, as said below
- clip_extent: int32 [16, 32, 3], P(None, ('vol', 'win')), may hold values from 2 to 7, as said below
- master: float32 [223488], P(('vol', 'win'))
- first_moment: float32 [223488], P(('vol', 'win'))
- second_moment: float32 [223488], P(('vol', 'win')), as said below
Outputs:
- output: bfloat16 [16, 32, 343, 96], P(None, ('vol', 'win'))
- input_grad: float32 [16, 32, 343, 96], P(None, ('vol', 'win'))
- new_master: float32 [223488], P(('vol', 'win'))
- new_first: float32 [223488], P(('vol', 'win'))
- new_second: float32 [223488], P(('vol', 'win'))
- new_copy: bfloat16 [223488], P(('vol', 'win'))
The draws below stay inside these ranges and needn't reach their ends.
Inputs may be any that keep to these rules, and one draw needn't show every extreme that they name: `window_volume`: windows of one micro-batch and one group with equal labels belong to one volume, which covers a box of places of the group's grid. `clip_extent`: a window has 7 voxels along a dimension unless it is the last of its volume along it. `second_moment`: positive.
All inputs are finite; a program needn't handle non-finite values.
Results may differ from the reference program's by a relative error of at most 0.012.
The reference program's roundings to bfloat16 on the way (of `roll`, `weights` and `attended`) count: a program that leaves them out, or rounds other values in their place, can miss the bound.
Values may be sent and summed in bfloat16 or wider, within the bound.
A program may use at most 384 MiB of HBM per device.

```python
import math
import jax
import jax.numpy as jnp
from jax import lax

C = 96
HEADS = 6
HEAD_DIM = 16
FF = 384
SIDE = 7
SHIFT = 3
WS = 343
MB = 16
STEP = 6
NW = 32
NPARAM = 223488
N_VOL = 4
N_WIN = 8


def volume_cuts(key):
    groups_a = N_WIN // 4
    starts = jax.random.randint(jax.random.fold_in(key, 101), (MB, N_VOL, groups_a), 0, 2)
    starts = starts.at[:, :, 0].set(1)
    starts = starts.at[0, 0, :].set(1)
    splits = jax.random.randint(jax.random.fold_in(key, 102), (MB, N_VOL, 2), 0, 2)
    splits = splits.at[0, 0, :].set(1)
    return (starts.astype(jnp.int32), splits.astype(jnp.int32))


def draw_window_volume(key, part):
    starts, splits = volume_cuts(key)
    along_a = jnp.cumsum(starts, axis=2) - 1
    halves = jnp.arange(2, dtype=jnp.int32)
    along_b = splits[:, :, 0, None] * halves[None, None, :]
    along_c = splits[:, :, 1, None] * halves[None, None, :]
    labels = (along_a[:, :, :, None, None] * 2 + along_b[:, :, None, :, None]) * 2 + along_c[:, :, None, None, :]
    return labels.reshape(MB, N_VOL * N_WIN).astype(jnp.int32)


def draw_clip_extent(key, part):
    starts, splits = volume_cuts(key)
    key = jax.random.fold_in(key, 4)
    groups_a = N_WIN // 4
    ending = jnp.ones((MB, N_VOL, 1), jnp.int32)
    last_a = jnp.concatenate((starts[:, :, 1:], ending), axis=2)
    halves = jnp.arange(2, dtype=jnp.int32)
    last_b = jnp.maximum(splits[:, :, 0, None], halves[None, None, :])
    last_c = jnp.maximum(splits[:, :, 1, None], halves[None, None, :])
    grid_shape = (MB, N_VOL, groups_a, 2, 2)
    flags = jnp.stack((jnp.broadcast_to(last_a[:, :, :, None, None], grid_shape), jnp.broadcast_to(last_b[:, :, None, :, None], grid_shape), jnp.broadcast_to(last_c[:, :, None, None, :], grid_shape)), axis=-1)
    clipped = jax.random.randint(key, grid_shape + (3,), 2, SIDE + 1)
    extent = jnp.where(flags > 0, clipped, SIDE)
    extent = extent.at[0, 0, 0, 0, 0, 0].set(2)
    return extent.reshape(MB, N_VOL * N_WIN, 3).astype(jnp.int32)


def region_bounds():
    return (3 * C * C, 4 * C * C, 4 * C * C + C * FF, 4 * C * C + 2 * C * FF)


def entry_position():
    block_len = 4 * C * C + 2 * C * FF + 8 * C + FF
    return jnp.arange(NPARAM, dtype=jnp.int32) % block_len


def gradient_size():
    position = entry_position()
    qkv_end, proj_end, up_end, down_end = region_bounds()
    factor = jnp.where(position < up_end, 0.3, jnp.where(position < down_end, 0.5, 1.0))
    return factor * math.sqrt(MB * N_VOL * N_WIN * SIDE ** 3)


def draw_master(key, part):
    key = jax.random.fold_in(key, 5)
    position = entry_position()
    qkv_end, proj_end, up_end, down_end = region_bounds()
    spread = jnp.where(position < qkv_end, C ** (-0.5), jnp.where(position < proj_end, 3.0 * C ** (-0.5), jnp.where(position < up_end, C ** (-0.5), FF ** (-0.5))))
    normal_part = jnp.clip(jax.random.normal(jax.random.fold_in(key, 1), (NPARAM,), jnp.float32), -5.0, 5.0)
    vector_slot = position - down_end
    is_gain = (vector_slot >= 0) & (vector_slot < C) | (vector_slot >= 5 * C) & (vector_slot < 6 * C)
    gain_value = jax.random.uniform(jax.random.fold_in(key, 2), (NPARAM,), jnp.float32, 0.6, 1.4)
    vector_value = jnp.where(is_gain, gain_value, 0.3 * normal_part)
    return jnp.where(position < down_end, spread * normal_part, vector_value).astype(jnp.float32)


def draw_first_moment(key, part):
    key = jax.random.fold_in(key, 6)
    normal_part = jnp.clip(jax.random.normal(key, (NPARAM,), jnp.float32), -4.0, 4.0)
    return (gradient_size() * normal_part).astype(jnp.float32)


def draw_second_moment(key, part):
    key = jax.random.fold_in(key, 7)
    factor = jnp.exp(jax.random.uniform(key, (NPARAM,), jnp.float32, 0.0, math.log(4.0)))
    size_now = gradient_size()
    return (size_now * size_now * factor).astype(jnp.float32)


def steps_of(key, shape, shards, least, top_value):
    level, own = 1.0, jax.random.fold_in(key, 6)
    for dim, parts in shards:
        heights = jnp.exp(jax.random.uniform(jax.random.fold_in(own, dim), (parts,), jnp.float32, least / len(shards), top_value / len(shards)))
        level = level * jnp.repeat(heights, shape[dim] // parts).reshape([-1 if axis == dim else 1 for axis in range(len(shape))])
    return level


def bell_draw(key, dims, deviation, bound, cuts=(), kind=jnp.bfloat16):
    values = jax.random.normal(key, dims, jnp.float32) * deviation
    if len(cuts) > 0:
        values = steps_of(key, dims, cuts, -0.22, 0.18) * values
    return jnp.clip(values, min=-bound, max=bound).astype(kind)


def setup_inputs(seed: int = 0) -> dict:
    keys = jax.random.split(jax.random.key(seed), 9)
    return {
        "tokens": bell_draw(keys[0], (MB, NW, WS, C), 1.0, 6.0, ((1, 32),)),
        "cotangent": bell_draw(keys[1], (MB, NW, WS, C), 1.0, 6.0, ((1, 32),)),
        "position_bias": bell_draw(keys[2], (2, HEADS, WS, WS), 1.0, 4.0),
        "window_volume": draw_window_volume(jax.random.fold_in(keys[8], 71), 0),
        "clip_extent": draw_clip_extent(jax.random.fold_in(keys[8], 71), 0),
        "master": draw_master(jax.random.fold_in(keys[8], 71), 0),
        "first_moment": draw_first_moment(jax.random.fold_in(keys[8], 71), 0),
        "second_moment": draw_second_moment(jax.random.fold_in(keys[8], 71), 0),
    }


NORM_EPS = 1e-05
MASK_FILL = -1000000000.0
BETA_FIRST = 0.5
BETA_SECOND = 0.5
ADAM_EPS = 1e-08
RATE_MATRIX = 0.1
RATE_VECTOR = 0.4
DECAY_MATRIX = 0.05
HIGHEST = lax.Precision.HIGHEST

@jax.custom_vjp
def low(v):
    return lax.optimization_barrier(v.astype(jnp.bfloat16)).astype(jnp.float32)

@jax.custom_vjp
def low_back(v):
    return v

def low_keep(v):
    return (low(v), None)

def low_pass(kept, grad):
    return (grad,)

def back_keep(v):
    return (v, None)

def back_low(kept, grad):
    return (low(grad),)
low.defvjp(low_keep, low_pass)
low_back.defvjp(back_keep, back_low)

def layer_norm(values, gain_vec, offset_vec):
    centred = values - lax.optimization_barrier(jnp.mean(values, axis=-1, keepdims=True))
    scaled = centred * lax.rsqrt(lax.optimization_barrier(jnp.mean(centred * centred, axis=-1, keepdims=True)) + NORM_EPS)
    return scaled * gain_vec + offset_vec

def block_length():
    return 4 * C * C + 2 * C * FF + 8 * C + FF

def unpack(params, which_layer):
    start_at = which_layer * block_length()
    w_qkv = params[start_at:start_at + 3 * C * C].reshape(C, 3 * C)
    start_at = start_at + 3 * C * C
    w_proj = params[start_at:start_at + C * C].reshape(C, C)
    start_at = start_at + C * C
    w_up = params[start_at:start_at + C * FF].reshape(C, FF)
    start_at = start_at + C * FF
    w_down = params[start_at:start_at + FF * C].reshape(FF, C)
    start_at = start_at + FF * C
    vectors = params[start_at:start_at + 8 * C + FF]
    return (w_qkv, w_proj, w_up, w_down, vectors)

def to_grid(windows):
    leading = windows.shape[0]
    channels = windows.shape[-1]
    shaped = windows.reshape(leading, N_VOL, N_WIN // 4, 2, 2, SIDE, SIDE, SIDE, channels)
    shaped = shaped.transpose(0, 1, 2, 5, 3, 6, 4, 7, 8)
    return shaped.reshape(leading, N_VOL, N_WIN // 4 * SIDE, 2 * SIDE, 2 * SIDE, channels)

def from_grid(grid):
    leading = grid.shape[0]
    channels = grid.shape[-1]
    shaped = grid.reshape(leading, N_VOL, N_WIN // 4, SIDE, 2, SIDE, 2, SIDE, channels)
    shaped = shaped.transpose(0, 1, 2, 4, 6, 3, 5, 7, 8)
    return shaped.reshape(leading, N_VOL * N_WIN, WS, channels)

def roll_windows(windows, amount):
    return from_grid(jnp.roll(to_grid(windows), amount, axis=(2, 3, 4)))

def wrap_code(leading):
    along_a = jnp.arange(N_WIN // 4 * SIDE, dtype=jnp.int32)
    along_b = jnp.arange(2 * SIDE, dtype=jnp.int32)
    wrapped_a = (jnp.roll(along_a, -SHIFT) < along_a).astype(jnp.int32)
    wrapped_b = (jnp.roll(along_b, -SHIFT) < along_b).astype(jnp.int32)
    pattern = wrapped_a[:, None, None] * 4 + wrapped_b[None, :, None] * 2 + wrapped_b[None, None, :]
    grid = jnp.broadcast_to(pattern[None, None, :, :, :, None], (leading, N_VOL) + pattern.shape + (1,))
    return from_grid(grid)[..., 0]

def window_masks(window_volume, clip_extent):
    coords = jnp.arange(SIDE, dtype=jnp.int32)
    inside = (coords[:, None, None] < clip_extent[:, :, 0, None, None, None]) & (coords[None, :, None] < clip_extent[:, :, 1, None, None, None]) & (coords[None, None, :] < clip_extent[:, :, 2, None, None, None])
    key_valid = inside.reshape(MB, N_VOL * N_WIN, WS).astype(jnp.int32)
    labels = jnp.broadcast_to(window_volume[:, :, None], key_valid.shape).astype(jnp.int32)
    return (key_valid, labels)

def attend_block(queries, key_heads, values, bias_table, key_valid, labels):
    raw = jnp.einsum('wqhd,wkhd->whqk', queries, key_heads, precision=HIGHEST)
    scores = low_back(raw) * HEAD_DIM ** (-0.5) + bias_table[None]
    same_region = labels[:, :, None] == labels[:, None, :]
    allowed = same_region & (key_valid[:, None, :] > 0) | jnp.eye(WS, dtype=bool)[None]
    scores = jnp.where(allowed[:, None], scores, MASK_FILL)
    softmax_w = low(jax.nn.softmax(scores, axis=-1))
    return jnp.einsum('whqk,wkhd->wqhd', softmax_w, values, precision=HIGHEST)

def attend_all(queries, key_heads, values, bias_table, key_valid, labels):
    window_count = queries.shape[0]

    def one_block(items):
        return attend_block(items[0], items[1], items[2], bias_table, items[3], items[4])

    def split_up(array):
        return array.reshape((window_count // 4, 4) + array.shape[1:])
    result = lax.map(jax.checkpoint(one_block), (split_up(queries), split_up(key_heads), split_up(values), split_up(key_valid), split_up(labels)))
    return result.reshape(queries.shape)

def swin_block(stream, weights, which_layer, bias_table, key_valid, labels, shifted):
    w_qkv, w_proj, w_up, w_down, vectors = unpack(weights, which_layer)
    window_count = stream.shape[0] * stream.shape[1]
    normed = low(layer_norm(stream, vectors[0:C], vectors[C:2 * C]))
    if shifted:
        normed = roll_windows(low_back(normed), -SHIFT)
    token_rows = normed.reshape(window_count * WS, C)
    projected = jnp.dot(token_rows, w_qkv, precision=HIGHEST)
    queries = low(low_back(projected[:, :C] + vectors[2 * C:3 * C]))
    key_heads = low(low_back(projected[:, C:2 * C]))
    values = low(low_back(projected[:, 2 * C:] + vectors[3 * C:4 * C]))
    head_shape = (window_count, WS, HEADS, HEAD_DIM)
    attended = attend_all(queries.reshape(head_shape), key_heads.reshape(head_shape), values.reshape(head_shape), bias_table, key_valid.reshape(window_count, WS), labels.reshape(window_count, WS))
    attended = low(low_back(attended.reshape(window_count * WS, C)))
    branch = low_back(jnp.dot(attended, w_proj, precision=HIGHEST) + vectors[4 * C:5 * C])
    branch = branch.reshape(stream.shape)
    if shifted:
        branch = roll_windows(low(branch), SHIFT)
    stream = stream + branch
    normed = low(layer_norm(stream, vectors[5 * C:6 * C], vectors[6 * C:7 * C]))
    hidden = low_back(jnp.dot(normed.reshape(window_count * WS, C), w_up, precision=HIGHEST) + vectors[8 * C:])
    active = low(jax.nn.gelu(hidden, approximate=False))
    branch = low_back(jnp.dot(active, w_down, precision=HIGHEST) + vectors[7 * C:8 * C])
    return stream + branch.reshape(stream.shape)

def adamw(master, first_moment, second_moment, gradient):
    position = jnp.arange(NPARAM, dtype=jnp.int32) % block_length()
    is_vector = position >= 4 * C * C + 2 * C * FF
    step_rate = jnp.where(is_vector, RATE_VECTOR, RATE_MATRIX)
    weight_decay = jnp.where(is_vector, 0.0, DECAY_MATRIX)
    moment_one = BETA_FIRST * first_moment + (1.0 - BETA_FIRST) * gradient
    moment_two = BETA_SECOND * second_moment + (1.0 - BETA_SECOND) * gradient * gradient
    corrected_one = moment_one / (1.0 - BETA_FIRST ** STEP)
    corrected_two = moment_two / (1.0 - BETA_SECOND ** STEP)
    normalized = corrected_one / (jnp.sqrt(corrected_two) + ADAM_EPS)
    updated = master - step_rate * (normalized + weight_decay * master)
    return (updated, moment_one, moment_two)

def reference(tokens, cotangent, position_bias, window_volume, clip_extent, master, first_moment, second_moment):
    key_valid, labels = window_masks(window_volume, clip_extent)
    shift_valid = roll_windows(key_valid[..., None], -SHIFT)[..., 0]
    shift_labels = roll_windows(labels[..., None], -SHIFT)[..., 0] * 8 + wrap_code(MB)
    keep_mask = key_valid.astype(jnp.float32)[..., None]
    bias_table = position_bias.astype(jnp.float32)

    def forward(stream, params):
        weights = low(params)
        stream = swin_block(stream, weights, 0, bias_table[0], key_valid, labels, False)
        stream = swin_block(stream, weights, 1, bias_table[1], shift_valid, shift_labels, True)
        return stream * keep_mask
    result, pullback = jax.vjp(forward, tokens.astype(jnp.float32), master)
    input_grad, gradient = pullback(cotangent.astype(jnp.float32))
    new_master, new_first, new_second = adamw(master, first_moment, second_moment, gradient)
    return (result.astype(jnp.bfloat16), input_grad, new_master, new_first, new_second, new_master.astype(jnp.bfloat16))
```

```python
from types import SimpleNamespace

import jax
import jax.numpy as jnp
import numpy as np
from jax import lax
from jax.experimental import pallas as pl
from jax.experimental.pallas import tpu as pltpu
from jax.sharding import PartitionSpec as P

C = 96
HEADS = 6
HEAD_DIM = 16
FF = 384
SIDE = 7
SHIFT = 3
WS = 343
STEP = 6
T = 384
CA = 128
BLOCK_ROWS = 1164

NORM_EPS = 1e-05
MASK_FILL = -1000000000.0
BETA_FIRST = 0.5
BETA_SECOND = 0.5
ADAM_EPS = 1e-08
RATE_MATRIX = 0.1
RATE_VECTOR = 0.4
DECAY_MATRIX = 0.05

BF = jnp.bfloat16
F32 = jnp.float32
NN = (((1,), (0,)), ((), ()))
NT = (((1,), (1,)), ((), ()))
BY_STEP, WHOLE, SMEM = -1, -2, -3
VOL, WIN = "vol", "win"


def octant_bits(octant):
    return (octant >> 2 & 1, octant >> 1 & 1, octant & 1)


OCT_SIZE = []
OCT_LEN = []
OCT_OFF = []
for _octant in range(8):
    _size = 1
    for _bit in octant_bits(_octant):
        _size *= SHIFT if _bit else SIDE - SHIFT
    OCT_OFF.append(sum(OCT_LEN))
    OCT_SIZE.append(_size)
    OCT_LEN.append(-(-_size // 16) * 16)


def slot_tables():
    perm = np.zeros((T, T), np.float32)
    order = np.zeros((T, WS), np.float32)
    rolled = np.full((T, 4), 99, np.int32)
    plain = np.full((T, 4), 99, np.int32)
    plain[:, 3] = 0
    for octant in range(8):
        bits = octant_bits(octant)
        lens = [SHIFT if bit else SIDE - SHIFT for bit in bits]
        rolled[OCT_OFF[octant] : OCT_OFF[octant] + OCT_LEN[octant], 3] = octant
        for i in range(lens[0]):
            for j in range(lens[1]):
                for k in range(lens[2]):
                    source = [v if bit else v + SHIFT for v, bit in zip((i, j, k), bits)]
                    q = OCT_OFF[octant] + (i * lens[1] + j) * lens[2] + k
                    t = (source[0] * SIDE + source[1]) * SIDE + source[2]
                    perm[q, t] = 1
                    own = [v + bit * (SIDE - SHIFT) for v, bit in zip((i, j, k), bits)]
                    order[q, (own[0] * SIDE + own[1]) * SIDE + own[2]] = 1
                    rolled[q, :3] = source
    for i in range(SIDE):
        for j in range(SIDE):
            for k in range(SIDE):
                plain[(i * SIDE + j) * SIDE + k, :3] = (i, j, k)
    return perm, order, plain, rolled


PERM, ORDER, PLAIN, ROLLED = slot_tables()


def dot(a, b, dims=NN):
    return lax.dot_general(a, b, dims, preferred_element_type=F32)


def wide(column):
    return jnp.concatenate([column] * (T // 128), axis=1)


def ln_stats(x):
    centred = x - jnp.mean(x, axis=0, keepdims=True)
    scale = lax.rsqrt(jnp.mean(centred * centred, axis=0, keepdims=True) + NORM_EPS)
    return centred * scale, scale


def norm_back(e, z, scale, gain):
    eg = e * gain
    return scale * (
        eg - jnp.mean(eg, axis=0, keepdims=True) - z * jnp.mean(eg * z, axis=0, keepdims=True)
    )


def gelu_pair(h):
    base = 1.0 + (0.3275911 * 0.7071067811865476) * jnp.abs(h)
    t = pl.reciprocal(base, approx=True)
    t = t * (2.0 - base * t)
    poly = t * (
        0.5 * 0.254829592
        + t
        * (
            0.5 * -0.284496736
            + t * (0.5 * 1.421413741 + t * (0.5 * -1.453152027 + t * (0.5 * 1.061405429)))
        )
    )
    bell = jnp.exp(-0.5 * (h * h))
    tail = poly * bell
    phi = jnp.where(h < 0.0, tail, 1.0 - tail)
    return h * phi, phi + h * bell * 0.3989422804014327


def ones_row(shape, row=0):
    return jnp.where(lax.broadcasted_iota(jnp.int32, shape, 0) == row, 1.0, 0.0)


def init_forward(r, sc):
    sc.qb[...] = jnp.zeros((CA, HEADS * T), BF)
    for h in range(HEADS):
        sc.vt[h, 16:32, :] = ones_row((16, T)).astype(BF)
        turned = dot(r.order[...], r.table[0, h], NT).astype(BF)
        sc.bias[h] = dot(turned, r.order[...], NT)


def init_backward(sc):
    sc.dab[...] = jnp.zeros((CA, HEADS * T), BF)
    sc.rb[...] = jnp.zeros((2 * C, 2 * HEADS * T), BF)
    for name, (shape, dtype) in GRADS.items():
        getattr(sc, name)[...] = jnp.zeros(shape, dtype)


def set_queries(sc, queries):
    for h in range(HEADS):
        sc.qb[16 * h : 16 * h + 16, T * h : T * h + T] = queries[16 * h : 16 * h + 16, :]


def forward_attention(sc, w, x, code_row):
    z, _ = ln_stats(x)
    sc.n1aug[C:CA, :] = ones_row((CA - C, T)).astype(BF)
    sc.attaug[C:CA, :] = ones_row((CA - C, T)).astype(BF)
    sc.n1aug[0:C, :] = (z * wide(w.vec[0]) + wide(w.vec[1])).astype(BF)
    qkv = dot(w.qkvT[...], sc.n1aug[...])
    queries = qkv[0:C].astype(BF)
    set_queries(sc, queries)
    sc.qT[...] = queries
    sc.kT[...] = qkv[C : 2 * C].astype(BF)
    values = qkv[2 * C :].astype(BF)
    for h in range(HEADS):
        sc.vt[h, 0:16, :] = values[16 * h : 16 * h + 16, :]
    kv = dot(sc.n1aug[...].T, w.kv[...]).astype(BF)
    sc.kn[...] = kv[:, 0:CA]
    sc.vn[...] = kv[:, CA:]
    eye = lax.broadcasted_iota(jnp.int32, (128, 128), 0) == lax.broadcasted_iota(
        jnp.int32, (128, 128), 1
    )
    tops = [None] * HEADS

    def scores(h, c):
        rows = slice(128 * c, 128 * c + 128)
        x_all = dot(sc.kn[rows], sc.qb[:, T * h : T * h + T])
        codes = sc.codes[rows]
        parts = []
        for j in range(3):
            lanes = slice(128 * j, 128 * j + 128)
            allowed = codes == code_row[:, lanes]
            if j == c:
                allowed = allowed | eye
            part = jnp.where(allowed, x_all[:, lanes] + sc.bias[h, rows, lanes], MASK_FILL)
            sc.s[h % 3, rows, lanes] = part
            parts.append(jnp.max(part.reshape(16, 8, 128), axis=0))
        top = jnp.concatenate(parts, axis=1)
        tops[h] = top if tops[h] is None else jnp.maximum(tops[h], top)

    def raise_(h, c):
        rows = slice(128 * c, 128 * c + 128)
        sc.e[rows, T * h : T * h + T] = jnp.exp(sc.s[h % 3, rows] - tops[h]).astype(BF)

    def attend(h):
        out = dot(sc.vt[h], sc.e[:, T * h : T * h + T])
        inverse = 1.0 / out[16:17]
        part = out[0:16] * inverse
        sc.att[16 * h : 16 * h + 16, :] = part
        sc.inv[h : h + 1, :] = inverse
        sc.attaug[16 * h : 16 * h + 16, :] = part.astype(BF)

    for h in range(HEADS + 3):
        for c in range(3):
            if h < HEADS:
                scores(h, c)
            if 0 <= h - 1 < HEADS:
                raise_(h - 1, c)
            if c == 0 and 0 <= h - 2 < HEADS:
                attend(h - 2)
        if h < HEADS:
            tops[h] = jnp.max(tops[h], axis=0, keepdims=True)
    return dot(w.projT[...], sc.attaug[...])


def backward_attention(sc, w, d_mid, z, scale, shifted):
    db = d_mid.astype(BF)
    sc.gproj[...] += dot(sc.attaug[...], db, NT)
    d_att = dot(w.proj[...], db).astype(BF).astype(F32)
    row = lax.broadcasted_iota(jnp.int32, (16, T), 0)
    for h in range(HEADS):
        part = (d_att[16 * h : 16 * h + 16] * sc.inv[h : h + 1, :]).astype(BF)
        cols = slice(T * h, T * h + T)
        sc.dab[16 * h : 16 * h + 16, cols] = part
        sc.rb[C + 16 * h : C + 16 * h + 16, 2 * T * h : 2 * T * h + T] = part
        sc.rb[16 * h : 16 * h + 16, 2 * T * h + T : 2 * T * h + 2 * T] = sc.qT[
            16 * h : 16 * h + 16, :
        ]
        inner = -jnp.sum(
            part.astype(F32) * sc.att[16 * h : 16 * h + 16, :], axis=0, keepdims=True
        )
        high = inner.astype(BF).astype(F32)
        low = inner - high
        sc.dab[C : C + 16, cols] = jnp.where(
            row == 0, high, jnp.where(row == 1, low, 0.0)
        ).astype(BF)
    total = None

    def soft(h):
        cols = slice(T * h, T * h + T)
        pull = dot(sc.vn[...], sc.dab[:, cols])
        sc.ds[:, cols] = (pull * sc.e[:, cols].astype(F32)).astype(BF)

    def to_queries(h):
        sc.dq[16 * h : 16 * h + 16, :] = dot(
            sc.kT[16 * h : 16 * h + 16, :], sc.ds[:, T * h : T * h + T]
        ).astype(BF)

    for h in range(HEADS + 1):
        if h < HEADS:
            soft(h)
        if h > 0:
            cols = slice(T * (h - 1), T * h)
            to_queries(h - 1)
            both = jnp.concatenate([sc.e[:, cols], sc.ds[:, cols]], axis=1)
            term = dot(both, sc.rb[:, 2 * T * (h - 1) : 2 * T * h], NT)
            total = term if total is None else total + term
    dkv = total.astype(BF)
    dq = sc.dq[...]
    sc.gkv[...] += dot(sc.n1aug[...], dkv)
    sc.gq[...] += dot(dq, sc.n1aug[...], NT)
    dn = dot(w.q[...], dq) + dot(w.kv96[...], dkv, NT)
    if shifted:
        dn = dn.astype(BF).astype(F32)
    sc.gvec[0] += dn * z
    sc.gvec[1] += dn
    return d_mid + norm_back(dn, z, scale, wide(w.vec[0]))


def feed_forward_back(sc, w, d, dd, z, scale):
    sc.gdown[...] += dot(sc.act[...], dd, NT)
    sc.gup[...] += dot(sc.dh[...], sc.n2aug[...], NT)
    sc.gvec[4] += dd.astype(F32)
    dn = dot(w.up[...], sc.dh[...])
    sc.gvec[2] += dn * z
    sc.gvec[3] += dn
    return d + norm_back(dn, z, scale, wide(w.vec[2]))


def write_grads(sc, out):
    gq = sc.gq[...].T
    gkv = sc.gkv[...]
    gup = sc.gup[...].T
    out[pl.ds(0, C, 3), :] = gq[0:C]
    out[pl.ds(1, C, 3), :] = gkv[0:C, 0:C]
    out[pl.ds(2, C, 3), :] = gkv[0:C, C : 2 * C]
    out[3 * C : 4 * C, :] = sc.gproj[0:C, :]
    for j in range(4):
        out[pl.ds(4 * C + j, C, 4), :] = gup[0:C, C * j : C * j + C]
    out[8 * C : 12 * C, :] = sc.gdown[...]
    sums = [jnp.sum(sc.gvec[n].T, axis=0, keepdims=True) for n in range(5)]
    rows = [
        sums[0],
        sums[1],
        gq[C : C + 1],
        gkv[C : C + 1, C : 2 * C],
        sc.gproj[C : C + 1, :],
        sums[2],
        sums[3],
        sums[4],
    ] + [gup[C : C + 1, C * j : C * j + C] for j in range(4)]
    for n, value in enumerate(rows):
        out[12 * C + n : 12 * C + n + 1, :] = value


FWD = dict(
    qb=((CA, HEADS * T), BF),
    vt=((HEADS, 32, T), BF),
    kn=((T, CA), BF),
    codes=((T, 128), F32),
    bias=((HEADS, T, T), F32),
    s=((3, T, T), F32),
)
KEPT = dict(
    qT=((C, T), BF),
    kT=((C, T), BF),
    vn=((T, CA), BF),
    e=((T, HEADS * T), BF),
    att=((C, T), F32),
    inv=((8, T), F32),
    attaug=((CA, T), BF),
    n1aug=((CA, T), BF),
    n2aug=((CA, T), BF),
    act=((FF, T), BF),
    gp=((FF, T), BF),
    xT=((C, T), F32),
    x1=((C, T), F32),
)
GRADS = dict(
    gq=((C, CA), F32),
    gkv=((CA, 2 * C), F32),
    gproj=((CA, C), F32),
    gup=((FF, CA), F32),
    gdown=((FF, C), F32),
    gvec=((5, C, T), F32),
)
BWD = dict(
    **GRADS,
    dab=((CA, HEADS * T), BF),
    rb=((2 * C, 2 * HEADS * T), BF),
    ds=((T, HEADS * T), BF),
    dq=((C, T), BF),
    dh=((FF, T), BF),
)


def by_step(r):
    return SimpleNamespace(**{**vars(r), **{n: getattr(r, n).at[0] for n in KEPT}})


def second_norm(sc, w, x):
    z, scale = ln_stats(x)
    sc.n2aug[C:CA, :] = ones_row((CA - C, T)).astype(BF)
    sc.n2aug[0:C, :] = (z * wide(w.vec[2]) + wide(w.vec[3])).astype(BF)
    return z, scale


def first_forward_kernel(r):
    w, sc = r, by_step(r)
    m = pl.program_id(0)

    @pl.when(m == 0)
    def _():
        init_forward(r, sc)
        sc.pad[...] = jnp.zeros((2, T, C), BF)

    sc.pad[0, 0:WS, :] = r.tokens[0, 0]
    sc.pad[1, 0:WS, :] = r.cotangent[0, 0]
    r.sent_cot[0] = dot(r.perm[...], sc.pad[1]).astype(BF)
    place = r.place
    valid = (
        (place[0] < r.info[m, 1]) & (place[1] < r.info[m, 2]) & (place[2] < r.info[m, 3])
    )
    sc.codes[...] = jnp.where(valid, 0.0, -1.0)
    x = dot(r.eye[...], sc.pad[0], NT)
    sc.xT[...] = x
    x = x + forward_attention(sc, w, x, jnp.zeros((1, T), F32))
    sc.x1[...] = x
    second_norm(sc, w, x)
    for c in range(3):
        rows = slice(128 * c, 128 * c + 128)
        active, slope = gelu_pair(dot(w.upT[rows], sc.n2aug[...]))
        sc.act[rows, :] = active.astype(BF)
        sc.gp[rows, :] = slope.astype(BF)
    x = x + (dot(w.downT[...], sc.act[...]) + wide(w.vec[4]))
    r.sent_x[0] = dot(r.perm[...], x.astype(BF), NT).astype(BF)


def second_kernel(r):
    w, sc = r, r
    m = pl.program_id(0)

    @pl.when(m == 0)
    def _():
        init_forward(r, sc)
        init_backward(sc)

    place, rows4 = r.place, r.places
    octant_row = rows4[3:4, :]
    label_row = jnp.zeros((1, T), F32)
    ends = [jnp.zeros((1, T), jnp.int32)] * 3
    for o in range(8):
        rows = slice(OCT_OFF[o], OCT_OFF[o] + OCT_LEN[o])
        item = [r.info[m, 4 * o + n] for n in range(4)]
        label = item[0].astype(F32)
        valid = (
            (place[0, rows] < item[1]) & (place[1, rows] < item[2]) & (place[2, rows] < item[3])
        )
        sc.codes[rows, :] = jnp.where(valid, label, -1.0)
        here = octant_row == o
        label_row = jnp.where(here, label, label_row)
        ends = [jnp.where(here, item[n + 1], ends[n]) for n in range(3)]
    keep = jnp.where(
        (rows4[0:1, :] < ends[0]) & (rows4[1:2, :] < ends[1]) & (rows4[2:3, :] < ends[2]), 1.0, 0.0
    )
    x = dot(r.eye[...], r.got_x[0], NT)
    d = dot(r.eye[...], r.got_cot[0], NT) * keep
    dd = d.astype(BF)
    sc.xT[...] = x
    branch = forward_attention(sc, w, x, label_row)
    x = x + branch.astype(BF).astype(F32)
    z, scale = second_norm(sc, w, x)
    for c in range(3):
        rows = slice(128 * c, 128 * c + 128)
        active, slope = gelu_pair(dot(w.upT[rows], sc.n2aug[...]))
        sc.act[rows, :] = active.astype(BF)
        sc.dh[rows, :] = (dot(w.down[rows], dd) * slope).astype(BF)
    x = x + (dot(w.downT[...], sc.act[...]) + wide(w.vec[4]))
    r.sent_out[0] = (x * keep).T.astype(BF)
    d = feed_forward_back(sc, w, d, dd, z, scale)
    z, scale = ln_stats(sc.xT[...])
    d = backward_attention(sc, w, d, z, scale, True)
    r.sent_d[0] = d.T.astype(BF)

    @pl.when(m == pl.num_programs(0) - 1)
    def _():
        write_grads(sc, r.grads)


def first_backward_kernel(r):
    w, sc = r, by_step(r)
    m = pl.program_id(0)

    @pl.when(m == 0)
    def _():
        init_backward(sc)

    r.output[0, 0] = dot(r.perm_back[...], r.got_out[0]).astype(BF)[0:WS]
    d = dot(dot(r.eye[...], r.got_d[0], NT).astype(BF), r.perm[...])
    dd = d.astype(BF)
    z, scale = ln_stats(sc.x1[...])
    for c in range(3):
        rows = slice(128 * c, 128 * c + 128)
        sc.dh[rows, :] = (dot(w.down[rows], dd) * sc.gp[rows, :].astype(F32)).astype(BF)
    d = feed_forward_back(sc, w, d, dd, z, scale)
    z, scale = ln_stats(sc.xT[...])
    d = backward_attention(sc, w, d, z, scale, False)
    r.input_grad[0, 0] = d.T[0:WS]

    @pl.when(m == pl.num_programs(0) - 1)
    def _():
        write_grads(sc, r.grads)


def call(kernel, steps, ins, outs, scratch):
    def spec(shape, kind):
        if kind is SMEM:
            return pl.BlockSpec(memory_space=pltpu.SMEM)
        zeros = (0,) * (len(shape) - 1)
        if kind is BY_STEP:
            return pl.BlockSpec((1,) + tuple(shape[1:]), lambda m: (m,) + zeros)
        if kind in (0, 1):
            return pl.BlockSpec((1,) + tuple(shape[1:]), lambda m: (kind,) + zeros)
        return pl.BlockSpec(tuple(shape), lambda m: (0,) + zeros)

    names = tuple(ins) + tuple(outs) + tuple(scratch)

    def body(*refs):
        kernel(SimpleNamespace(**dict(zip(names, refs))))

    results = pl.pallas_call(
        body,
        grid=(steps,),
        in_specs=[spec(a.shape, kind) for a, kind in ins.values()],
        out_specs=[spec(shape, kind) for shape, _, kind in outs.values()],
        out_shape=[jax.ShapeDtypeStruct(shape, dtype) for shape, dtype, _ in outs.values()],
        scratch_shapes=[pltpu.VMEM(shape, dtype) for shape, dtype in scratch.values()],
        compiler_params=pltpu.CompilerParams(vmem_limit_bytes=60 * 2**20),
    )(*[a for a, _ in ins.values()])
    return SimpleNamespace(**dict(zip(outs, results)))


def layer_operands(params, which_layer):
    rows = params[which_layer * BLOCK_ROWS : (which_layer + 1) * BLOCK_ROWS]
    wq, wk, wv = (rows[0 : 3 * C].reshape(C, 3, C)[:, n] for n in range(3))
    proj = rows[3 * C : 4 * C]
    up = rows[4 * C : 8 * C].reshape(C, FF)
    down = rows[8 * C : 12 * C]
    vectors = rows[12 * C : 12 * C + 8]
    bias_up = rows[12 * C + 8 :].reshape(FF)
    gain1, offset1, bias_q, bias_v, bias_proj, gain2, offset2, bias_down = vectors
    quarter = jnp.asarray(0.25, BF)

    def aug(matrix, bias):
        return jnp.concatenate(
            [matrix, bias[:, None], jnp.zeros((matrix.shape[0], CA - C - 1), BF)], axis=1
        )

    none = jnp.zeros((C,), BF)
    kn = aug(wk.T, none).T
    vn = jnp.concatenate([aug(wv.T, bias_v).T, jnp.zeros((CA, CA - C), BF)], axis=1)
    vn = vn.at[C, C : C + 2].set(1.0)
    kn = jnp.concatenate([kn, jnp.zeros((CA, CA - C), BF)], axis=1)
    columns = jnp.stack([gain1, offset1, gain2, offset2, bias_down]).astype(F32)
    return dict(
        qkvT=jnp.concatenate(
            [aug(wq.T * quarter, bias_q * quarter), aug(wk.T * quarter, none), aug(wv.T, bias_v)]
        ),
        kv=jnp.concatenate([kn, vn], axis=1),
        projT=aug(proj.T, bias_proj),
        proj=proj,
        upT=aug(up.T, bias_up),
        up=up,
        downT=down.T,
        down=down,
        q=wq,
        kv96=jnp.concatenate([wk, wv], axis=1),
        vec=jnp.broadcast_to(columns[:, :, None], (5, C, 128)),
    )


def exchange(x, forward, groups_a):
    sign = -1 if forward else 1
    blocks = []
    for octant in range(8):
        part = x[:, OCT_OFF[octant] : OCT_OFF[octant] + OCT_LEN[octant]]
        if octant:
            bits = octant_bits(octant)
            pairs = []
            for w in range(4 * groups_a):
                place = (w // 4, w // 2 % 2, w % 2)
                a, b, c = (
                    (p + sign * bit) % n for p, bit, n in zip(place, bits, (groups_a, 2, 2))
                )
                pairs.append((w, (a * 2 + b) * 2 + c))
            part = lax.ppermute(part, WIN, pairs)
        blocks.append(part)
    return jnp.concatenate(blocks, axis=1)


def octant_info(group_info, groups_a):
    index_win = lax.axis_index(WIN)
    place = (index_win // 4, index_win // 2 % 2, index_win % 2)
    items = []
    for octant in range(8):
        bits = octant_bits(octant)
        a, b, c = ((p + bit) % n for p, bit, n in zip(place, bits, (groups_a, 2, 2)))
        wraps = [
            bit * (p == n - 1).astype(jnp.int32) for p, bit, n in zip(place, bits, (groups_a, 2, 2))
        ]
        source = lax.dynamic_index_in_dim(group_info, (a * 2 + b) * 2 + c, 1, keepdims=False)
        code = wraps[0] * 4 + wraps[1] * 2 + wraps[2]
        items.append(source * jnp.array([8, 1, 1, 1]) + code * jnp.array([1, 0, 0, 0]))
    return jnp.concatenate(items, axis=1)


def on_device(
    tokens,
    cotangent,
    position_bias,
    window_volume,
    clip_extent,
    master,
    first_moment,
    second_moment,
):
    groups_a = lax.axis_size(WIN) // 4
    steps = tokens.shape[0]
    params = lax.all_gather(master.astype(BF), (VOL, WIN), axis=0, tiled=True)
    own_info = jnp.concatenate((window_volume[:, :, None], clip_extent), axis=2)
    group_info = lax.all_gather(own_info, WIN, axis=1, tiled=True)
    info = octant_info(group_info, groups_a)
    params = params.reshape(2 * BLOCK_ROWS, C)
    weights = [layer_operands(params, n) for n in range(2)]

    def whole(table):
        return {n: (a, WHOLE) for n, a in table.items()}

    def tables(which):
        place = (PLAIN, ROLLED)[which]
        order = (np.eye(T, WS), ORDER)[which]
        return dict(
            place=(jnp.asarray(np.broadcast_to(place.T[:3, :, None], (3, T, 128))), WHOLE),
            order=(jnp.asarray(order, BF), WHOLE),
            table=(position_bias, which),
            eye=(jnp.asarray(np.eye(C), BF), WHOLE),
        )

    perm = jnp.asarray(PERM, BF)
    got = call(
        first_forward_kernel,
        steps,
        dict(
            tokens=(tokens, BY_STEP),
            cotangent=(cotangent, BY_STEP),
            info=(own_info[:, 0], SMEM),
            perm=(perm, WHOLE),
            **tables(0),
            **whole(weights[0]),
        ),
        dict(
            sent_x=((steps, T, C), BF, BY_STEP),
            sent_cot=((steps, T, C), BF, BY_STEP),
            **{n: ((steps,) + shape, dtype, BY_STEP) for n, (shape, dtype) in KEPT.items()},
        ),
        dict(**FWD, pad=((2, T, C), BF)),
    )
    kept = {n: (getattr(got, n), BY_STEP) for n in KEPT}
    rows = np.zeros((8, T), np.int32)
    rows[:4] = ROLLED.T
    second = call(
        second_kernel,
        steps,
        dict(
            got_x=(exchange(got.sent_x, True, groups_a), BY_STEP),
            got_cot=(exchange(got.sent_cot, True, groups_a), BY_STEP),
            info=(info, SMEM),
            places=(jnp.asarray(rows), WHOLE),
            **tables(1),
            **whole(weights[1]),
        ),
        dict(
            sent_out=((steps, T, C), BF, BY_STEP),
            sent_d=((steps, T, C), BF, BY_STEP),
            grads=((BLOCK_ROWS, C), F32, WHOLE),
        ),
        dict(**FWD, **KEPT, **BWD),
    )
    first = call(
        first_backward_kernel,
        steps,
        dict(
            got_out=(exchange(second.sent_out, False, groups_a), BY_STEP),
            got_d=(exchange(second.sent_d, False, groups_a), BY_STEP),
            perm=(perm, WHOLE),
            perm_back=(jnp.asarray(PERM.T, BF), WHOLE),
            eye=(jnp.asarray(np.eye(C), BF), WHOLE),
            **kept,
            **whole(weights[0]),
        ),
        dict(
            output=((steps, 1, WS, C), BF, BY_STEP),
            input_grad=((steps, 1, WS, C), F32, BY_STEP),
            grads=((BLOCK_ROWS, C), F32, WHOLE),
        ),
        BWD,
    )
    all_grads = jnp.concatenate((first.grads, second.grads)).reshape(-1)
    shard_grad = lax.psum_scatter(all_grads, (VOL, WIN), scatter_dimension=0, tiled=True)
    shard_len = master.shape[0]
    position = (
        lax.axis_index((VOL, WIN)) * shard_len + jnp.arange(shard_len, dtype=jnp.int32)
    ) % (BLOCK_ROWS * C)
    is_vector = position >= 12 * C * C
    step_rate = jnp.where(is_vector, RATE_VECTOR, RATE_MATRIX)
    weight_decay = jnp.where(is_vector, 0.0, DECAY_MATRIX)
    moment_one = BETA_FIRST * first_moment + (1.0 - BETA_FIRST) * shard_grad
    moment_two = BETA_SECOND * second_moment + (1.0 - BETA_SECOND) * shard_grad * shard_grad
    corrected_one = moment_one / (1.0 - BETA_FIRST**STEP)
    corrected_two = moment_two / (1.0 - BETA_SECOND**STEP)
    normalized = corrected_one / (jnp.sqrt(corrected_two) + ADAM_EPS)
    new_master = master - step_rate * (normalized + weight_decay * master)
    return (
        first.output,
        first.input_grad,
        new_master,
        moment_one,
        moment_two,
        new_master.astype(BF),
    )


def solution(mesh):
    placed = (
        P(None, (VOL, WIN), None, None),
        P(None, (VOL, WIN), None, None),
        P(),
        P(None, (VOL, WIN)),
        P(None, (VOL, WIN), None),
        P((VOL, WIN)),
        P((VOL, WIN)),
        P((VOL, WIN)),
    )
    return jax.shard_map(
        on_device,
        mesh=mesh,
        in_specs=placed,
        out_specs=(
            P(None, (VOL, WIN), None, None),
            P(None, (VOL, WIN), None, None),
            P((VOL, WIN)),
            P((VOL, WIN)),
            P((VOL, WIN)),
            P((VOL, WIN)),
        ),
        check_vma=False,
    )
```

```python
from types import SimpleNamespace

import jax
import jax.numpy as jnp
import numpy as np
from jax import lax
from jax.experimental import pallas as pl
from jax.experimental.pallas import tpu as pltpu
from jax.sharding import PartitionSpec as P

C = 96
HEADS = 6
HEAD_DIM = 16
FF = 384
SIDE = 7
SHIFT = 3
WS = 343
STEP = 6
T = 384
CA = 128
BLOCK_ROWS = 1164

NORM_EPS = 1e-05
MASK_FILL = -1000000000.0
BETA_FIRST = 0.5
BETA_SECOND = 0.5
ADAM_EPS = 1e-08
RATE_MATRIX = 0.1
RATE_VECTOR = 0.4
DECAY_MATRIX = 0.05

BF = jnp.bfloat16
F32 = jnp.float32
NN = (((1,), (0,)), ((), ()))
NT = (((1,), (1,)), ((), ()))
BY_STEP, WHOLE, SMEM, HBM = -1, -2, -3, -4
MESH = pl.DeviceIdType.MESH
VOL, WIN = "vol", "win"


def octant_bits(octant):
    return (octant >> 2 & 1, octant >> 1 & 1, octant & 1)


OCT_SIZE = []
OCT_LEN = []
OCT_OFF = []
for _octant in range(8):
    _size = 1
    for _bit in octant_bits(_octant):
        _size *= SHIFT if _bit else SIDE - SHIFT
    OCT_OFF.append(sum(OCT_LEN))
    OCT_SIZE.append(_size)
    OCT_LEN.append(-(-_size // 16) * 16)


def slot_tables():
    perm = np.zeros((T, T), np.float32)
    order = np.zeros((T, WS), np.float32)
    places = np.full((8, T), 99, np.int32)
    for octant in range(8):
        bits = octant_bits(octant)
        lens = [SHIFT if bit else SIDE - SHIFT for bit in bits]
        for i in range(lens[0]):
            for j in range(lens[1]):
                for k in range(lens[2]):
                    source = [v if bit else v + SHIFT for v, bit in zip((i, j, k), bits)]
                    own = [v + bit * (SIDE - SHIFT) for v, bit in zip((i, j, k), bits)]
                    q = OCT_OFF[octant] + (i * lens[1] + j) * lens[2] + k
                    t = (source[0] * SIDE + source[1]) * SIDE + source[2]
                    perm[q, t] = 1
                    order[q, (own[0] * SIDE + own[1]) * SIDE + own[2]] = 1
                    places[:3, t] = source
    return perm, order, places


PERM, ORDER, PLACES = slot_tables()


def dot(a, b, dims=NN):
    return lax.dot_general(a, b, dims, preferred_element_type=F32)


def wide(column):
    return jnp.concatenate([column] * (T // 128), axis=1)


def ln_stats(x):
    centred = x - jnp.mean(x, axis=0, keepdims=True)
    scale = lax.rsqrt(jnp.mean(centred * centred, axis=0, keepdims=True) + NORM_EPS)
    return centred * scale, scale


def norm_back(e, z, scale, gain):
    eg = e * gain
    return scale * (
        eg - jnp.mean(eg, axis=0, keepdims=True) - z * jnp.mean(eg * z, axis=0, keepdims=True)
    )


def gelu_pair(h):
    base = 1.0 + (0.3275911 * 0.7071067811865476) * jnp.abs(h)
    t = pl.reciprocal(base, approx=True)
    t = t * (2.0 - base * t)
    poly = t * (
        0.5 * 0.254829592
        + t
        * (
            0.5 * -0.284496736
            + t * (0.5 * 1.421413741 + t * (0.5 * -1.453152027 + t * (0.5 * 1.061405429)))
        )
    )
    bell = jnp.exp(-0.5 * (h * h))
    tail = poly * bell
    phi = jnp.where(h < 0.0, tail, 1.0 - tail)
    return h * phi, phi + h * bell * 0.3989422804014327


def ones_row(shape, row=0):
    return jnp.where(lax.broadcasted_iota(jnp.int32, shape, 0) == row, 1.0, 0.0)


def init_forward(r, sc):
    sc.qb[...] = jnp.zeros((CA, HEADS * T), BF)
    for h in range(HEADS):
        sc.vt[h, 16:32, :] = ones_row((16, T)).astype(BF)
        turned = dot(r.order[...], r.table[h], NT).astype(BF)
        sc.bias[h] = dot(turned, r.order[...], NT)


def init_backward(sc):
    sc.dab[...] = jnp.zeros((CA, HEADS * T), BF)
    sc.rb[...] = jnp.zeros((2 * C, 2 * HEADS * T), BF)
    for name, (shape, dtype) in GRADS.items():
        getattr(sc, name)[...] = jnp.zeros(shape, dtype)


def set_queries(sc, queries):
    for h in range(HEADS):
        sc.qb[16 * h : 16 * h + 16, T * h : T * h + T] = queries[16 * h : 16 * h + 16, :]


def forward_attention(sc, w, x, code_row):
    z, _ = ln_stats(x)
    sc.n1aug[C:CA, :] = ones_row((CA - C, T)).astype(BF)
    sc.attaug[C:CA, :] = ones_row((CA - C, T)).astype(BF)
    sc.n1aug[0:C, :] = (z * wide(w.vec[0]) + wide(w.vec[1])).astype(BF)
    qkv = dot(w.qkvT[...], sc.n1aug[...])
    queries = qkv[0:C].astype(BF)
    set_queries(sc, queries)
    sc.qT[...] = queries
    sc.kT[...] = qkv[C : 2 * C].astype(BF)
    values = qkv[2 * C :].astype(BF)
    for h in range(HEADS):
        sc.vt[h, 0:16, :] = values[16 * h : 16 * h + 16, :]
    kv = dot(sc.n1aug[...].T, w.kv[...]).astype(BF)
    sc.kn[...] = kv[:, 0:CA]
    sc.vn[...] = kv[:, CA:]
    eye = lax.broadcasted_iota(jnp.int32, (128, 128), 0) == lax.broadcasted_iota(
        jnp.int32, (128, 128), 1
    )
    tops = [None] * HEADS

    def scores(h, c):
        rows = slice(128 * c, 128 * c + 128)
        x_all = dot(sc.kn[rows], sc.qb[:, T * h : T * h + T])
        codes = sc.codes[rows]
        parts = []
        for j in range(3):
            lanes = slice(128 * j, 128 * j + 128)
            allowed = codes == code_row[:, lanes]
            if j == c:
                allowed = allowed | eye
            part = jnp.where(allowed, x_all[:, lanes] + sc.bias[h, rows, lanes], MASK_FILL)
            sc.s[h % 3, rows, lanes] = part
            parts.append(jnp.max(part.reshape(16, 8, 128), axis=0))
        top = jnp.concatenate(parts, axis=1)
        tops[h] = top if tops[h] is None else jnp.maximum(tops[h], top)

    def raise_(h, c):
        rows = slice(128 * c, 128 * c + 128)
        sc.e[rows, T * h : T * h + T] = jnp.exp(sc.s[h % 3, rows] - tops[h]).astype(BF)

    def attend(h):
        out = dot(sc.vt[h], sc.e[:, T * h : T * h + T])
        inverse = 1.0 / out[16:17]
        part = out[0:16] * inverse
        sc.att[16 * h : 16 * h + 16, :] = part
        sc.inv[h : h + 1, :] = inverse
        sc.attaug[16 * h : 16 * h + 16, :] = part.astype(BF)

    for h in range(HEADS + 3):
        for c in range(3):
            if h < HEADS:
                scores(h, c)
            if 0 <= h - 1 < HEADS:
                raise_(h - 1, c)
            if c == 0 and 0 <= h - 2 < HEADS:
                attend(h - 2)
        if h < HEADS:
            tops[h] = jnp.max(tops[h], axis=0, keepdims=True)
    return dot(w.projT[...], sc.attaug[...])


def backward_attention(sc, w, d_mid, z, scale, shifted):
    db = d_mid.astype(BF)
    sc.gproj[...] += dot(sc.attaug[...], db, NT)
    d_att = dot(w.proj[...], db).astype(BF).astype(F32)
    row = lax.broadcasted_iota(jnp.int32, (16, T), 0)
    for h in range(HEADS):
        part = (d_att[16 * h : 16 * h + 16] * sc.inv[h : h + 1, :]).astype(BF)
        cols = slice(T * h, T * h + T)
        sc.dab[16 * h : 16 * h + 16, cols] = part
        sc.rb[C + 16 * h : C + 16 * h + 16, 2 * T * h : 2 * T * h + T] = part
        sc.rb[16 * h : 16 * h + 16, 2 * T * h + T : 2 * T * h + 2 * T] = sc.qT[
            16 * h : 16 * h + 16, :
        ]
        inner = -jnp.sum(
            part.astype(F32) * sc.att[16 * h : 16 * h + 16, :], axis=0, keepdims=True
        )
        high = inner.astype(BF).astype(F32)
        low = inner - high
        sc.dab[C : C + 16, cols] = jnp.where(
            row == 0, high, jnp.where(row == 1, low, 0.0)
        ).astype(BF)
    total = None

    def soft(h):
        cols = slice(T * h, T * h + T)
        pull = dot(sc.vn[...], sc.dab[:, cols])
        sc.ds[:, cols] = (pull * sc.e[:, cols].astype(F32)).astype(BF)

    def to_queries(h):
        sc.dq[16 * h : 16 * h + 16, :] = dot(
            sc.kT[16 * h : 16 * h + 16, :], sc.ds[:, T * h : T * h + T]
        ).astype(BF)

    for h in range(HEADS + 1):
        if h < HEADS:
            soft(h)
        if h > 0:
            cols = slice(T * (h - 1), T * h)
            to_queries(h - 1)
            both = jnp.concatenate([sc.e[:, cols], sc.ds[:, cols]], axis=1)
            term = dot(both, sc.rb[:, 2 * T * (h - 1) : 2 * T * h], NT)
            total = term if total is None else total + term
    dkv = total.astype(BF)
    dq = sc.dq[...]
    sc.gkv[...] += dot(sc.n1aug[...], dkv)
    sc.gq[...] += dot(dq, sc.n1aug[...], NT)
    dn = dot(w.q[...], dq) + dot(w.kv96[...], dkv, NT)
    if shifted:
        dn = dn.astype(BF).astype(F32)
    sc.gvec[0] += dn * z
    sc.gvec[1] += dn
    return d_mid + norm_back(dn, z, scale, wide(w.vec[0]))


def feed_forward_back(sc, w, d, dd, z, scale):
    sc.gdown[...] += dot(sc.act[...], dd, NT)
    sc.gup[...] += dot(sc.dh[...], sc.n2aug[...], NT)
    sc.gvec[4] += dd.astype(F32)
    dn = dot(w.up[...], sc.dh[...])
    sc.gvec[2] += dn * z
    sc.gvec[3] += dn
    return d + norm_back(dn, z, scale, wide(w.vec[2]))


def write_grads(sc, out):
    gq = sc.gq[...].T
    gkv = sc.gkv[...]
    gup = sc.gup[...].T
    out[pl.ds(0, C, 3), :] = gq[0:C]
    out[pl.ds(1, C, 3), :] = gkv[0:C, 0:C]
    out[pl.ds(2, C, 3), :] = gkv[0:C, C : 2 * C]
    out[3 * C : 4 * C, :] = sc.gproj[0:C, :]
    for j in range(4):
        out[pl.ds(4 * C + j, C, 4), :] = gup[0:C, C * j : C * j + C]
    out[8 * C : 12 * C, :] = sc.gdown[...]
    sums = [jnp.sum(sc.gvec[n].T, axis=0, keepdims=True) for n in range(5)]
    rows = [
        sums[0],
        sums[1],
        gq[C : C + 1],
        gkv[C : C + 1, C : 2 * C],
        sc.gproj[C : C + 1, :],
        sums[2],
        sums[3],
        sums[4],
    ] + [gup[C : C + 1, C * j : C * j + C] for j in range(4)]
    for n, value in enumerate(rows):
        out[12 * C + n : 12 * C + n + 1, :] = value


FWD = dict(
    qb=((CA, HEADS * T), BF),
    vt=((HEADS, 32, T), BF),
    kn=((T, CA), BF),
    codes=((T, 128), F32),
    bias=((HEADS, T, T), F32),
    s=((3, T, T), F32),
)
KEPT = dict(
    qT=((C, T), BF),
    kT=((C, T), BF),
    vn=((T, CA), BF),
    e=((T, HEADS * T), BF),
    att=((C, T), F32),
    inv=((8, T), F32),
    attaug=((CA, T), BF),
    n1aug=((CA, T), BF),
    n2aug=((CA, T), BF),
    act=((FF, T), BF),
    gp=((FF, T), BF),
    xT=((C, T), F32),
    x1=((C, T), F32),
)
GRADS = dict(
    gq=((C, CA), F32),
    gkv=((CA, 2 * C), F32),
    gproj=((CA, C), F32),
    gup=((FF, CA), F32),
    gdown=((FF, C), F32),
    gvec=((5, C, T), F32),
)
BWD = dict(
    **GRADS,
    dab=((CA, HEADS * T), BF),
    rb=((2 * C, 2 * HEADS * T), BF),
    ds=((T, HEADS * T), BF),
    dq=((C, T), BF),
    dh=((FF, T), BF),
)


def by_step(r):
    return SimpleNamespace(**{**vars(r), **{n: getattr(r, n).at[0] for n in KEPT}})


def second_norm(sc, w, x):
    z, scale = ln_stats(x)
    sc.n2aug[C:CA, :] = ones_row((CA - C, T)).astype(BF)
    sc.n2aug[0:C, :] = (z * wide(w.vec[2]) + wide(w.vec[3])).astype(BF)
    return z, scale


def grid_place(groups_a):
    win = lax.axis_index(WIN)
    return (win // 4, win // 2 % 2, win % 2), (groups_a, 2, 2)


def neighbour(octant, sign, groups_a):
    place, sizes = grid_place(groups_a)
    a, b, c = (
        (p + sign * bit + n) % n for p, bit, n in zip(place, octant_bits(octant), sizes)
    )
    return lax.axis_index(VOL), (a * 2 + b) * 2 + c


def greet(peers):
    barrier = pltpu.get_barrier_semaphore()
    for peer in peers:
        pl.semaphore_signal(barrier, inc=1, device_id=peer, device_id_type=MESH)
    pl.semaphore_wait(barrier, len(peers))


def block_copy(r, m, octant, sign, groups_a):
    rows = pl.ds(OCT_OFF[octant], OCT_LEN[octant])
    source, target = r.stage.at[m % 2, rows], r.got.at[m, rows]
    if octant == 0:
        return pltpu.make_async_copy(source, target, r.sent.at[m % 2, 0])
    return pltpu.make_async_remote_copy(
        src_ref=source,
        dst_ref=target,
        send_sem=r.sent.at[m % 2, octant],
        recv_sem=r.arrived.at[m, octant],
        device_id=neighbour(octant, sign, groups_a),
        device_id_type=MESH,
    )


def wait_sent(r, m, sign, groups_a):
    for octant in range(8):
        copy = block_copy(r, m, octant, sign, groups_a)
        copy.wait_send() if octant else copy.wait()


def send_blocks(r, m, sign, groups_a):
    for octant in range(8):
        block_copy(r, m, octant, sign, groups_a).start()


def finish_blocks(r, steps, sign, groups_a):
    for m in range(max(steps - 2, 0), steps):
        wait_sent(r, m, sign, groups_a)

    def arrival(m, carry):
        for octant in range(1, 8):
            block_copy(r, m, octant, sign, groups_a).wait_recv()
        return carry

    lax.fori_loop(0, steps, arrival, 0)


def first_forward_kernel(groups_a, steps, r):
    w, sc = r, by_step(r)
    m = pl.program_id(0)

    @pl.when(m == 0)
    def _():
        greet([neighbour(octant, 1, groups_a) for octant in range(1, 8)])
        init_forward(r, sc)
        sc.pad[...] = jnp.zeros((C, T), BF)
        sc.cot[...] = jnp.zeros((C, T), BF)

    @pl.when(m >= 2)
    def _():
        wait_sent(r, m - 2, -1, groups_a)

    sc.pad[:, 0:WS] = r.tokens[0, 0]
    sc.cot[:, 0:WS] = r.cotangent[0, 0]
    slot = m % 2
    r.stage[slot, :, CA:] = jnp.concatenate(
        [dot(r.perm[...], sc.cot[...], NT), jnp.zeros((T, CA - C), F32)], axis=1
    ).astype(BF)
    places = r.places
    valid = (
        (places[0:1, :] < r.info[m, 1])
        & (places[1:2, :] < r.info[m, 2])
        & (places[2:3, :] < r.info[m, 3])
    )
    valid = jnp.where(valid, 1.0, 0.0)
    sc.codes[...] = jnp.broadcast_to(valid - 1.0, (128, T)).T
    x = sc.pad[...].astype(F32)
    sc.xT[...] = x
    x = x + forward_attention(sc, w, x, jnp.zeros((1, T), F32))
    sc.x1[...] = x
    second_norm(sc, w, x)
    for c in range(3):
        rows = slice(128 * c, 128 * c + 128)
        active, slope = gelu_pair(dot(w.upT[rows], sc.n2aug[...]))
        sc.act[rows, :] = active.astype(BF)
        sc.gp[rows, :] = slope.astype(BF)
    x = x + (dot(w.downT[...], sc.act[...]) + wide(w.vec[4]))
    row = lax.broadcasted_iota(jnp.int32, (CA - C, T), 0)
    label = r.info[m, 0].astype(F32)
    extra = jnp.where(row == 0, label, jnp.where(row == 1, valid, 0.0))
    x = jnp.concatenate([x, extra], axis=0).astype(BF)
    r.stage[slot, :, 0:CA] = dot(r.perm[...], x, NT).astype(BF)
    send_blocks(r, m, -1, groups_a)

    @pl.when(m == steps - 1)
    def _():
        finish_blocks(r, steps, -1, groups_a)


def second_kernel(groups_a, steps, r):
    w, sc = r, r
    m = pl.program_id(0)

    @pl.when(m == 0)
    def _():
        greet([neighbour(octant, -1, groups_a) for octant in range(1, 8)])
        init_forward(r, sc)
        init_backward(sc)

    @pl.when(m >= 2)
    def _():
        wait_sent(r, m - 2, 1, groups_a)

    came = r.came[0, :, 0:CA]
    x = dot(r.eye[...], came, NT)
    place, sizes = grid_place(groups_a)
    code_row = []
    for octant in range(8):
        rows = slice(OCT_OFF[octant], OCT_OFF[octant] + OCT_LEN[octant])
        wraps = [
            bit * jnp.where(p == n - 1, 1, 0)
            for p, bit, n in zip(place, octant_bits(octant), sizes)
        ]
        wrap = (wraps[0] * 4 + wraps[1] * 2 + wraps[2]).astype(F32)
        columns = came[rows].astype(F32)
        code = jnp.where(columns[:, C + 1 : C + 2] > 0.0, columns[:, C : C + 1] * 8.0 + wrap, -1.0)
        sc.codes[rows, :] = jnp.broadcast_to(code, (OCT_LEN[octant], 128))
        code_row.append(jnp.full((1, OCT_LEN[octant]), wrap))
    code_row = jnp.concatenate(code_row, axis=1) + 8.0 * x[C : C + 1]
    keep = x[C + 1 : C + 2]
    x = x[0:C]
    d = dot(r.eye[0:C], r.came[0, :, CA:], NT) * keep
    dd = d.astype(BF)
    sc.xT[...] = x
    branch = forward_attention(sc, w, x, code_row)
    x = x + branch.astype(BF).astype(F32)
    z, scale = second_norm(sc, w, x)
    for c in range(3):
        rows = slice(128 * c, 128 * c + 128)
        active, slope = gelu_pair(dot(w.upT[rows], sc.n2aug[...]))
        sc.act[rows, :] = active.astype(BF)
        sc.dh[rows, :] = (dot(w.down[rows], dd) * slope).astype(BF)
    x = x + (dot(w.downT[...], sc.act[...]) + wide(w.vec[4]))
    slot = m % 2
    none = jnp.zeros((CA - C, T), F32)
    r.stage[slot, :, 0:CA] = jnp.concatenate([x * keep, none], axis=0).T.astype(BF)
    d = feed_forward_back(sc, w, d, dd, z, scale)
    z, scale = ln_stats(sc.xT[...])
    d = backward_attention(sc, w, d, z, scale, True)
    r.stage[slot, :, CA:] = jnp.concatenate([d, none], axis=0).T.astype(BF)
    send_blocks(r, m, 1, groups_a)

    @pl.when(m == steps - 1)
    def _():
        finish_blocks(r, steps, 1, groups_a)
        write_grads(sc, r.grads)


def first_backward_kernel(steps, r):
    w, sc = r, by_step(r)
    m = pl.program_id(0)

    @pl.when(m == 0)
    def _():
        init_backward(sc)

    came = dot(r.eye[...], r.came[0], NT).astype(BF)
    came = dot(came, r.perm[...])
    r.output[0, 0] = came[0:C, 0:WS].astype(BF)
    d = came[CA : CA + C]
    dd = d.astype(BF)
    z, scale = ln_stats(sc.x1[...])
    for c in range(3):
        rows = slice(128 * c, 128 * c + 128)
        sc.dh[rows, :] = (dot(w.down[rows], dd) * sc.gp[rows, :].astype(F32)).astype(BF)
    d = feed_forward_back(sc, w, d, dd, z, scale)
    z, scale = ln_stats(sc.xT[...])
    d = backward_attention(sc, w, d, z, scale, False)
    r.input_grad[0, 0] = d[:, 0:WS]

    @pl.when(m == steps - 1)
    def _():
        write_grads(sc, r.grads)


def shard_rows(device, shard_len):
    return device * shard_len // C, -(-(device + 1) * shard_len // C)


def flat_offset(device, shard_len):
    return device * shard_len % C


def slab_rows(shard_len):
    return -(-((shard_len + C - 2) // C + 1) // 16) * 16


def own_place():
    win = lax.axis_index(WIN)
    return lax.axis_index(VOL), win // 2, win % 2


def all_peers(n_vol, n_plane):
    vol, plane, core = own_place()
    return (
        [((vol + j) % n_vol, plane * 2 + core) for j in range(1, n_vol)]
        + [(vol, (plane + j) % n_plane * 2 + core) for j in range(1, n_plane)]
        + [(vol, plane * 2 + 1 - core)]
    )


def transpose_with(matrix, extra):
    below = jnp.where(lax.broadcasted_iota(jnp.int32, (CA - C, C), 0) == 0, extra, 0.0)
    return jnp.concatenate([matrix, below], axis=0).T


def gather_kernel(n_vol, n_plane, shard_len, r):
    vol, plane, core = own_place()
    peers = all_peers(n_vol, n_plane)
    greet(peers)
    buf = r.buf

    def copy(ref, n):
        return pltpu.make_async_remote_copy(
            src_ref=ref,
            dst_ref=ref,
            send_sem=r.sent.at[n],
            recv_sem=r.arrived.at[n],
            device_id=peers[n],
            device_id_type=MESH,
        )

    buf[core, plane, vol] = r.shard[...]
    stages = [
        [copy(buf.at[core, plane, vol], n) for n in range(n_vol - 1)],
        [copy(buf.at[core, plane], n_vol - 1 + n) for n in range(n_plane - 1)],
        [copy(buf.at[core], n_vol + n_plane - 2)],
    ]
    for copies in stages:
        for c in copies:
            c.start()
        for c in copies:
            c.wait()
    flat = r.flat
    flat[...] = jnp.zeros(flat.shape, F32)
    for v in range(n_vol):
        for p in range(n_plane):
            for c in range(2):
                start, stop = shard_rows((v * n_plane + p) * 2 + c, shard_len)
                flat[start:stop, :] += buf[c, p, v, 0 : stop - start].astype(F32)
    for layer in range(2):
        at = layer * BLOCK_ROWS

        def rows(start, count=C, stride=1):
            return flat[pl.ds(at + start, count, stride), :]

        def vector(n):
            return rows(12 * C + n, 1)

        o = {n: getattr(r, n).at[layer] for n in WEIGHTS}
        o = SimpleNamespace(**o)
        none = jnp.zeros((1, C), F32)
        wq, wk, wv = (rows(n, C, 3) for n in range(3))
        o.q[...] = wq.astype(BF)
        o.kv96[...] = jnp.concatenate([wk, wv], axis=1).astype(BF)
        o.qkvT[0:C, :] = (transpose_with(wq, vector(2)) * 0.25).astype(BF)
        o.qkvT[C : 2 * C, :] = (transpose_with(wk, none) * 0.25).astype(BF)
        o.qkvT[2 * C :, :] = transpose_with(wv, vector(3)).astype(BF)
        row = lax.broadcasted_iota(jnp.int32, (CA - C, CA), 0)
        lane = lax.broadcasted_iota(jnp.int32, (CA - C, CA), 1)
        blank = jnp.zeros((C, CA - C), F32)
        bias_v = jnp.concatenate([vector(3), blank[0:1]], axis=1)
        ones = jnp.where((lane == C) | (lane == C + 1), 1.0, bias_v)
        o.kv[0:C, :] = jnp.concatenate([wk, blank, wv, blank], axis=1).astype(BF)
        o.kv[C:, 0:CA] = jnp.zeros((CA - C, CA), BF)
        o.kv[C:, CA:] = jnp.where(row == 0, ones, 0.0).astype(BF)
        proj = rows(3 * C)
        o.proj[...] = proj.astype(BF)
        o.projT[...] = transpose_with(proj, vector(4)).astype(BF)
        ups = [rows(4 * C + j, C, 4) for j in range(4)]
        o.up[...] = jnp.concatenate(ups, axis=1).astype(BF)
        for j in range(4):
            o.upT[C * j : C * j + C, :] = transpose_with(ups[j], vector(8 + j)).astype(BF)
        down = rows(8 * C, FF)
        o.down[...] = down.astype(BF)
        o.downT[...] = down.T.astype(BF)
        for n, source in enumerate((0, 1, 5, 6, 7)):
            o.vec[n] = jnp.broadcast_to(vector(source), (128, C)).T


def reduce_kernel(n_vol, n_plane, shard_len, r):
    vol, plane, core = own_place()
    peers = all_peers(n_vol, n_plane)
    greet(peers)
    work = r.work
    half = 2 * n_vol * n_plane // 2
    for v in range(n_vol):
        for p in range(n_plane):
            for c in range(2):
                device = (v * n_plane + p) * 2 + c
                start, stop = shard_rows(device, shard_len)
                source = (r.first, r.second)[device // half]
                start, stop = (n - device // half * BLOCK_ROWS for n in (start, stop))
                work[c, p, v, 0 : stop - start] = source[start:stop, :]

    def copy(source, target, n):
        return pltpu.make_async_remote_copy(
            src_ref=source,
            dst_ref=target,
            send_sem=r.sent.at[n],
            recv_sem=r.arrived.at[n],
            device_id=peers[n],
            device_id_type=MESH,
        )

    def exchange(copies):
        for c in copies:
            c.start()
        for c in copies:
            c.wait()

    exchange([copy(work.at[1 - core], r.from_core, n_vol + n_plane - 2)])
    work[core] += r.from_core[...]
    exchange(
        [
            copy(work.at[core, (plane + j) % n_plane], r.from_plane.at[j - 1], n_vol - 2 + j)
            for j in range(1, n_plane)
        ]
    )
    total = work[core, plane]
    for j in range(n_plane - 1):
        total = total + r.from_plane[j]
    work[core, plane] = total
    exchange(
        [
            copy(work.at[core, plane, (vol + j) % n_vol], r.from_vol.at[j - 1], j - 1)
            for j in range(1, n_vol)
        ]
    )
    total = work[core, plane, vol]
    for j in range(n_vol - 1):
        total = total + r.from_vol[j]
    r.total[...] = total


def call(kernel, steps, ins, outs, scratch, semaphores=(), collective_id=None):
    def spec(shape, kind):
        if kind is SMEM:
            return pl.BlockSpec(memory_space=pltpu.SMEM)
        if kind is HBM:
            return pl.BlockSpec(memory_space=pl.ANY)
        zeros = (0,) * (len(shape) - 1)
        if kind is BY_STEP:
            return pl.BlockSpec((1,) + tuple(shape[1:]), lambda m: (m,) + zeros)
        if kind in (0, 1):
            return pl.BlockSpec((pl.squeezed,) + tuple(shape[1:]), lambda m: (kind,) + zeros)
        return pl.BlockSpec(tuple(shape), lambda m: (0,) + zeros)

    semaphores = dict(semaphores)
    names = tuple(ins) + tuple(outs) + tuple(scratch) + tuple(semaphores)

    def body(*refs):
        kernel(SimpleNamespace(**dict(zip(names, refs))))

    results = pl.pallas_call(
        body,
        grid=(steps,),
        in_specs=[spec(a.shape, kind) for a, kind in ins.values()],
        out_specs=[spec(shape, kind) for shape, _, kind in outs.values()],
        out_shape=[jax.ShapeDtypeStruct(shape, dtype) for shape, dtype, _ in outs.values()],
        scratch_shapes=[pltpu.VMEM(shape, dtype) for shape, dtype in scratch.values()]
        + [pltpu.SemaphoreType.DMA(shape) for shape in semaphores.values()],
        compiler_params=pltpu.CompilerParams(
            vmem_limit_bytes=60 * 2**20,
            collective_id=collective_id,
            has_side_effects=collective_id is not None,
        ),
    )(*[a for a, _ in ins.values()])
    return SimpleNamespace(**dict(zip(outs, results)))


WEIGHTS = dict(
    qkvT=((3 * C, CA), BF),
    kv=((CA, 2 * CA), BF),
    projT=((C, CA), BF),
    proj=((C, C), BF),
    upT=((FF, CA), BF),
    up=((C, FF), BF),
    downT=((C, FF), BF),
    down=((FF, C), BF),
    q=((C, C), BF),
    kv96=((C, 2 * C), BF),
    vec=((5, C, 128), F32),
)


def on_device(
    tokens,
    cotangent,
    position_bias,
    window_volume,
    clip_extent,
    master,
    first_moment,
    second_moment,
):
    n_vol, n_win = lax.axis_size(VOL), lax.axis_size(WIN)
    groups_a, n_plane = n_win // 4, n_win // 2
    steps = tokens.shape[0]
    shard_len = master.shape[0]
    device = lax.axis_index((VOL, WIN))
    slab = slab_rows(shard_len)
    offset = flat_offset(device, shard_len)
    shard = lax.dynamic_update_slice(jnp.zeros((slab * C,), BF), master.astype(BF), (offset,))
    n_peers = n_vol + n_plane - 1
    weights = call(
        lambda r: gather_kernel(n_vol, n_plane, shard_len, r),
        1,
        dict(shard=(shard.reshape(slab, C), WHOLE)),
        {n: ((2,) + shape, dtype, WHOLE) for n, (shape, dtype) in WEIGHTS.items()},
        dict(
            buf=((2, n_plane, n_vol, slab, C), BF),
            flat=((2 * BLOCK_ROWS + 8, C), F32),
        ),
        dict(sent=(n_peers,), arrived=(n_peers,)),
        collective_id=0,
    )
    info = jnp.concatenate((window_volume[:, :, None], clip_extent), axis=2)[:, 0]

    def layer(which):
        return {n: (a, which) for n, a in vars(weights).items()}

    def table(which, order):
        return dict(order=(jnp.asarray(order, BF), WHOLE), table=(position_bias, which))

    perm = (jnp.asarray(PERM, BF), WHOLE)
    eye = (jnp.asarray(np.eye(CA), BF), WHOLE)
    stage = dict(stage=((2, T, 2 * CA), BF))
    copies = dict(sent=(2, 8), arrived=(steps, 8))
    got = call(
        lambda r: first_forward_kernel(groups_a, steps, r),
        steps,
        dict(
            tokens=(tokens.transpose(0, 1, 3, 2), BY_STEP),
            cotangent=(cotangent.transpose(0, 1, 3, 2), BY_STEP),
            info=(info, SMEM),
            perm=perm,
            places=(jnp.asarray(PLACES), WHOLE),
            **table(0, np.eye(T, WS)),
            **layer(0),
        ),
        dict(
            got=((steps, T, 2 * CA), BF, HBM),
            **{n: ((steps,) + shape, dtype, BY_STEP) for n, (shape, dtype) in KEPT.items()},
        ),
        dict(**FWD, **stage, pad=((C, T), BF), cot=((C, T), BF)),
        copies,
        collective_id=1,
    )
    second = call(
        lambda r: second_kernel(groups_a, steps, r),
        steps,
        dict(
            came=(got.got, BY_STEP),
            eye=eye,
            **table(1, ORDER),
            **layer(1),
        ),
        dict(
            got=((steps, T, 2 * CA), BF, HBM),
            grads=((BLOCK_ROWS, C), F32, WHOLE),
        ),
        dict(**FWD, **KEPT, **BWD, **stage),
        copies,
        collective_id=2,
    )
    first = call(
        lambda r: first_backward_kernel(steps, r),
        steps,
        dict(
            came=(second.got, BY_STEP),
            perm=perm,
            eye=(jnp.asarray(np.eye(2 * CA), BF), WHOLE),
            **{n: (getattr(got, n), BY_STEP) for n in KEPT},
            **layer(0),
        ),
        dict(
            output=((steps, 1, C, WS), BF, BY_STEP),
            input_grad=((steps, 1, C, WS), F32, BY_STEP),
            grads=((BLOCK_ROWS, C), F32, WHOLE),
        ),
        BWD,
    )
    reduced = call(
        lambda r: reduce_kernel(n_vol, n_plane, shard_len, r),
        1,
        dict(first=(first.grads, WHOLE), second=(second.grads, WHOLE)),
        dict(total=((slab, C), F32, WHOLE)),
        dict(
            work=((2, n_plane, n_vol, slab, C), F32),
            from_core=((n_plane, n_vol, slab, C), F32),
            from_plane=((n_plane - 1, n_vol, slab, C), F32),
            from_vol=((n_vol - 1, slab, C), F32),
        ),
        dict(sent=(n_peers,), arrived=(n_peers,)),
        collective_id=3,
    )
    shard_grad = lax.dynamic_slice(reduced.total.reshape(-1), (offset,), (shard_len,))
    position = (device * shard_len + jnp.arange(shard_len, dtype=jnp.int32)) % (BLOCK_ROWS * C)
    is_vector = position >= 12 * C * C
    step_rate = jnp.where(is_vector, RATE_VECTOR, RATE_MATRIX)
    weight_decay = jnp.where(is_vector, 0.0, DECAY_MATRIX)
    moment_one = BETA_FIRST * first_moment + (1.0 - BETA_FIRST) * shard_grad
    moment_two = BETA_SECOND * second_moment + (1.0 - BETA_SECOND) * shard_grad * shard_grad
    corrected_one = moment_one / (1.0 - BETA_FIRST**STEP)
    corrected_two = moment_two / (1.0 - BETA_SECOND**STEP)
    normalized = corrected_one / (jnp.sqrt(corrected_two) + ADAM_EPS)
    new_master = master - step_rate * (normalized + weight_decay * master)
    return (
        first.output.transpose(0, 1, 3, 2),
        first.input_grad.transpose(0, 1, 3, 2),
        new_master,
        moment_one,
        moment_two,
        new_master.astype(BF),
    )


def solution(mesh):
    placed = (
        P(None, (VOL, WIN), None, None),
        P(None, (VOL, WIN), None, None),
        P(),
        P(None, (VOL, WIN)),
        P(None, (VOL, WIN), None),
        P((VOL, WIN)),
        P((VOL, WIN)),
        P((VOL, WIN)),
    )
    return jax.shard_map(
        on_device,
        mesh=mesh,
        in_specs=placed,
        out_specs=(
            P(None, (VOL, WIN), None, None),
            P(None, (VOL, WIN), None, None),
            P((VOL, WIN)),
            P((VOL, WIN)),
            P((VOL, WIN)),
            P((VOL, WIN)),
        ),
        check_vma=False,
    )
```

```python
from types import SimpleNamespace

import jax
import jax.numpy as jnp
import numpy as np
from jax import lax
from jax.experimental import pallas as pl
from jax.experimental.pallas import tpu as pltpu
from jax.sharding import PartitionSpec as P

C = 96
HEADS = 6
HEAD_DIM = 16
FF = 384
SIDE = 7
SHIFT = 3
WS = 343
STEP = 6
T = 384
WINDOWS = 2
CA = 128
BLOCK_ROWS = 1164

NORM_EPS = 1e-05
MASK_FILL = -1000000000.0
BETA_FIRST = 0.5
BETA_SECOND = 0.5
ADAM_EPS = 1e-08
RATE_MATRIX = 0.1
RATE_VECTOR = 0.4
DECAY_MATRIX = 0.05

BF = jnp.bfloat16
F32 = jnp.float32
NN = (((1,), (0,)), ((), ()))
NT = (((1,), (1,)), ((), ()))
BY_STEP, WHOLE, SMEM, HBM = -1, -2, -3, -4
MESH = pl.DeviceIdType.MESH
VOL, WIN = "vol", "win"


def octant_bits(octant):
    return (octant >> 2 & 1, octant >> 1 & 1, octant & 1)


OCT_SIZE = []
OCT_LEN = []
OCT_OFF = []
for _octant in range(8):
    _size = 1
    for _bit in octant_bits(_octant):
        _size *= SHIFT if _bit else SIDE - SHIFT
    OCT_OFF.append(sum(OCT_LEN))
    OCT_SIZE.append(_size)
    OCT_LEN.append(-(-_size // 16) * 16)


def slot_tables():
    perm = np.zeros((T, T), np.float32)
    order = np.zeros((T, WS), np.float32)
    places = np.full((8, T), 99, np.int32)
    for octant in range(8):
        bits = octant_bits(octant)
        lens = [SHIFT if bit else SIDE - SHIFT for bit in bits]
        for i in range(lens[0]):
            for j in range(lens[1]):
                for k in range(lens[2]):
                    source = [v if bit else v + SHIFT for v, bit in zip((i, j, k), bits)]
                    own = [v + bit * (SIDE - SHIFT) for v, bit in zip((i, j, k), bits)]
                    q = OCT_OFF[octant] + (i * lens[1] + j) * lens[2] + k
                    t = (source[0] * SIDE + source[1]) * SIDE + source[2]
                    perm[q, t] = 1
                    order[q, (own[0] * SIDE + own[1]) * SIDE + own[2]] = 1
                    places[:3, t] = source
    return perm, order, places


PERM, ORDER, PLACES = slot_tables()


def dot(a, b, dims=NN):
    return lax.dot_general(a, b, dims, preferred_element_type=F32)


def wide(column):
    return jnp.concatenate([column] * (T // 128), axis=1)


def ln_stats(x):
    centred = x - jnp.mean(x, axis=0, keepdims=True)
    scale = lax.rsqrt(jnp.mean(centred * centred, axis=0, keepdims=True) + NORM_EPS)
    return centred * scale, scale


def norm_back(e, z, scale, gain):
    eg = e * gain
    return scale * (
        eg - jnp.mean(eg, axis=0, keepdims=True) - z * jnp.mean(eg * z, axis=0, keepdims=True)
    )


def gelu_pair(h):
    base = 1.0 + (0.3275911 * 0.7071067811865476) * jnp.abs(h)
    t = pl.reciprocal(base, approx=True)
    t = t * (2.0 - base * t)
    poly = t * (
        0.5 * 0.254829592
        + t
        * (
            0.5 * -0.284496736
            + t * (0.5 * 1.421413741 + t * (0.5 * -1.453152027 + t * (0.5 * 1.061405429)))
        )
    )
    bell = jnp.exp(-0.5 * (h * h))
    tail = poly * bell
    phi = jnp.where(h < 0.0, tail, 1.0 - tail)
    return h * phi, phi + h * bell * 0.3989422804014327


def ones_row(shape, row=0):
    return jnp.where(lax.broadcasted_iota(jnp.int32, shape, 0) == row, 1.0, 0.0)


def weave(tasks, lag):
    clocks = [lag * n for n in range(len(tasks))]
    while tasks:
        n = clocks.index(min(clocks))
        cost = next(tasks[n], None)
        if cost is None:
            tasks, clocks = (x[:n] + x[n + 1 :] for x in (tasks, clocks))
        else:
            clocks[n] += cost


def init_forward(r, windows):
    for sc in windows:
        sc.qb[...] = jnp.zeros((CA, HEADS * T), BF)
        for h in range(HEADS):
            sc.vt[h, 16:32, :] = ones_row((16, T)).astype(BF)
    for h in range(HEADS):
        turned = dot(r.order[...], r.table[h], NT).astype(BF)
        r.bias[h] = dot(turned, r.order[...], NT)


def init_backward(r, windows):
    for sc in windows:
        sc.dab[...] = jnp.zeros((CA, HEADS * T), BF)
        sc.rb[...] = jnp.zeros((2 * C, 2 * HEADS * T), BF)
    for name, (shape, dtype) in GRADS.items():
        getattr(r, name)[...] = jnp.zeros(shape, dtype)


def set_queries(sc, queries):
    for h in range(HEADS):
        sc.qb[16 * h : 16 * h + 16, T * h : T * h + T] = queries[16 * h : 16 * h + 16, :]


def forward_attention(sc, w, st, code_row):
    z, _ = ln_stats(st.x)
    sc.n1aug[C:CA, :] = ones_row((CA - C, T)).astype(BF)
    sc.attaug[C:CA, :] = ones_row((CA - C, T)).astype(BF)
    sc.n1aug[0:C, :] = (z * wide(w.vec[0]) + wide(w.vec[1])).astype(BF)
    yield 150
    kv = dot(sc.n1aug[...].T, w.kv[...]).astype(BF)
    sc.kn[...] = kv[:, 0:CA]
    sc.vn[...] = kv[:, CA:]
    yield 200
    qkv = dot(w.qkvT[...], sc.n1aug[...])
    queries = qkv[0:C].astype(BF)
    set_queries(sc, queries)
    sc.qT[...] = queries
    sc.kT[...] = qkv[C : 2 * C].astype(BF)
    values = qkv[2 * C :].astype(BF)
    for h in range(HEADS):
        sc.vt[h, 0:16, :] = values[16 * h : 16 * h + 16, :]
    yield 150
    eye = lax.broadcasted_iota(jnp.int32, (128, 128), 0) == lax.broadcasted_iota(
        jnp.int32, (128, 128), 1
    )
    tops = [None] * HEADS

    def scores(h, c):
        rows = slice(128 * c, 128 * c + 128)
        x_all = dot(sc.kn[rows], sc.qb[:, T * h : T * h + T])
        codes = sc.codes[rows]
        parts = []
        for j in range(3):
            lanes = slice(128 * j, 128 * j + 128)
            allowed = codes == code_row[:, lanes]
            if j == c:
                allowed = allowed | eye
            part = jnp.where(allowed, x_all[:, lanes] + sc.bias[h, rows, lanes], MASK_FILL)
            sc.s[h % 3, rows, lanes] = part
            parts.append(jnp.max(part.reshape(16, 8, 128), axis=0))
        top = jnp.concatenate(parts, axis=1)
        tops[h] = top if tops[h] is None else jnp.maximum(tops[h], top)

    def raise_(h, c):
        rows = slice(128 * c, 128 * c + 128)
        sc.e[rows, T * h : T * h + T] = jnp.exp(sc.s[h % 3, rows] - tops[h]).astype(BF)

    def attend(h):
        out = dot(sc.vt[h], sc.e[:, T * h : T * h + T])
        inverse = 1.0 / out[16:17]
        part = out[0:16] * inverse
        sc.att[16 * h : 16 * h + 16, :] = part
        sc.inv[h : h + 1, :] = inverse
        sc.attaug[16 * h : 16 * h + 16, :] = part.astype(BF)

    for h in range(HEADS + 2):
        for c in range(3):
            if h < HEADS:
                scores(h, c)
            if 0 <= h - 1 < HEADS:
                raise_(h - 1, c)
            if c == 0 and 0 <= h - 2 < HEADS:
                attend(h - 2)
            yield 70
        if h < HEADS:
            tops[h] = jnp.max(tops[h], axis=0, keepdims=True)
    st.branch = dot(w.projT[...], sc.attaug[...])
    yield 100


def backward_attention(sc, w, st, z, scale, shifted):
    d_mid = st.d
    db = d_mid.astype(BF)
    d_att = dot(w.proj[...], db).astype(BF).astype(F32)
    sc.gproj[...] += dot(sc.attaug[...], db, NT)
    yield 150
    row = lax.broadcasted_iota(jnp.int32, (16, T), 0)
    for h in range(HEADS):
        part = (d_att[16 * h : 16 * h + 16] * sc.inv[h : h + 1, :]).astype(BF)
        cols = slice(T * h, T * h + T)
        sc.dab[16 * h : 16 * h + 16, cols] = part
        sc.rb[C + 16 * h : C + 16 * h + 16, 2 * T * h : 2 * T * h + T] = part
        sc.rb[16 * h : 16 * h + 16, 2 * T * h + T : 2 * T * h + 2 * T] = sc.qT[
            16 * h : 16 * h + 16, :
        ]
        inner = -jnp.sum(
            part.astype(F32) * sc.att[16 * h : 16 * h + 16, :], axis=0, keepdims=True
        )
        high = inner.astype(BF).astype(F32)
        low = inner - high
        sc.dab[C : C + 16, cols] = jnp.where(
            row == 0, high, jnp.where(row == 1, low, 0.0)
        ).astype(BF)
    yield 100
    total = None

    def soft(h):
        cols = slice(T * h, T * h + T)
        pull = dot(sc.vn[...], sc.dab[:, cols])
        sc.ds[:, cols] = (pull * sc.e[:, cols].astype(F32)).astype(BF)

    def to_queries(h):
        sc.dq[16 * h : 16 * h + 16, :] = dot(
            sc.kT[16 * h : 16 * h + 16, :], sc.ds[:, T * h : T * h + T]
        ).astype(BF)

    for h in range(HEADS + 1):
        if h < HEADS:
            soft(h)
            yield 120
        if h > 0:
            cols = slice(T * (h - 1), T * h)
            to_queries(h - 1)
            yield 60
            both = jnp.concatenate([sc.e[:, cols], sc.ds[:, cols]], axis=1)
            term = dot(both, sc.rb[:, 2 * T * (h - 1) : 2 * T * h], NT)
            total = term if total is None else total + term
            yield 180
    dkv = total.astype(BF)
    dq = sc.dq[...]
    dn = dot(w.q[...], dq) + dot(w.kv96[...], dkv, NT)
    yield 120
    sc.gkv[...] += dot(sc.n1aug[...], dkv)
    sc.gq[...] += dot(dq, sc.n1aug[...], NT)
    yield 150
    if shifted:
        dn = dn.astype(BF).astype(F32)
    sc.gvec[0] += dn * z
    sc.gvec[1] += dn
    st.d = d_mid + norm_back(dn, z, scale, wide(w.vec[0]))
    yield 150


def feed_forward_back(sc, w, st, dd, z, scale):
    dn = dot(w.up[...], sc.dh[...])
    yield 120
    sc.gdown[...] += dot(sc.act[...], dd, NT)
    yield 120
    sc.gup[...] += dot(sc.dh[...], sc.n2aug[...], NT)
    yield 120
    sc.gvec[4] += dd.astype(F32)
    sc.gvec[2] += dn * z
    sc.gvec[3] += dn
    st.d = st.d + norm_back(dn, z, scale, wide(w.vec[2]))
    yield 150


def write_grads(sc, out):
    gq = sc.gq[...].T
    gkv = sc.gkv[...]
    gup = sc.gup[...].T
    out[pl.ds(0, C, 3), :] = gq[0:C]
    out[pl.ds(1, C, 3), :] = gkv[0:C, 0:C]
    out[pl.ds(2, C, 3), :] = gkv[0:C, C : 2 * C]
    out[3 * C : 4 * C, :] = sc.gproj[0:C, :]
    for j in range(4):
        out[pl.ds(4 * C + j, C, 4), :] = gup[0:C, C * j : C * j + C]
    out[8 * C : 12 * C, :] = sc.gdown[...]
    sums = [jnp.sum(sc.gvec[n].T, axis=0, keepdims=True) for n in range(5)]
    rows = [
        sums[0],
        sums[1],
        gq[C : C + 1],
        gkv[C : C + 1, C : 2 * C],
        sc.gproj[C : C + 1, :],
        sums[2],
        sums[3],
        sums[4],
    ] + [gup[C : C + 1, C * j : C * j + C] for j in range(4)]
    for n, value in enumerate(rows):
        out[12 * C + n : 12 * C + n + 1, :] = value


FWD = dict(
    qb=((CA, HEADS * T), BF),
    vt=((HEADS, 32, T), BF),
    kn=((T, CA), BF),
    codes=((T, 128), F32),
    s=((3, T, T), F32),
)
BIAS = dict(bias=((HEADS, T, T), F32))
KEPT = dict(
    qT=((C, T), BF),
    kT=((C, T), BF),
    vn=((T, CA), BF),
    e=((T, HEADS * T), BF),
    att=((C, T), F32),
    inv=((8, T), F32),
    attaug=((CA, T), BF),
    n1aug=((CA, T), BF),
    n2aug=((CA, T), BF),
    act=((FF, T), BF),
    gp=((FF, T), BF),
    xT=((C, T), F32),
    x1=((C, T), F32),
)
GRADS = dict(
    gq=((C, CA), F32),
    gkv=((CA, 2 * C), F32),
    gproj=((CA, C), F32),
    gup=((FF, CA), F32),
    gdown=((FF, C), F32),
    gvec=((5, C, T), F32),
)
BWD = dict(
    dab=((CA, HEADS * T), BF),
    rb=((2 * C, 2 * HEADS * T), BF),
    ds=((T, HEADS * T), BF),
    dq=((C, T), BF),
    dh=((FF, T), BF),
)


PADS = dict(pad=((C, T), BF), cot=((C, T), BF))
LAGS = (0, 0, 0)


def by_window(r, own):
    return [
        SimpleNamespace(**{**vars(r), **{n: getattr(r, n).at[i] for n in own if hasattr(r, n)}})
        for i in range(WINDOWS)
    ]


def second_norm(sc, w, x):
    z, scale = ln_stats(x)
    sc.n2aug[C:CA, :] = ones_row((CA - C, T)).astype(BF)
    sc.n2aug[0:C, :] = (z * wide(w.vec[2]) + wide(w.vec[3])).astype(BF)
    return z, scale


def grid_place(groups_a):
    win = lax.axis_index(WIN)
    return (win // 4, win // 2 % 2, win % 2), (groups_a, 2, 2)


def neighbour(octant, sign, groups_a):
    place, sizes = grid_place(groups_a)
    a, b, c = (
        (p + sign * bit + n) % n for p, bit, n in zip(place, octant_bits(octant), sizes)
    )
    return lax.axis_index(VOL), (a * 2 + b) * 2 + c


def greet(peers):
    barrier = pltpu.get_barrier_semaphore()
    for peer in peers:
        pl.semaphore_signal(barrier, inc=1, device_id=peer, device_id_type=MESH)


def await_greetings(peers):
    pl.semaphore_wait(pltpu.get_barrier_semaphore(), len(peers))


def block_copy(r, m, octant, sign, groups_a):
    rows = pl.ds(OCT_OFF[octant], OCT_LEN[octant])
    slot = m % 2
    source = r.stage.at[slot, :, rows]
    target = r.got.at[pl.ds(m * WINDOWS, WINDOWS), rows]
    if octant == 0:
        return pltpu.make_async_copy(source, target, r.sent.at[slot, 0])
    return pltpu.make_async_remote_copy(
        src_ref=source,
        dst_ref=target,
        send_sem=r.sent.at[slot, octant],
        recv_sem=r.arrived.at[m, octant],
        device_id=neighbour(octant, sign, groups_a),
        device_id_type=MESH,
    )


def wait_sent(r, m, sign, groups_a):
    for octant in range(8):
        copy = block_copy(r, m, octant, sign, groups_a)
        copy.wait_send() if octant else copy.wait()


def send_blocks(r, m, sign, groups_a):
    @pl.when(m == 0)
    def _():
        pl.semaphore_wait(pltpu.get_barrier_semaphore(), 7)

    for octant in range(8):
        block_copy(r, m, octant, sign, groups_a).start()


def finish_blocks(r, steps, sign, groups_a):
    for m in range(max(steps - 2, 0), steps):
        wait_sent(r, m, sign, groups_a)

    def arrival(m, carry):
        for octant in range(1, 8):
            block_copy(r, m, octant, sign, groups_a).wait_recv()
        return carry

    lax.fori_loop(0, steps, arrival, 0)


def first_forward(r, sc, m, i):
    w, st = r, SimpleNamespace()
    slot = m % 2
    sc.pad[:, 0:WS] = r.tokens[i, 0]
    st.x = sc.pad[...].astype(F32)
    sc.xT[...] = st.x
    places = r.places
    valid = (
        (places[0:1, :] < r.info[m * WINDOWS + i, 1])
        & (places[1:2, :] < r.info[m * WINDOWS + i, 2])
        & (places[2:3, :] < r.info[m * WINDOWS + i, 3])
    )
    valid = jnp.where(valid, 1.0, 0.0)
    sc.codes[...] = jnp.broadcast_to(valid - 1.0, (128, T)).T
    yield 100
    yield from forward_attention(sc, w, st, jnp.zeros((1, T), F32))
    sc.cot[:, 0:WS] = r.cotangent[i, 0]
    r.stage[slot, i, :, CA:] = jnp.concatenate(
        [dot(r.perm[...], sc.cot[...], NT), jnp.zeros((T, CA - C), F32)], axis=1
    ).astype(BF)
    yield 100
    x = st.x + st.branch
    sc.x1[...] = x
    second_norm(sc, w, x)
    yield 150
    for c in range(6):
        rows = slice(64 * c, 64 * c + 64)
        active, slope = gelu_pair(dot(w.upT[rows], sc.n2aug[...]))
        sc.act[rows, :] = active.astype(BF)
        sc.gp[rows, :] = slope.astype(BF)
        yield 100
    x = x + (dot(w.downT[...], sc.act[...]) + wide(w.vec[4]))
    yield 100
    row = lax.broadcasted_iota(jnp.int32, (CA - C, T), 0)
    label = r.info[m * WINDOWS + i, 0].astype(F32)
    extra = jnp.where(row == 0, label, jnp.where(row == 1, valid, 0.0))
    x = jnp.concatenate([x, extra], axis=0).astype(BF)
    r.stage[slot, i, :, 0:CA] = dot(r.perm[...], x, NT).astype(BF)
    yield 100


def first_forward_kernel(groups_a, steps, lag, r):
    windows = by_window(r, dict(**FWD, **KEPT, **PADS))
    m = pl.program_id(0)

    @pl.when(m == 0)
    def _():
        greet([neighbour(octant, 1, groups_a) for octant in range(1, 8)])
        init_forward(r, windows)
        for sc in windows:
            sc.pad[...] = jnp.zeros((C, T), BF)
            sc.cot[...] = jnp.zeros((C, T), BF)

    @pl.when(m >= 2)
    def _():
        wait_sent(r, m - 2, -1, groups_a)

    weave([first_forward(r, sc, m, i) for i, sc in enumerate(windows)], lag)
    send_blocks(r, m, -1, groups_a)

    @pl.when(m == steps - 1)
    def _():
        finish_blocks(r, steps, -1, groups_a)


def second_layer(r, sc, m, i, groups_a):
    w, st = r, SimpleNamespace()
    came = r.came[i, :, 0:CA]
    x = dot(r.eye[...], came, NT)
    place, sizes = grid_place(groups_a)
    code_row = []
    for octant in range(8):
        rows = slice(OCT_OFF[octant], OCT_OFF[octant] + OCT_LEN[octant])
        wraps = [
            bit * jnp.where(p == n_ - 1, 1, 0)
            for p, bit, n_ in zip(place, octant_bits(octant), sizes)
        ]
        wrap = (wraps[0] * 4 + wraps[1] * 2 + wraps[2]).astype(F32)
        columns = came[rows].astype(F32)
        code = jnp.where(columns[:, C + 1 : C + 2] > 0.0, columns[:, C : C + 1] * 8.0 + wrap, -1.0)
        sc.codes[rows, :] = jnp.broadcast_to(code, (OCT_LEN[octant], 128))
        code_row.append(jnp.full((1, OCT_LEN[octant]), wrap))
    code_row = jnp.concatenate(code_row, axis=1) + 8.0 * x[C : C + 1]
    keep = x[C + 1 : C + 2]
    x = x[0:C]
    sc.xT[...] = x
    st.x = x
    yield 150
    yield from forward_attention(sc, w, st, code_row)
    st.d = dot(r.eye[0:C], r.came[i, :, CA:], NT) * keep
    dd = st.d.astype(BF)
    x = sc.xT[...] + st.branch.astype(BF).astype(F32)
    z, scale = second_norm(sc, w, x)
    yield 200
    for c in range(6):
        rows = slice(64 * c, 64 * c + 64)
        active, slope = gelu_pair(dot(w.upT[rows], sc.n2aug[...]))
        sc.act[rows, :] = active.astype(BF)
        sc.dh[rows, :] = (dot(w.down[rows], dd) * slope).astype(BF)
        yield 120
    x = x + (dot(w.downT[...], sc.act[...]) + wide(w.vec[4]))
    slot = m % 2
    none = jnp.zeros((CA - C, T), F32)
    r.stage[slot, i, :, 0:CA] = jnp.concatenate([x * keep, none], axis=0).T.astype(BF)
    yield 150
    yield from feed_forward_back(sc, w, st, dd, z, scale)
    z, scale = ln_stats(sc.xT[...])
    yield from backward_attention(sc, w, st, z, scale, True)
    r.stage[slot, i, :, CA:] = jnp.concatenate([st.d, none], axis=0).T.astype(BF)
    yield 100


def second_kernel(groups_a, steps, lag, r):
    windows = by_window(r, dict(**FWD, **KEPT, **BWD))
    m = pl.program_id(0)

    @pl.when(m == 0)
    def _():
        greet([neighbour(octant, -1, groups_a) for octant in range(1, 8)])
        init_forward(r, windows)
        init_backward(r, windows)

    @pl.when(m >= 2)
    def _():
        wait_sent(r, m - 2, 1, groups_a)

    weave(
        [second_layer(r, sc, m, i, groups_a) for i, sc in enumerate(windows)], lag
    )
    send_blocks(r, m, 1, groups_a)

    @pl.when(m == steps - 1)
    def _():
        finish_blocks(r, steps, 1, groups_a)
        write_grads(r, r.grads)


def first_backward(r, sc, i):
    w, st = r, SimpleNamespace()
    came = dot(r.eye[...], r.came[i], NT).astype(BF)
    yield 200
    came = dot(came, r.perm[...])
    r.output[i, 0] = came[0:C, 0:WS].astype(BF)
    st.d = came[CA : CA + C]
    dd = st.d.astype(BF)
    z, scale = ln_stats(sc.x1[...])
    yield 200
    for c in range(3):
        rows = slice(128 * c, 128 * c + 128)
        sc.dh[rows, :] = (dot(w.down[rows], dd) * sc.gp[rows, :].astype(F32)).astype(BF)
        yield 50
    yield from feed_forward_back(sc, w, st, dd, z, scale)
    z, scale = ln_stats(sc.xT[...])
    yield from backward_attention(sc, w, st, z, scale, False)
    r.input_grad[i, 0] = st.d[:, 0:WS]
    yield 50


def first_backward_kernel(steps, lag, r):
    windows = by_window(r, dict(**KEPT, **BWD))
    m = pl.program_id(0)

    @pl.when(m == 0)
    def _():
        init_backward(r, windows)

    weave([first_backward(r, sc, i) for i, sc in enumerate(windows)], lag)

    @pl.when(m == steps - 1)
    def _():
        write_grads(r, r.grads)


def shard_rows(device, shard_len):
    return device * shard_len // C, -(-(device + 1) * shard_len // C)


def flat_offset(device, shard_len):
    return device * shard_len % C


def slab_rows(shard_len):
    return -(-((shard_len + C - 2) // C + 1) // 16) * 16


def own_place():
    win = lax.axis_index(WIN)
    return lax.axis_index(VOL), win // 2, win % 2


def all_peers(n_vol, n_plane):
    vol, plane, core = own_place()
    return (
        [((vol + j) % n_vol, plane * 2 + core) for j in range(1, n_vol)]
        + [(vol, (plane + j) % n_plane * 2 + core) for j in range(1, n_plane)]
        + [(vol, plane * 2 + 1 - core)]
    )


def transpose_with(matrix, extra):
    below = jnp.where(lax.broadcasted_iota(jnp.int32, (CA - C, C), 0) == 0, extra, 0.0)
    return jnp.concatenate([matrix, below], axis=0).T


def gather_kernel(n_vol, n_plane, shard_len, r):
    vol, plane, core = own_place()
    peers = all_peers(n_vol, n_plane)
    greet(peers)
    await_greetings(peers)
    buf = r.buf

    def copy(ref, n):
        return pltpu.make_async_remote_copy(
            src_ref=ref,
            dst_ref=ref,
            send_sem=r.sent.at[n],
            recv_sem=r.arrived.at[n],
            device_id=peers[n],
            device_id_type=MESH,
        )

    buf[core, plane, vol] = r.shard[...]
    stages = [
        [copy(buf.at[core, plane, vol], n) for n in range(n_vol - 1)],
        [copy(buf.at[core, plane], n_vol - 1 + n) for n in range(n_plane - 1)],
        [copy(buf.at[core], n_vol + n_plane - 2)],
    ]
    for copies in stages:
        for c in copies:
            c.start()
        for c in copies:
            c.wait()
    flat = r.flat
    flat[...] = jnp.zeros(flat.shape, F32)
    for v in range(n_vol):
        for p in range(n_plane):
            for c in range(2):
                start, stop = shard_rows((v * n_plane + p) * 2 + c, shard_len)
                flat[start:stop, :] += buf[c, p, v, 0 : stop - start].astype(F32)
    for layer in range(2):
        at = layer * BLOCK_ROWS

        def rows(start, count=C, stride=1):
            return flat[pl.ds(at + start, count, stride), :]

        def vector(n):
            return rows(12 * C + n, 1)

        o = {n: getattr(r, n).at[layer] for n in WEIGHTS}
        o = SimpleNamespace(**o)
        none = jnp.zeros((1, C), F32)
        wq, wk, wv = (rows(n, C, 3) for n in range(3))
        o.q[...] = wq.astype(BF)
        o.kv96[...] = jnp.concatenate([wk, wv], axis=1).astype(BF)
        o.qkvT[0:C, :] = (transpose_with(wq, vector(2)) * 0.25).astype(BF)
        o.qkvT[C : 2 * C, :] = (transpose_with(wk, none) * 0.25).astype(BF)
        o.qkvT[2 * C :, :] = transpose_with(wv, vector(3)).astype(BF)
        row = lax.broadcasted_iota(jnp.int32, (CA - C, CA), 0)
        lane = lax.broadcasted_iota(jnp.int32, (CA - C, CA), 1)
        blank = jnp.zeros((C, CA - C), F32)
        bias_v = jnp.concatenate([vector(3), blank[0:1]], axis=1)
        ones = jnp.where((lane == C) | (lane == C + 1), 1.0, bias_v)
        o.kv[0:C, :] = jnp.concatenate([wk, blank, wv, blank], axis=1).astype(BF)
        o.kv[C:, 0:CA] = jnp.zeros((CA - C, CA), BF)
        o.kv[C:, CA:] = jnp.where(row == 0, ones, 0.0).astype(BF)
        proj = rows(3 * C)
        o.proj[...] = proj.astype(BF)
        o.projT[...] = transpose_with(proj, vector(4)).astype(BF)
        ups = [rows(4 * C + j, C, 4) for j in range(4)]
        o.up[...] = jnp.concatenate(ups, axis=1).astype(BF)
        for j in range(4):
            o.upT[C * j : C * j + C, :] = transpose_with(ups[j], vector(8 + j)).astype(BF)
        down = rows(8 * C, FF)
        o.down[...] = down.astype(BF)
        o.downT[...] = down.T.astype(BF)
        for n, source in enumerate((0, 1, 5, 6, 7)):
            o.vec[n] = jnp.broadcast_to(vector(source), (128, C)).T


def reduce_kernel(n_vol, n_plane, shard_len, r):
    vol, plane, core = own_place()
    peers = all_peers(n_vol, n_plane)
    greet(peers)
    await_greetings(peers)
    work = r.work
    half = 2 * n_vol * n_plane // 2
    for v in range(n_vol):
        for p in range(n_plane):
            for c in range(2):
                device = (v * n_plane + p) * 2 + c
                start, stop = shard_rows(device, shard_len)
                source = (r.first, r.second)[device // half]
                start, stop = (n - device // half * BLOCK_ROWS for n in (start, stop))
                work[c, p, v, 0 : stop - start] = source[start:stop, :]

    def copy(source, target, n):
        return pltpu.make_async_remote_copy(
            src_ref=source,
            dst_ref=target,
            send_sem=r.sent.at[n],
            recv_sem=r.arrived.at[n],
            device_id=peers[n],
            device_id_type=MESH,
        )

    def exchange(copies):
        for c in copies:
            c.start()
        for c in copies:
            c.wait()

    exchange([copy(work.at[1 - core], r.from_core, n_vol + n_plane - 2)])
    work[core] += r.from_core[...]
    exchange(
        [
            copy(work.at[core, (plane + j) % n_plane], r.from_plane.at[j - 1], n_vol - 2 + j)
            for j in range(1, n_plane)
        ]
    )
    total = work[core, plane]
    for j in range(n_plane - 1):
        total = total + r.from_plane[j]
    work[core, plane] = total
    exchange(
        [
            copy(work.at[core, plane, (vol + j) % n_vol], r.from_vol.at[j - 1], j - 1)
            for j in range(1, n_vol)
        ]
    )
    total = work[core, plane, vol]
    for j in range(n_vol - 1):
        total = total + r.from_vol[j]
    r.total[...] = total


def call(kernel, steps, ins, outs, scratch, semaphores=(), collective_id=None):
    def spec(shape, kind):
        if kind is SMEM:
            return pl.BlockSpec(memory_space=pltpu.SMEM)
        if kind is HBM:
            return pl.BlockSpec(memory_space=pl.ANY)
        zeros = (0,) * (len(shape) - 1)
        if kind is BY_STEP:
            return pl.BlockSpec((shape[0] // steps,) + tuple(shape[1:]), lambda m: (m,) + zeros)
        if kind in (0, 1):
            return pl.BlockSpec((pl.squeezed,) + tuple(shape[1:]), lambda m: (kind,) + zeros)
        return pl.BlockSpec(tuple(shape), lambda m: (0,) + zeros)

    semaphores = dict(semaphores)
    names = tuple(ins) + tuple(outs) + tuple(scratch) + tuple(semaphores)

    def body(*refs):
        kernel(SimpleNamespace(**dict(zip(names, refs))))

    results = pl.pallas_call(
        body,
        grid=(steps,),
        in_specs=[spec(a.shape, kind) for a, kind in ins.values()],
        out_specs=[spec(shape, kind) for shape, _, kind in outs.values()],
        out_shape=[jax.ShapeDtypeStruct(shape, dtype) for shape, dtype, _ in outs.values()],
        scratch_shapes=[pltpu.VMEM(shape, dtype) for shape, dtype in scratch.values()]
        + [pltpu.SemaphoreType.DMA(shape) for shape in semaphores.values()],
        compiler_params=pltpu.CompilerParams(
            vmem_limit_bytes=60 * 2**20,
            collective_id=collective_id,
            has_side_effects=collective_id is not None,
        ),
    )(*[a for a, _ in ins.values()])
    return SimpleNamespace(**dict(zip(outs, results)))


WEIGHTS = dict(
    qkvT=((3 * C, CA), BF),
    kv=((CA, 2 * CA), BF),
    projT=((C, CA), BF),
    proj=((C, C), BF),
    upT=((FF, CA), BF),
    up=((C, FF), BF),
    downT=((C, FF), BF),
    down=((FF, C), BF),
    q=((C, C), BF),
    kv96=((C, 2 * C), BF),
    vec=((5, C, 128), F32),
)


def on_device(
    tokens,
    cotangent,
    position_bias,
    window_volume,
    clip_extent,
    master,
    first_moment,
    second_moment,
):
    n_vol, n_win = lax.axis_size(VOL), lax.axis_size(WIN)
    groups_a, n_plane = n_win // 4, n_win // 2
    count = tokens.shape[0]
    steps = count // WINDOWS
    shard_len = master.shape[0]
    device = lax.axis_index((VOL, WIN))
    slab = slab_rows(shard_len)
    offset = flat_offset(device, shard_len)
    shard = lax.dynamic_update_slice(jnp.zeros((slab * C,), BF), master.astype(BF), (offset,))
    n_peers = n_vol + n_plane - 1
    weights = call(
        lambda r: gather_kernel(n_vol, n_plane, shard_len, r),
        1,
        dict(shard=(shard.reshape(slab, C), WHOLE)),
        {n: ((2,) + shape, dtype, WHOLE) for n, (shape, dtype) in WEIGHTS.items()},
        dict(
            buf=((2, n_plane, n_vol, slab, C), BF),
            flat=((2 * BLOCK_ROWS + 8, C), F32),
        ),
        dict(sent=(n_peers,), arrived=(n_peers,)),
        collective_id=0,
    )
    info = jnp.concatenate((window_volume[:, :, None], clip_extent), axis=2)[:, 0]

    def each(table):
        return {n: ((WINDOWS,) + shape, dtype) for n, (shape, dtype) in table.items()}

    def layer(which):
        return {n: (a, which) for n, a in vars(weights).items()}

    def table(which, order):
        return dict(order=(jnp.asarray(order, BF), WHOLE), table=(position_bias, which))

    perm = (jnp.asarray(PERM, BF), WHOLE)
    eye = (jnp.asarray(np.eye(CA), BF), WHOLE)
    stage = dict(stage=((2, WINDOWS, T, 2 * CA), BF))
    copies = dict(sent=(2, 8), arrived=(steps, 8))
    got = call(
        lambda r: first_forward_kernel(groups_a, steps, LAGS[0], r),
        steps,
        dict(
            tokens=(tokens.transpose(0, 1, 3, 2), BY_STEP),
            cotangent=(cotangent.transpose(0, 1, 3, 2), BY_STEP),
            info=(info, SMEM),
            perm=perm,
            places=(jnp.asarray(PLACES), WHOLE),
            **table(0, np.eye(T, WS)),
            **layer(0),
        ),
        dict(
            got=((count, T, 2 * CA), BF, HBM),
            **{n: ((count,) + shape, dtype, BY_STEP) for n, (shape, dtype) in KEPT.items()},
        ),
        dict(**BIAS, **stage, **each(FWD), **each(PADS)),
        copies,
        collective_id=1,
    )
    second = call(
        lambda r: second_kernel(groups_a, steps, LAGS[1], r),
        steps,
        dict(
            came=(got.got, BY_STEP),
            eye=eye,
            **table(1, ORDER),
            **layer(1),
        ),
        dict(
            got=((count, T, 2 * CA), BF, HBM),
            grads=((BLOCK_ROWS, C), F32, WHOLE),
        ),
        dict(**BIAS, **stage, **GRADS, **each(FWD), **each(KEPT), **each(BWD)),
        copies,
        collective_id=2,
    )
    first = call(
        lambda r: first_backward_kernel(steps, LAGS[2], r),
        steps,
        dict(
            came=(second.got, BY_STEP),
            perm=perm,
            eye=(jnp.asarray(np.eye(2 * CA), BF), WHOLE),
            **{n: (getattr(got, n), BY_STEP) for n in KEPT},
            **layer(0),
        ),
        dict(
            output=((count, 1, C, WS), BF, BY_STEP),
            input_grad=((count, 1, C, WS), F32, BY_STEP),
            grads=((BLOCK_ROWS, C), F32, WHOLE),
        ),
        dict(**GRADS, **each(BWD)),
    )
    reduced = call(
        lambda r: reduce_kernel(n_vol, n_plane, shard_len, r),
        1,
        dict(first=(first.grads, WHOLE), second=(second.grads, WHOLE)),
        dict(total=((slab, C), F32, WHOLE)),
        dict(
            work=((2, n_plane, n_vol, slab, C), F32),
            from_core=((n_plane, n_vol, slab, C), F32),
            from_plane=((n_plane - 1, n_vol, slab, C), F32),
            from_vol=((n_vol - 1, slab, C), F32),
        ),
        dict(sent=(n_peers,), arrived=(n_peers,)),
        collective_id=3,
    )
    shard_grad = lax.dynamic_slice(reduced.total.reshape(-1), (offset,), (shard_len,))
    position = (device * shard_len + jnp.arange(shard_len, dtype=jnp.int32)) % (BLOCK_ROWS * C)
    is_vector = position >= 12 * C * C
    step_rate = jnp.where(is_vector, RATE_VECTOR, RATE_MATRIX)
    weight_decay = jnp.where(is_vector, 0.0, DECAY_MATRIX)
    moment_one = BETA_FIRST * first_moment + (1.0 - BETA_FIRST) * shard_grad
    moment_two = BETA_SECOND * second_moment + (1.0 - BETA_SECOND) * shard_grad * shard_grad
    corrected_one = moment_one / (1.0 - BETA_FIRST**STEP)
    corrected_two = moment_two / (1.0 - BETA_SECOND**STEP)
    normalized = corrected_one / (jnp.sqrt(corrected_two) + ADAM_EPS)
    new_master = master - step_rate * (normalized + weight_decay * master)
    return (
        first.output.transpose(0, 1, 3, 2),
        first.input_grad.transpose(0, 1, 3, 2),
        new_master,
        moment_one,
        moment_two,
        new_master.astype(BF),
    )


def solution(mesh):
    placed = (
        P(None, (VOL, WIN), None, None),
        P(None, (VOL, WIN), None, None),
        P(),
        P(None, (VOL, WIN)),
        P(None, (VOL, WIN), None),
        P((VOL, WIN)),
        P((VOL, WIN)),
        P((VOL, WIN)),
    )
    return jax.shard_map(
        on_device,
        mesh=mesh,
        in_specs=placed,
        out_specs=(
            P(None, (VOL, WIN), None, None),
            P(None, (VOL, WIN), None, None),
            P((VOL, WIN)),
            P((VOL, WIN)),
            P((VOL, WIN)),
            P((VOL, WIN)),
        ),
        check_vma=False,
    )
```

```python
from types import SimpleNamespace

import jax
import jax.numpy as jnp
import numpy as np
from jax import lax
from jax.experimental import pallas as pl
from jax.experimental.pallas import tpu as pltpu
from jax.sharding import PartitionSpec as P

C = 96
HEADS = 6
HEAD_DIM = 16
FF = 384
SIDE = 7
SHIFT = 3
WS = 343
STEP = 6
T = 384
WINDOWS = 2
TABLE_SLOTS = 4
CA = 128
BLOCK_ROWS = 1164

NORM_EPS = 1e-05
MASK_FILL = -1000000000.0
BETA_FIRST = 0.5
BETA_SECOND = 0.5
ADAM_EPS = 1e-08
RATE_MATRIX = 0.1
RATE_VECTOR = 0.4
DECAY_MATRIX = 0.05

BF = jnp.bfloat16
F32 = jnp.float32
NN = (((1,), (0,)), ((), ()))
NT = (((1,), (1,)), ((), ()))
BY_STEP, WHOLE, SMEM, HBM = range(4)
MESH = pl.DeviceIdType.MESH
VOL, WIN = "vol", "win"
KEPT_NAMES = ("a0", "a1"), ("b0", "b1")


def octant_bits(octant):
    return (octant >> 2 & 1, octant >> 1 & 1, octant & 1)


OCT_SIZE = []
OCT_LEN = []
OCT_OFF = []
for _octant in range(8):
    _size = 1
    for _bit in octant_bits(_octant):
        _size *= SHIFT if _bit else SIDE - SHIFT
    OCT_OFF.append(sum(OCT_LEN))
    OCT_SIZE.append(_size)
    OCT_LEN.append(-(-_size // 16) * 16)


def slot_tables():
    perm = np.zeros((T, T), np.float32)
    order = np.zeros((T, WS), np.float32)
    places = np.full((8, T), 99, np.int32)
    for octant in range(8):
        bits = octant_bits(octant)
        lens = [SHIFT if bit else SIDE - SHIFT for bit in bits]
        for i in range(lens[0]):
            for j in range(lens[1]):
                for k in range(lens[2]):
                    source = [v if bit else v + SHIFT for v, bit in zip((i, j, k), bits)]
                    own = [v + bit * (SIDE - SHIFT) for v, bit in zip((i, j, k), bits)]
                    q = OCT_OFF[octant] + (i * lens[1] + j) * lens[2] + k
                    t = (source[0] * SIDE + source[1]) * SIDE + source[2]
                    perm[q, t] = 1
                    order[q, (own[0] * SIDE + own[1]) * SIDE + own[2]] = 1
                    places[:3, t] = source
    return perm, order, places


PERM, ORDER, PLACES = slot_tables()


def dot(a, b, dims=NN):
    return lax.dot_general(a, b, dims, preferred_element_type=F32)


def wide(column):
    return jnp.concatenate([column] * (T // 128), axis=1)


def ln_stats(x):
    centred = x - jnp.mean(x, axis=0, keepdims=True)
    scale = lax.rsqrt(jnp.mean(centred * centred, axis=0, keepdims=True) + NORM_EPS)
    return centred * scale, scale


def norm_back(e, z, scale, gain):
    eg = e * gain
    return scale * (
        eg - jnp.mean(eg, axis=0, keepdims=True) - z * jnp.mean(eg * z, axis=0, keepdims=True)
    )


def gelu_pair(h):
    base = 1.0 + (0.3275911 * 0.7071067811865476) * jnp.abs(h)
    t = pl.reciprocal(base, approx=True)
    t = t * (2.0 - base * t)
    poly = t * (
        0.5 * 0.254829592
        + t
        * (
            0.5 * -0.284496736
            + t * (0.5 * 1.421413741 + t * (0.5 * -1.453152027 + t * (0.5 * 1.061405429)))
        )
    )
    bell = jnp.exp(-0.5 * (h * h))
    tail = poly * bell
    phi = jnp.where(h < 0.0, tail, 1.0 - tail)
    return h * phi, phi + h * bell * 0.3989422804014327


def ones_row(shape, row=0):
    return jnp.where(lax.broadcasted_iota(jnp.int32, shape, 0) == row, 1.0, 0.0)


def weave(tasks, lag):
    clocks = [lag * n for n in range(len(tasks))]
    while tasks:
        n = clocks.index(min(clocks))
        cost = next(tasks[n], None)
        if cost is None:
            tasks, clocks = (x[:n] + x[n + 1 :] for x in (tasks, clocks))
        else:
            clocks[n] += cost


def clear_scratch(r):
    zeros = jnp.zeros((CA, HEADS * T), BF)
    for i in range(WINDOWS):
        r.qb[i] = zeros
        r.dab[i] = zeros
        r.rb[i] = jnp.zeros((2, 2 * C, 2 * T), BF)
        r.pad[i] = jnp.zeros((C, T), BF)
        r.cot[i] = jnp.zeros((C, T), BF)
        for h in range(HEADS):
            r.vt[i, h, 16:32, :] = ones_row((16, T)).astype(BF)
    for name, (shape, dtype) in GRADS.items():
        getattr(r, name)[...] = jnp.zeros((2,) + shape, dtype)


def table_copy(r, n):
    slot = n % TABLE_SLOTS
    return pltpu.make_async_copy(
        r.table.at[n // HEADS, n % HEADS], r.page.at[slot], r.turned.at[slot]
    )


def turn_tables(r, layer):
    for n in range(HEADS * layer, HEADS * layer + HEADS):
        table_copy(r, n).wait()
        half = dot(r.order[layer], r.page[n % TABLE_SLOTS], NT).astype(BF)
        if n + TABLE_SLOTS < 2 * HEADS:
            table_copy(r, n + TABLE_SLOTS).start()
        r.bias[layer, n % HEADS] = dot(half, r.order[layer], NT)


def set_queries(sc, queries):
    for h in range(HEADS):
        sc.qb[16 * h : 16 * h + 16, T * h : T * h + T] = queries[16 * h : 16 * h + 16, :]


def forward_attention(sc, w, st, code_row):
    z, _ = ln_stats(st.x)
    sc.n1aug[C:CA, :] = ones_row((CA - C, T)).astype(BF)
    sc.attaug[C:CA, :] = ones_row((CA - C, T)).astype(BF)
    sc.n1aug[0:C, :] = (z * wide(w.vec[0]) + wide(w.vec[1])).astype(BF)
    yield 150
    kv = dot(sc.n1aug[...].T, w.kv[...]).astype(BF)
    sc.kn[...] = kv[:, 0:CA]
    sc.vn[...] = kv[:, CA:]
    yield 200
    qkv = dot(w.qkvT[...], sc.n1aug[...])
    queries = qkv[0:C].astype(BF)
    set_queries(sc, queries)
    sc.qT[...] = queries
    sc.kT[...] = qkv[C : 2 * C].astype(BF)
    values = qkv[2 * C :].astype(BF)
    for h in range(HEADS):
        sc.vt[h, 0:16, :] = values[16 * h : 16 * h + 16, :]
    yield 150
    eye = lax.broadcasted_iota(jnp.int32, (128, 128), 0) == lax.broadcasted_iota(
        jnp.int32, (128, 128), 1
    )
    tops = [None] * HEADS

    def scores(h, c):
        rows = slice(128 * c, 128 * c + 128)
        x_all = dot(sc.kn[rows], sc.qb[:, T * h : T * h + T])
        codes = sc.codes[rows]
        parts = []
        for j in range(3):
            lanes = slice(128 * j, 128 * j + 128)
            allowed = codes == code_row[:, lanes]
            if j == c:
                allowed = allowed | eye
            part = jnp.where(allowed, x_all[:, lanes] + sc.bias[h, rows, lanes], MASK_FILL)
            sc.s[h % 2, rows, lanes] = part
            parts.append(jnp.max(part.reshape(16, 8, 128), axis=0))
        top = jnp.concatenate(parts, axis=1)
        tops[h] = top if tops[h] is None else jnp.maximum(tops[h], top)

    def raise_(h, c):
        rows = slice(128 * c, 128 * c + 128)
        sc.e[rows, T * h : T * h + T] = jnp.exp(sc.s[h % 2, rows] - tops[h]).astype(BF)

    def attend(h):
        out = dot(sc.vt[h], sc.e[:, T * h : T * h + T])
        inverse = 1.0 / out[16:17]
        part = out[0:16] * inverse
        sc.att[16 * h : 16 * h + 16, :] = part
        sc.inv[h : h + 1, :] = inverse
        sc.attaug[16 * h : 16 * h + 16, :] = part.astype(BF)

    for h in range(HEADS + 2):
        for c in range(3):
            if h < HEADS:
                scores(h, c)
            if 0 <= h - 1 < HEADS:
                raise_(h - 1, c)
            if c == 0 and 0 <= h - 2 < HEADS:
                attend(h - 2)
            yield 70
        if h < HEADS:
            tops[h] = jnp.max(tops[h], axis=0, keepdims=True)
    st.branch = dot(w.projT[...], sc.attaug[...])
    yield 100


def backward_attention(sc, w, st, z, scale, shifted):
    d_mid = st.d
    db = d_mid.astype(BF)
    d_att = dot(w.proj[...], db).astype(BF).astype(F32)
    sc.gproj[...] += dot(sc.attaug[...], db, NT)
    yield 150
    row = lax.broadcasted_iota(jnp.int32, (16, T), 0)
    for h in range(HEADS):
        part = (d_att[16 * h : 16 * h + 16] * sc.inv[h : h + 1, :]).astype(BF)
        cols = slice(T * h, T * h + T)
        sc.dab[16 * h : 16 * h + 16, cols] = part
        inner = -jnp.sum(
            part.astype(F32) * sc.att[16 * h : 16 * h + 16, :], axis=0, keepdims=True
        )
        high = inner.astype(BF).astype(F32)
        low = inner - high
        sc.dab[C : C + 16, cols] = jnp.where(
            row == 0, high, jnp.where(row == 1, low, 0.0)
        ).astype(BF)
    yield 100
    total = None
    none = jnp.zeros((16, T), BF)

    def soft(h):
        cols = slice(T * h, T * h + T)
        pull = dot(sc.vn[...], sc.dab[:, cols])
        sc.ds[h % 2] = (pull * sc.e[:, cols].astype(F32)).astype(BF)

    def place_rows(h):
        rb = sc.rb.at[h % 2]
        last = (h - 2) % HEADS
        rb[16 * last : 16 * last + 16, T:] = none
        rb[C + 16 * last : C + 16 * last + 16, 0:T] = none
        rb[16 * h : 16 * h + 16, T:] = sc.qT[16 * h : 16 * h + 16, :]
        rb[C + 16 * h : C + 16 * h + 16, 0:T] = sc.dab[
            16 * h : 16 * h + 16, T * h : T * h + T
        ]

    def to_queries(h):
        sc.dq[16 * h : 16 * h + 16, :] = dot(sc.kT[16 * h : 16 * h + 16, :], sc.ds[h % 2]).astype(BF)

    for h in range(HEADS + 1):
        if h < HEADS:
            place_rows(h)
            soft(h)
            yield 120
        if h > 0:
            to_queries(h - 1)
            yield 60
            both = jnp.concatenate([sc.e[:, T * (h - 1) : T * h], sc.ds[(h - 1) % 2]], axis=1)
            term = dot(both, sc.rb[(h - 1) % 2], NT)
            total = term if total is None else total + term
            yield 180
    dkv = total.astype(BF)
    dq = sc.dq[...]
    dn = dot(w.q[...], dq) + dot(w.kv96[...], dkv, NT)
    yield 120
    sc.gkv[...] += dot(sc.n1aug[...], dkv)
    sc.gq[...] += dot(dq, sc.n1aug[...], NT)
    yield 150
    if shifted:
        dn = dn.astype(BF).astype(F32)
    sc.gvec[0] += dn * z
    sc.gvec[1] += dn
    st.d = d_mid + norm_back(dn, z, scale, wide(w.vec[0]))
    yield 150


def feed_forward_back(sc, w, st, dd, z, scale):
    dn = dot(w.up[...], sc.dh[...])
    yield 120
    sc.gdown[...] += dot(sc.act[...], dd, NT)
    yield 120
    sc.gup[...] += dot(sc.dh[...], sc.n2aug[...], NT)
    yield 120
    sc.gvec[4] += dd.astype(F32)
    sc.gvec[2] += dn * z
    sc.gvec[3] += dn
    st.d = st.d + norm_back(dn, z, scale, wide(w.vec[2]))
    yield 150


def write_grads(sc, out):
    gq = sc.gq[...].T
    gkv = sc.gkv[...]
    gup = sc.gup[...].T
    out[pl.ds(0, C, 3), :] = gq[0:C]
    out[pl.ds(1, C, 3), :] = gkv[0:C, 0:C]
    out[pl.ds(2, C, 3), :] = gkv[0:C, C : 2 * C]
    out[3 * C : 4 * C, :] = sc.gproj[0:C, :]
    for j in range(4):
        out[pl.ds(4 * C + j, C, 4), :] = gup[0:C, C * j : C * j + C]
    out[8 * C : 12 * C, :] = sc.gdown[...]
    sums = [jnp.sum(sc.gvec[n].T, axis=0, keepdims=True) for n in range(5)]
    rows = [
        sums[0],
        sums[1],
        gq[C : C + 1],
        gkv[C : C + 1, C : 2 * C],
        sc.gproj[C : C + 1, :],
        sums[2],
        sums[3],
        sums[4],
    ] + [gup[C : C + 1, C * j : C * j + C] for j in range(4)]
    for n, value in enumerate(rows):
        out[12 * C + n : 12 * C + n + 1, :] = value


FWD = dict(
    qb=((CA, HEADS * T), BF),
    vt=((HEADS, 32, T), BF),
    kn=((T, CA), BF),
    codes=((T, 128), F32),
    s=((2, T, T), F32),
)
BIAS = dict(bias=((HEADS, T, T), F32))
KEPT = dict(
    qT=((C, T), BF),
    kT=((C, T), BF),
    vn=((T, CA), BF),
    e=((T, HEADS * T), BF),
    att=((C, T), F32),
    inv=((8, T), F32),
    attaug=((CA, T), BF),
    n1aug=((CA, T), BF),
    n2aug=((CA, T), BF),
    act=((FF, T), BF),
    gp=((FF, T), BF),
    xT=((C, T), F32),
    x1=((C, T), F32),
)
GRADS = dict(
    gq=((C, CA), F32),
    gkv=((CA, 2 * C), F32),
    gproj=((CA, C), F32),
    gup=((FF, CA), F32),
    gdown=((FF, C), F32),
    gvec=((5, C, T), F32),
)
BWD = dict(
    dab=((CA, HEADS * T), BF),
    rb=((2, 2 * C, 2 * T), BF),
    ds=((2, T, T), BF),
    dq=((C, T), BF),
    dh=((FF, T), BF),
)


PADS = dict(pad=((C, T), BF), cot=((C, T), BF))
WEIGHTS = dict(
    qkvT=((3 * C, CA), BF),
    kv=((CA, 2 * CA), BF),
    projT=((C, CA), BF),
    proj=((C, C), BF),
    upT=((FF, CA), BF),
    up=((C, FF), BF),
    downT=((C, FF), BF),
    down=((FF, C), BF),
    q=((C, C), BF),
    kv96=((C, 2 * C), BF),
    vec=((5, C, 128), F32),
)


def of_layer(r, layer, slot):
    shared = {n: getattr(r, n).at[layer] for n in (*WEIGHTS, *GRADS, *BIAS)}
    return [
        SimpleNamespace(
            **shared,
            **{n: getattr(r, n).at[i] for n in (*FWD, *BWD, *PADS)},
            **{n: getattr(r, KEPT_NAMES[layer][i] + n).at[slot] for n in KEPT},
        )
        for i in range(WINDOWS)
    ]


def second_norm(sc, w, x):
    z, scale = ln_stats(x)
    sc.n2aug[C:CA, :] = ones_row((CA - C, T)).astype(BF)
    sc.n2aug[0:C, :] = (z * wide(w.vec[2]) + wide(w.vec[3])).astype(BF)
    return z, scale


def grid_place(groups_a):
    win = lax.axis_index(WIN)
    return (win // 4, win // 2 % 2, win % 2), (groups_a, 2, 2)


def neighbour(octant, sign, groups_a):
    place, sizes = grid_place(groups_a)
    a, b, c = (
        (p + sign * bit + n) % n for p, bit, n in zip(place, octant_bits(octant), sizes)
    )
    return lax.axis_index(VOL), (a * 2 + b) * 2 + c


def greet(peers):
    barrier = pltpu.get_barrier_semaphore()
    for peer in peers:
        pl.semaphore_signal(barrier, inc=1, device_id=peer, device_id_type=MESH)


def await_greetings(peers):
    pl.semaphore_wait(pltpu.get_barrier_semaphore(), len(peers))


def block_copy(way, m, octant, groups_a):
    rows = pl.ds(OCT_OFF[octant], OCT_LEN[octant])
    slot = m % 2
    source = way.stage.at[slot, :, rows]
    target = way.got.at[pl.ds(m * WINDOWS, WINDOWS), rows]
    if octant == 0:
        return pltpu.make_async_copy(source, target, way.arrived.at[m, 0])
    return pltpu.make_async_remote_copy(
        src_ref=source,
        dst_ref=target,
        send_sem=way.sent.at[slot, octant],
        recv_sem=way.arrived.at[m, octant],
        device_id=neighbour(octant, way.sign, groups_a),
        device_id_type=MESH,
    )


def send_blocks(way, m, groups_a):
    for octant in range(8):
        block_copy(way, m, octant, groups_a).start()


def wait_sent(way, m, groups_a):
    for octant in range(1, 8):
        block_copy(way, m, octant, groups_a).wait_send()


def wait_arrived(way, m, groups_a):
    block_copy(way, m, 0, groups_a).wait()
    for octant in range(1, 8):
        block_copy(way, m, octant, groups_a).wait_recv()


def first_forward(r, sc, m, i):
    w, st = sc, SimpleNamespace()
    stage = r.x_stage.at[m % 2, i]
    sc.pad[:, 0:WS] = r.tokens[i, 0]
    st.x = sc.pad[...].astype(F32)
    sc.xT[...] = st.x
    places = r.places
    valid = (
        (places[0:1, :] < r.info[m * WINDOWS + i, 1])
        & (places[1:2, :] < r.info[m * WINDOWS + i, 2])
        & (places[2:3, :] < r.info[m * WINDOWS + i, 3])
    )
    valid = jnp.where(valid, 1.0, 0.0)
    sc.codes[...] = jnp.broadcast_to(valid - 1.0, (128, T)).T
    yield 100
    yield from forward_attention(sc, w, st, jnp.zeros((1, T), F32))
    sc.cot[:, 0:WS] = r.cotangent[i, 0]
    stage[:, CA:] = jnp.concatenate(
        [dot(r.perm[...], sc.cot[...], NT), jnp.zeros((T, CA - C), F32)], axis=1
    ).astype(BF)
    yield 100
    x = st.x + st.branch
    sc.x1[...] = x
    second_norm(sc, w, x)
    yield 150
    for c in range(6):
        rows = slice(64 * c, 64 * c + 64)
        active, slope = gelu_pair(dot(w.upT[rows], sc.n2aug[...]))
        sc.act[rows, :] = active.astype(BF)
        sc.gp[rows, :] = slope.astype(BF)
        yield 100
    x = x + (dot(w.downT[...], sc.act[...]) + wide(w.vec[4]))
    yield 100
    row = lax.broadcasted_iota(jnp.int32, (CA - C, T), 0)
    label = r.info[m * WINDOWS + i, 0].astype(F32)
    extra = jnp.where(row == 0, label, jnp.where(row == 1, valid, 0.0))
    x = jnp.concatenate([x, extra], axis=0).astype(BF)
    stage[:, 0:CA] = dot(r.perm[...], x, NT).astype(BF)
    yield 100


def second_layer(r, sc, m, i, groups_a):
    w, st = sc, SimpleNamespace()
    stage = r.d_stage.at[m % 2, i]
    n = m * WINDOWS + i
    came = r.x_got[n, :, 0:CA]
    x = dot(r.eye[0:CA, 0:CA], came, NT)
    place, sizes = grid_place(groups_a)
    code_row = []
    for octant in range(8):
        rows = slice(OCT_OFF[octant], OCT_OFF[octant] + OCT_LEN[octant])
        wraps = [
            bit * jnp.where(p == n_ - 1, 1, 0)
            for p, bit, n_ in zip(place, octant_bits(octant), sizes)
        ]
        wrap = (wraps[0] * 4 + wraps[1] * 2 + wraps[2]).astype(F32)
        columns = came[rows].astype(F32)
        code = jnp.where(columns[:, C + 1 : C + 2] > 0.0, columns[:, C : C + 1] * 8.0 + wrap, -1.0)
        sc.codes[rows, :] = jnp.broadcast_to(code, (OCT_LEN[octant], 128))
        code_row.append(jnp.full((1, OCT_LEN[octant]), wrap))
    code_row = jnp.concatenate(code_row, axis=1) + 8.0 * x[C : C + 1]
    keep = x[C + 1 : C + 2]
    x = x[0:C]
    sc.xT[...] = x
    st.x = x
    yield 150
    yield from forward_attention(sc, w, st, code_row)
    st.d = dot(r.eye[0:C, 0:CA], r.x_got[n, :, CA:], NT) * keep
    dd = st.d.astype(BF)
    x = sc.xT[...] + st.branch.astype(BF).astype(F32)
    z, scale = second_norm(sc, w, x)
    yield 200
    for c in range(6):
        rows = slice(64 * c, 64 * c + 64)
        active, slope = gelu_pair(dot(w.upT[rows], sc.n2aug[...]))
        sc.act[rows, :] = active.astype(BF)
        sc.dh[rows, :] = (dot(w.down[rows], dd) * slope).astype(BF)
        yield 120
    x = x + (dot(w.downT[...], sc.act[...]) + wide(w.vec[4]))
    none = jnp.zeros((CA - C, T), F32)
    stage[:, 0:CA] = jnp.concatenate([x * keep, none], axis=0).T.astype(BF)
    yield 150
    yield from feed_forward_back(sc, w, st, dd, z, scale)
    z, scale = ln_stats(sc.xT[...])
    yield from backward_attention(sc, w, st, z, scale, True)
    stage[:, CA:] = jnp.concatenate([st.d, none], axis=0).T.astype(BF)
    yield 100


def first_backward(r, sc, m, i):
    w, st = sc, SimpleNamespace()
    came = dot(r.eye[...], r.d_got[m * WINDOWS + i], NT).astype(BF)
    yield 200
    came = dot(came, r.perm[...])
    r.output[i, 0] = came[0:C, 0:WS].astype(BF)
    st.d = came[CA : CA + C]
    dd = st.d.astype(BF)
    z, scale = ln_stats(sc.x1[...])
    yield 200
    for c in range(3):
        rows = slice(128 * c, 128 * c + 128)
        sc.dh[rows, :] = (dot(w.down[rows], dd) * sc.gp[rows, :].astype(F32)).astype(BF)
        yield 50
    yield from feed_forward_back(sc, w, st, dd, z, scale)
    z, scale = ln_stats(sc.xT[...])
    yield from backward_attention(sc, w, st, z, scale, False)
    r.input_grad[i, 0] = st.d[:, 0:WS]
    yield 50


def layers_kernel(n_vol, n_plane, shard_len, steps, r):
    groups_a = n_plane // 2
    s = pl.program_id(0)
    forth = SimpleNamespace(
        stage=r.x_stage, got=r.x_got, sent=r.x_sent, arrived=r.x_arrived, sign=-1
    )
    back = SimpleNamespace(
        stage=r.d_stage, got=r.d_got, sent=r.d_sent, arrived=r.d_arrived, sign=1
    )

    @pl.when(s == 0)
    def _():
        far = all_peers(n_vol, n_plane)
        peers = far + [
            neighbour(octant, sign, groups_a) for sign in (1, -1) for octant in range(1, 8)
        ]
        greet(peers)
        for n in range(TABLE_SLOTS):
            table_copy(r, n).start()
        vol, plane, core = own_place()
        r.buf[core, plane, vol] = r.shard[...]
        clear_scratch(r)
        await_greetings(peers)
        meanwhile = (lambda: None, lambda: turn_tables(r, 0), lambda: turn_tables(r, 1))
        for copies, work in zip(gather_stages(r, far, n_vol, n_plane), meanwhile):
            for c in copies:
                c.start()
            work()
            for c in copies:
                c.wait()
        prepare(r, n_vol, n_plane, shard_len)

    @pl.when(s < steps)
    def _():
        @pl.when(s >= 2)
        def _():
            wait_sent(forth, s - 2, groups_a)

        windows = of_layer(r, 0, s % 3)
        weave([first_forward(r, sc, s, i) for i, sc in enumerate(windows)], 0)
        send_blocks(forth, s, groups_a)

    @pl.when((s >= 1) & (s <= steps))
    def _():
        m = s - 1
        wait_arrived(forth, m, groups_a)

        @pl.when(m >= 2)
        def _():
            wait_sent(back, m - 2, groups_a)

        windows = of_layer(r, 1, 0)
        weave([second_layer(r, sc, m, i, groups_a) for i, sc in enumerate(windows)], 0)
        send_blocks(back, m, groups_a)

    @pl.when(s >= 2)
    def _():
        m = s - 2
        wait_arrived(back, m, groups_a)
        windows = of_layer(r, 0, m % 3)
        weave([first_backward(r, sc, m, i) for i, sc in enumerate(windows)], 0)

    @pl.when(s == steps + 1)
    def _():
        for m in range(max(steps - 2, 0), steps):
            wait_sent(forth, m, groups_a)
            wait_sent(back, m, groups_a)
        for layer in range(2):
            write_grads(of_layer(r, layer, 0)[0], r.grads.at[layer])


def shard_rows(device, shard_len):
    return device * shard_len // C, -(-(device + 1) * shard_len // C)


def flat_offset(device, shard_len):
    return device * shard_len % C


def slab_rows(shard_len):
    return -(-((shard_len + C - 2) // C + 1) // 16) * 16


def own_place():
    win = lax.axis_index(WIN)
    return lax.axis_index(VOL), win // 2, win % 2


def all_peers(n_vol, n_plane):
    vol, plane, core = own_place()
    return (
        [((vol + j) % n_vol, plane * 2 + core) for j in range(1, n_vol)]
        + [(vol, (plane + j) % n_plane * 2 + core) for j in range(1, n_plane)]
        + [(vol, plane * 2 + 1 - core)]
    )


def transpose_with(matrix, extra):
    below = jnp.where(lax.broadcasted_iota(jnp.int32, (CA - C, C), 0) == 0, extra, 0.0)
    return jnp.concatenate([matrix, below], axis=0).T


def gather_stages(r, peers, n_vol, n_plane):
    vol, plane, core = own_place()

    def copy(ref, n):
        return pltpu.make_async_remote_copy(
            src_ref=ref,
            dst_ref=ref,
            send_sem=r.g_sent.at[n],
            recv_sem=r.g_arrived.at[n],
            device_id=peers[n],
            device_id_type=MESH,
        )

    return (
        [copy(r.buf.at[core, plane, vol], n) for n in range(n_vol - 1)],
        [copy(r.buf.at[core, plane], n_vol - 1 + n) for n in range(n_plane - 1)],
        [copy(r.buf.at[core], n_vol + n_plane - 2)],
    )


def prepare(r, n_vol, n_plane, shard_len):
    buf = r.buf
    flat = r.grads
    flat[...] = jnp.zeros(flat.shape, F32)
    half = n_vol * n_plane
    for v in range(n_vol):
        for p in range(n_plane):
            for c in range(2):
                device = (v * n_plane + p) * 2 + c
                start, stop = shard_rows(device % half, shard_len)
                flat[device // half, start:stop, :] += buf[c, p, v, 0 : stop - start].astype(F32)
    for layer in range(2):

        def rows(start, count=C, stride=1):
            return flat[layer, pl.ds(start, count, stride), :]

        def vector(n):
            return rows(12 * C + n, 1)

        o = SimpleNamespace(**{n: getattr(r, n).at[layer] for n in WEIGHTS})
        none = jnp.zeros((1, C), F32)
        wq, wk, wv = (rows(n, C, 3) for n in range(3))
        o.q[...] = wq.astype(BF)
        o.kv96[...] = jnp.concatenate([wk, wv], axis=1).astype(BF)
        o.qkvT[0:C, :] = (transpose_with(wq, vector(2)) * 0.25).astype(BF)
        o.qkvT[C : 2 * C, :] = (transpose_with(wk, none) * 0.25).astype(BF)
        o.qkvT[2 * C :, :] = transpose_with(wv, vector(3)).astype(BF)
        row = lax.broadcasted_iota(jnp.int32, (CA - C, CA), 0)
        lane = lax.broadcasted_iota(jnp.int32, (CA - C, CA), 1)
        blank = jnp.zeros((C, CA - C), F32)
        bias_v = jnp.concatenate([vector(3), blank[0:1]], axis=1)
        ones = jnp.where((lane == C) | (lane == C + 1), 1.0, bias_v)
        o.kv[0:C, :] = jnp.concatenate([wk, blank, wv, blank], axis=1).astype(BF)
        o.kv[C:, 0:CA] = jnp.zeros((CA - C, CA), BF)
        o.kv[C:, CA:] = jnp.where(row == 0, ones, 0.0).astype(BF)
        proj = rows(3 * C)
        o.proj[...] = proj.astype(BF)
        o.projT[...] = transpose_with(proj, vector(4)).astype(BF)
        ups = [rows(4 * C + j, C, 4) for j in range(4)]
        o.up[...] = jnp.concatenate(ups, axis=1).astype(BF)
        for j in range(4):
            o.upT[C * j : C * j + C, :] = transpose_with(ups[j], vector(8 + j)).astype(BF)
        down = rows(8 * C, FF)
        o.down[...] = down.astype(BF)
        o.downT[...] = down.T.astype(BF)
        for n, source in enumerate((0, 1, 5, 6, 7)):
            o.vec[n] = jnp.broadcast_to(vector(source), (128, C)).T


def reduce_kernel(n_vol, n_plane, shard_len, r):
    vol, plane, core = own_place()
    peers = all_peers(n_vol, n_plane)
    greet(peers)
    await_greetings(peers)
    work = r.work
    half = n_vol * n_plane
    for v in range(n_vol):
        for p in range(n_plane):
            for c in range(2):
                device = (v * n_plane + p) * 2 + c
                start, stop = shard_rows(device % half, shard_len)
                source = r.grads.at[device // half]
                work[c, p, v, 0 : stop - start] = source[start:stop, :]

    def copy(source, target, n):
        return pltpu.make_async_remote_copy(
            src_ref=source,
            dst_ref=target,
            send_sem=r.sent.at[n],
            recv_sem=r.arrived.at[n],
            device_id=peers[n],
            device_id_type=MESH,
        )

    def exchange(copies):
        for c in copies:
            c.start()
        for c in copies:
            c.wait()

    exchange([copy(work.at[1 - core], r.from_core, n_vol + n_plane - 2)])
    work[core] += r.from_core[...]
    exchange(
        [
            copy(work.at[core, (plane + j) % n_plane], r.from_plane.at[j - 1], n_vol - 2 + j)
            for j in range(1, n_plane)
        ]
    )
    total = work[core, plane]
    for j in range(n_plane - 1):
        total = total + r.from_plane[j]
    work[core, plane] = total
    exchange(
        [
            copy(work.at[core, plane, (vol + j) % n_vol], r.from_vol.at[j - 1], j - 1)
            for j in range(1, n_vol)
        ]
    )
    total = work[core, plane, vol]
    for j in range(n_vol - 1):
        total = total + r.from_vol[j]
    r.total[...] = total


def call(kernel, steps, ins, outs, scratch, semaphores=(), collective_id=None, lag=0):
    def spec(shape, kind, late):
        if kind in (SMEM, HBM):
            return pl.BlockSpec(memory_space=pltpu.SMEM if kind is SMEM else pl.ANY)
        zeros = (0,) * (len(shape) - 1)
        if kind is BY_STEP:

            def index(s):
                return (jnp.clip(s - late, 0, steps - 1),) + zeros

            return pl.BlockSpec((shape[0] // steps,) + tuple(shape[1:]), index)
        return pl.BlockSpec(
            tuple(shape), lambda s: (0,) + zeros, pipeline_mode=None if late else pl.Buffered(1)
        )

    semaphores = dict(semaphores)
    names = tuple(ins) + tuple(outs) + tuple(scratch) + tuple(semaphores)

    def body(*refs):
        kernel(SimpleNamespace(**dict(zip(names, refs))))

    results = pl.pallas_call(
        body,
        grid=(steps + lag,),
        in_specs=[spec(a.shape, kind, 0) for a, kind in ins.values()],
        out_specs=[spec(shape, kind, lag) for shape, _, kind in outs.values()],
        out_shape=[jax.ShapeDtypeStruct(shape, dtype) for shape, dtype, _ in outs.values()],
        scratch_shapes=[pltpu.VMEM(shape, dtype) for shape, dtype in scratch.values()]
        + [pltpu.SemaphoreType.DMA(shape) for shape in semaphores.values()],
        compiler_params=pltpu.CompilerParams(
            vmem_limit_bytes=60 * 2**20,
            collective_id=collective_id,
            has_side_effects=collective_id is not None,
        ),
    )(*[a for a, _ in ins.values()])
    return SimpleNamespace(**dict(zip(outs, results)))


def on_device(
    tokens,
    cotangent,
    position_bias,
    window_volume,
    clip_extent,
    master,
    first_moment,
    second_moment,
):
    n_vol, n_win = lax.axis_size(VOL), lax.axis_size(WIN)
    n_plane = n_win // 2
    count = tokens.shape[0]
    steps = count // WINDOWS
    shard_len = master.shape[0]
    device = lax.axis_index((VOL, WIN))
    slab = slab_rows(shard_len)
    offset = flat_offset(device, shard_len)
    shard = lax.dynamic_update_slice(jnp.zeros((slab * C,), BF), master.astype(BF), (offset,))
    n_peers = n_vol + n_plane - 1
    info = jnp.concatenate((window_volume[:, :, None], clip_extent), axis=2)[:, 0]

    def each(table, *sizes):
        return {n: (sizes + shape, dtype) for n, (shape, dtype) in table.items()}

    def kept(layer, slots):
        shapes = dict(KEPT, gp=((16, T), BF)) if layer else KEPT
        return {name + n: v for name in KEPT_NAMES[layer] for n, v in each(shapes, slots).items()}

    stage, landing = ((2, WINDOWS, T, 2 * CA), BF), ((count, T, 2 * CA), BF)
    layers = call(
        lambda r: layers_kernel(n_vol, n_plane, shard_len, steps, r),
        steps,
        dict(
            tokens=(tokens.transpose(0, 1, 3, 2), BY_STEP),
            cotangent=(cotangent.transpose(0, 1, 3, 2), BY_STEP),
            info=(info, SMEM),
            perm=(jnp.asarray(PERM, BF), WHOLE),
            places=(jnp.asarray(PLACES), WHOLE),
            order=(jnp.asarray(np.stack([np.eye(T, WS), ORDER]), BF), WHOLE),
            table=(position_bias, HBM),
            shard=(shard.reshape(slab, C), WHOLE),
            eye=(jnp.asarray(np.eye(2 * CA), BF), WHOLE),
        ),
        dict(
            output=((count, 1, C, WS), BF, BY_STEP),
            input_grad=((count, 1, C, WS), F32, BY_STEP),
            grads=((2, BLOCK_ROWS, C), F32, WHOLE),
        ),
        dict(
            **each(FWD, WINDOWS),
            **each(BWD, WINDOWS),
            **each(PADS, WINDOWS),
            **each(GRADS, 2),
            **each(BIAS, 2),
            **kept(0, 3),
            **kept(1, 1),
            **each(WEIGHTS, 2),
            page=((TABLE_SLOTS, WS, WS), BF),
            buf=((2, n_plane, n_vol, slab, C), BF),
            x_stage=stage,
            d_stage=stage,
            x_got=landing,
            d_got=landing,
        ),
        dict(
            x_sent=(2, 8),
            x_arrived=(steps, 8),
            d_sent=(2, 8),
            d_arrived=(steps, 8),
            g_sent=(n_peers,),
            g_arrived=(n_peers,),
            turned=(TABLE_SLOTS,),
        ),
        collective_id=1,
        lag=2,
    )
    reduced = call(
        lambda r: reduce_kernel(n_vol, n_plane, shard_len, r),
        1,
        dict(grads=(layers.grads, WHOLE)),
        dict(total=((slab, C), F32, WHOLE)),
        dict(
            work=((2, n_plane, n_vol, slab, C), F32),
            from_core=((n_plane, n_vol, slab, C), F32),
            from_plane=((n_plane - 1, n_vol, slab, C), F32),
            from_vol=((n_vol - 1, slab, C), F32),
        ),
        dict(sent=(n_peers,), arrived=(n_peers,)),
        collective_id=2,
    )
    shard_grad = lax.dynamic_slice(reduced.total.reshape(-1), (offset,), (shard_len,))
    position = (device * shard_len + jnp.arange(shard_len, dtype=jnp.int32)) % (BLOCK_ROWS * C)
    is_vector = position >= 12 * C * C
    step_rate = jnp.where(is_vector, RATE_VECTOR, RATE_MATRIX)
    weight_decay = jnp.where(is_vector, 0.0, DECAY_MATRIX)
    moment_one = BETA_FIRST * first_moment + (1.0 - BETA_FIRST) * shard_grad
    moment_two = BETA_SECOND * second_moment + (1.0 - BETA_SECOND) * shard_grad * shard_grad
    corrected_one = moment_one / (1.0 - BETA_FIRST**STEP)
    corrected_two = moment_two / (1.0 - BETA_SECOND**STEP)
    normalized = corrected_one / (jnp.sqrt(corrected_two) + ADAM_EPS)
    new_master = master - step_rate * (normalized + weight_decay * master)
    return (
        layers.output.transpose(0, 1, 3, 2),
        layers.input_grad.transpose(0, 1, 3, 2),
        new_master,
        moment_one,
        moment_two,
        new_master.astype(BF),
    )


def solution(mesh):
    placed = (
        P(None, (VOL, WIN), None, None),
        P(None, (VOL, WIN), None, None),
        P(),
        P(None, (VOL, WIN)),
        P(None, (VOL, WIN), None),
        P((VOL, WIN)),
        P((VOL, WIN)),
        P((VOL, WIN)),
    )
    return jax.shard_map(
        on_device,
        mesh=mesh,
        in_specs=placed,
        out_specs=(
            P(None, (VOL, WIN), None, None),
            P(None, (VOL, WIN), None, None),
            P((VOL, WIN)),
            P((VOL, WIN)),
            P((VOL, WIN)),
            P((VOL, WIN)),
        ),
        check_vma=False,
    )
```

```python
from types import SimpleNamespace

import jax
import jax.numpy as jnp
import numpy as np
from jax import lax
from jax.experimental import pallas as pl
from jax.experimental.pallas import tpu as pltpu
from jax.sharding import PartitionSpec as P

C = 96
HEADS = 6
HEAD_DIM = 16
FF = 384
SIDE = 7
SHIFT = 3
WS = 343
STEP = 6
T = 384
WINDOWS = 2
TABLE_SLOTS = 3
ROWS = (352, T)
CA = 128
BLOCK_ROWS = 1164

NORM_EPS = 1e-05
MASK_FILL = -1000000000.0
BETA_FIRST = 0.5
BETA_SECOND = 0.5
ADAM_EPS = 1e-08
RATE_MATRIX = 0.1
RATE_VECTOR = 0.4
DECAY_MATRIX = 0.05

BF = jnp.bfloat16
F32 = jnp.float32
NN = (((1,), (0,)), ((), ()))
NT = (((1,), (1,)), ((), ()))
BY_STEP, WHOLE, SMEM, HBM = range(4)
MESH = pl.DeviceIdType.MESH
VOL, WIN = "vol", "win"
KEPT_NAMES = ("a0", "a1"), ("b0", "b1")


def octant_bits(octant):
    return (octant >> 2 & 1, octant >> 1 & 1, octant & 1)


OCT_SIZE = []
OCT_LEN = []
OCT_OFF = []
for _octant in range(8):
    _size = 1
    for _bit in octant_bits(_octant):
        _size *= SHIFT if _bit else SIDE - SHIFT
    OCT_OFF.append(sum(OCT_LEN))
    OCT_SIZE.append(_size)
    OCT_LEN.append(-(-_size // 16) * 16)


def slot_tables():
    perm = np.zeros((T, T), np.float32)
    order = np.zeros((T, WS), np.float32)
    places = np.full((8, T), 99, np.int32)
    for octant in range(8):
        bits = octant_bits(octant)
        lens = [SHIFT if bit else SIDE - SHIFT for bit in bits]
        for i in range(lens[0]):
            for j in range(lens[1]):
                for k in range(lens[2]):
                    source = [v if bit else v + SHIFT for v, bit in zip((i, j, k), bits)]
                    own = [v + bit * (SIDE - SHIFT) for v, bit in zip((i, j, k), bits)]
                    q = OCT_OFF[octant] + (i * lens[1] + j) * lens[2] + k
                    t = (source[0] * SIDE + source[1]) * SIDE + source[2]
                    perm[q, t] = 1
                    order[q, (own[0] * SIDE + own[1]) * SIDE + own[2]] = 1
                    places[:3, t] = source
    return perm, order, places


PERM, ORDER, PLACES = slot_tables()


def dot(a, b, dims=NN):
    return lax.dot_general(a, b, dims, preferred_element_type=F32)


def wide(column):
    return jnp.concatenate([column] * (T // 128), axis=1)


def ln_stats(x):
    centred = x - jnp.mean(x, axis=0, keepdims=True)
    scale = lax.rsqrt(jnp.mean(centred * centred, axis=0, keepdims=True) + NORM_EPS)
    return centred * scale, scale


def norm_back(e, z, scale, gain):
    eg = e * gain
    return scale * (
        eg - jnp.mean(eg, axis=0, keepdims=True) - z * jnp.mean(eg * z, axis=0, keepdims=True)
    )


def gelu_pair(h):
    base = 1.0 + (0.3275911 * 0.7071067811865476) * jnp.abs(h)
    t = pl.reciprocal(base, approx=True)
    t = t * (2.0 - base * t)
    poly = t * (
        0.5 * 0.254829592
        + t
        * (
            0.5 * -0.284496736
            + t * (0.5 * 1.421413741 + t * (0.5 * -1.453152027 + t * (0.5 * 1.061405429)))
        )
    )
    bell = jnp.exp(-0.5 * (h * h))
    tail = poly * bell
    phi = jnp.where(h < 0.0, tail, 1.0 - tail)
    return h * phi, phi + h * bell * 0.3989422804014327


def ones_row(shape, row=0):
    return jnp.where(lax.broadcasted_iota(jnp.int32, shape, 0) == row, 1.0, 0.0)


def weave(tasks, lag):
    clocks = [lag * n for n in range(len(tasks))]
    while tasks:
        n = clocks.index(min(clocks))
        cost = next(tasks[n], None)
        if cost is None:
            tasks, clocks = (x[:n] + x[n + 1 :] for x in (tasks, clocks))
        else:
            clocks[n] += cost


def clear_scratch(r):
    zeros = jnp.zeros((CA, HEADS * T), BF)
    for i in range(WINDOWS):
        r.qb[i] = zeros
        r.dab[i] = zeros
        r.rb[i] = jnp.zeros((2, 2 * C, 2 * T), BF)
        r.pad[i] = jnp.zeros((C, T), BF)
        r.cot[i] = jnp.zeros((C, T), BF)
        for h in range(HEADS):
            r.vt[i, h, 16:32, :] = ones_row((16, T)).astype(BF)
    for name, (shape, dtype) in GRADS.items():
        getattr(r, name)[...] = jnp.zeros((2,) + shape, dtype)


def table_copy(r, n):
    slot = n % TABLE_SLOTS
    return pltpu.make_async_copy(
        r.table.at[n // HEADS, n % HEADS], r.page.at[slot], r.turned.at[slot]
    )


def turn_tables(r, layer):
    for n in range(HEADS * layer, HEADS * layer + HEADS):
        table_copy(r, n).wait()
        half = dot(r.order[layer], r.page[n % TABLE_SLOTS], NT).astype(BF)
        if n + TABLE_SLOTS < 2 * HEADS:
            table_copy(r, n + TABLE_SLOTS).start()
        r.bias[layer, n % HEADS] = dot(half, r.order[layer], NT)


def set_queries(sc, queries):
    for h in range(HEADS):
        sc.qb[16 * h : 16 * h + 16, T * h : T * h + T] = queries[16 * h : 16 * h + 16, :]


def forward_attention(sc, w, st, code_row):
    z, _ = ln_stats(st.x)
    sc.n1aug[C:CA, :] = ones_row((CA - C, T)).astype(BF)
    sc.attaug[C:CA, :] = ones_row((CA - C, T)).astype(BF)
    sc.n1aug[0:C, :] = (z * wide(w.vec[0]) + wide(w.vec[1])).astype(BF)
    yield 150
    kv = dot(sc.n1aug[...].T, w.kv[...]).astype(BF)
    sc.kn[...] = kv[:, 0:CA]
    sc.vn[...] = kv[:, CA:]
    yield 200
    qkv = dot(w.qkvT[...], sc.n1aug[...])
    queries = qkv[0:C].astype(BF)
    set_queries(sc, queries)
    sc.qT[...] = queries
    sc.kT[...] = qkv[C : 2 * C].astype(BF)
    values = qkv[2 * C :].astype(BF)
    for h in range(HEADS):
        sc.vt[h, 0:16, :] = values[16 * h : 16 * h + 16, :]
    yield 150
    eye = lax.broadcasted_iota(jnp.int32, (128, 128), 0) == lax.broadcasted_iota(
        jnp.int32, (128, 128), 1
    )
    tops = [None] * HEADS

    def scores(h, c):
        rows = slice(128 * c, min(128 * c + 128, sc.rows))
        count = rows.stop - rows.start
        x_all = dot(sc.kn[rows], sc.qb[:, T * h : T * h + T])
        codes = sc.codes[rows]
        parts = []
        for j in range(3):
            lanes = slice(128 * j, 128 * j + 128)
            allowed = codes == code_row[:, lanes]
            if j == c:
                allowed = allowed | eye[0:count]
            part = jnp.where(allowed, x_all[:, lanes] + sc.bias[h, rows, lanes], MASK_FILL)
            sc.s[h % 2, rows, lanes] = part
            parts.append(jnp.max(part.reshape(count // 8, 8, 128), axis=0))
        top = jnp.concatenate(parts, axis=1)
        tops[h] = top if tops[h] is None else jnp.maximum(tops[h], top)

    def raise_(h, c):
        rows = slice(128 * c, min(128 * c + 128, sc.rows))
        sc.e[rows, T * h : T * h + T] = jnp.exp(sc.s[h % 2, rows] - tops[h]).astype(BF)

    def attend(h):
        out = dot(sc.vt[h, :, 0 : sc.rows], sc.e[:, T * h : T * h + T])
        inverse = 1.0 / out[16:17]
        part = out[0:16] * inverse
        sc.att[16 * h : 16 * h + 16, :] = part
        sc.inv[h : h + 1, :] = inverse
        sc.attaug[16 * h : 16 * h + 16, :] = part.astype(BF)

    for h in range(HEADS + 2):
        for c in range(3):
            if h < HEADS:
                scores(h, c)
            if 0 <= h - 1 < HEADS:
                raise_(h - 1, c)
            if c == 0 and 0 <= h - 2 < HEADS:
                attend(h - 2)
            yield 70
        if h < HEADS:
            tops[h] = jnp.max(tops[h], axis=0, keepdims=True)
    st.branch = dot(w.projT[...], sc.attaug[...])
    yield 100


def backward_attention(sc, w, st, z, scale, shifted):
    d_mid = st.d
    db = d_mid.astype(BF)
    d_att = dot(w.proj[...], db).astype(BF).astype(F32)
    sc.gproj[...] += dot(sc.attaug[...], db, NT)
    yield 150
    row = lax.broadcasted_iota(jnp.int32, (16, T), 0)
    for h in range(HEADS):
        part = (d_att[16 * h : 16 * h + 16] * sc.inv[h : h + 1, :]).astype(BF)
        cols = slice(T * h, T * h + T)
        sc.dab[16 * h : 16 * h + 16, cols] = part
        inner = -jnp.sum(
            part.astype(F32) * sc.att[16 * h : 16 * h + 16, :], axis=0, keepdims=True
        )
        high = inner.astype(BF).astype(F32)
        low = inner - high
        sc.dab[C : C + 16, cols] = jnp.where(
            row == 0, high, jnp.where(row == 1, low, 0.0)
        ).astype(BF)
    yield 100
    total = None
    none = jnp.zeros((16, T), BF)

    def soft(h):
        cols = slice(T * h, T * h + T)
        pull = dot(sc.vn[0 : sc.rows], sc.dab[:, cols])
        sc.ds[h % 2, 0 : sc.rows] = (pull * sc.e[:, cols].astype(F32)).astype(BF)

    def place_rows(h):
        rb = sc.rb.at[h % 2]
        last = (h - 2) % HEADS
        rb[16 * last : 16 * last + 16, T:] = none
        rb[C + 16 * last : C + 16 * last + 16, 0:T] = none
        rb[16 * h : 16 * h + 16, T:] = sc.qT[16 * h : 16 * h + 16, :]
        rb[C + 16 * h : C + 16 * h + 16, 0:T] = sc.dab[
            16 * h : 16 * h + 16, T * h : T * h + T
        ]

    def to_queries(h):
        sc.dq[16 * h : 16 * h + 16, :] = dot(
            sc.kT[16 * h : 16 * h + 16, 0 : sc.rows], sc.ds[h % 2, 0 : sc.rows]
        ).astype(BF)

    for h in range(HEADS + 1):
        if h < HEADS:
            place_rows(h)
            soft(h)
            yield 120
        if h > 0:
            to_queries(h - 1)
            yield 60
            both = jnp.concatenate(
                [sc.e[:, T * (h - 1) : T * h], sc.ds[(h - 1) % 2, 0 : sc.rows]], axis=1
            )
            term = dot(both, sc.rb[(h - 1) % 2], NT)
            total = term if total is None else total + term
            yield 180
    dkv = total.astype(BF)
    if sc.rows < T:
        dkv = jnp.concatenate([dkv, jnp.zeros((T - sc.rows, 2 * C), BF)], axis=0)
    dq = sc.dq[...]
    dn = dot(w.q[...], dq) + dot(w.kv96[...], dkv, NT)
    yield 120
    sc.gkv[...] += dot(sc.n1aug[...], dkv)
    sc.gq[...] += dot(dq, sc.n1aug[...], NT)
    yield 150
    if shifted:
        dn = dn.astype(BF).astype(F32)
    sc.gvec[0] += dn * z
    sc.gvec[1] += dn
    st.d = d_mid + norm_back(dn, z, scale, wide(w.vec[0]))
    yield 150


def feed_forward_back(sc, w, st, dd, z, scale):
    dn = dot(w.up[...], sc.dh[...])
    yield 120
    sc.gdown[...] += dot(sc.act[...], dd, NT)
    yield 120
    sc.gup[...] += dot(sc.dh[...], sc.n2aug[...], NT)
    yield 120
    sc.gvec[4] += dd.astype(F32)
    sc.gvec[2] += dn * z
    sc.gvec[3] += dn
    st.d = st.d + norm_back(dn, z, scale, wide(w.vec[2]))
    yield 150


def write_grads(sc, out):
    gq = sc.gq[...].T
    gkv = sc.gkv[...]
    gup = sc.gup[...].T
    out[pl.ds(0, C, 3), :] = gq[0:C]
    out[pl.ds(1, C, 3), :] = gkv[0:C, 0:C]
    out[pl.ds(2, C, 3), :] = gkv[0:C, C : 2 * C]
    out[3 * C : 4 * C, :] = sc.gproj[0:C, :]
    for j in range(4):
        out[pl.ds(4 * C + j, C, 4), :] = gup[0:C, C * j : C * j + C]
    out[8 * C : 12 * C, :] = sc.gdown[...]
    sums = [jnp.sum(sc.gvec[n].T, axis=0, keepdims=True) for n in range(5)]
    rows = [
        sums[0],
        sums[1],
        gq[C : C + 1],
        gkv[C : C + 1, C : 2 * C],
        sc.gproj[C : C + 1, :],
        sums[2],
        sums[3],
        sums[4],
    ] + [gup[C : C + 1, C * j : C * j + C] for j in range(4)]
    for n, value in enumerate(rows):
        out[12 * C + n : 12 * C + n + 1, :] = value


FWD = dict(
    qb=((CA, HEADS * T), BF),
    vt=((HEADS, 32, T), BF),
    kn=((T, CA), BF),
    codes=((T, 128), F32),
    s=((2, T, T), F32),
)
BIAS = dict(bias=((HEADS, T, T), F32))
KEPT = dict(
    qT=((C, T), BF),
    kT=((C, T), BF),
    vn=((T, CA), BF),
    e=((T, HEADS * T), BF),
    att=((C, T), F32),
    inv=((8, T), F32),
    attaug=((CA, T), BF),
    n1aug=((CA, T), BF),
    n2aug=((CA, T), BF),
    act=((FF, T), BF),
    gp=((FF, T), BF),
    xT=((C, T), BF),
    x1=((C, T), F32),
)
GRADS = dict(
    gq=((C, CA), F32),
    gkv=((CA, 2 * C), F32),
    gproj=((CA, C), F32),
    gup=((FF, CA), F32),
    gdown=((FF, C), F32),
    gvec=((5, C, T), F32),
)
BWD = dict(
    dab=((CA, HEADS * T), BF),
    rb=((2, 2 * C, 2 * T), BF),
    ds=((2, T, T), BF),
    dq=((C, T), BF),
    dh=((FF, T), BF),
)


PADS = dict(pad=((C, T), BF), cot=((C, T), BF))
WEIGHTS = dict(
    qkvT=((3 * C, CA), BF),
    kv=((CA, 2 * CA), BF),
    projT=((C, CA), BF),
    proj=((C, C), BF),
    upT=((FF, CA), BF),
    up=((C, FF), BF),
    downT=((C, FF), BF),
    down=((FF, C), BF),
    q=((C, C), BF),
    kv96=((C, 2 * C), BF),
    vec=((5, C, 128), F32),
)


def of_layer(r, layer, slot):
    shared = {n: getattr(r, n).at[layer] for n in (*WEIGHTS, *GRADS, *BIAS)}
    return [
        SimpleNamespace(
            rows=ROWS[layer],
            **shared,
            **{n: getattr(r, n).at[i] for n in (*FWD, *BWD, *PADS)},
            **{n: getattr(r, KEPT_NAMES[layer][i] + n).at[slot] for n in KEPT},
        )
        for i in range(WINDOWS)
    ]


def second_norm(sc, w, x):
    z, scale = ln_stats(x)
    sc.n2aug[C:CA, :] = ones_row((CA - C, T)).astype(BF)
    sc.n2aug[0:C, :] = (z * wide(w.vec[2]) + wide(w.vec[3])).astype(BF)
    return z, scale


def grid_place(groups_a):
    win = lax.axis_index(WIN)
    return (win // 4, win // 2 % 2, win % 2), (groups_a, 2, 2)


def neighbour(octant, sign, groups_a):
    place, sizes = grid_place(groups_a)
    a, b, c = (
        (p + sign * bit + n) % n for p, bit, n in zip(place, octant_bits(octant), sizes)
    )
    return lax.axis_index(VOL), (a * 2 + b) * 2 + c


def greet(peers):
    barrier = pltpu.get_barrier_semaphore()
    for peer in peers:
        pl.semaphore_signal(barrier, inc=1, device_id=peer, device_id_type=MESH)


def await_greetings(peers):
    pl.semaphore_wait(pltpu.get_barrier_semaphore(), len(peers))


def block_copy(way, m, octant, groups_a):
    rows = pl.ds(OCT_OFF[octant], OCT_LEN[octant])
    slot = m % 2
    source = way.stage.at[slot, :, rows]
    target = way.got.at[pl.ds(m * WINDOWS, WINDOWS), rows]
    if octant == 0:
        return pltpu.make_async_copy(source, target, way.arrived.at[m, 0])
    return pltpu.make_async_remote_copy(
        src_ref=source,
        dst_ref=target,
        send_sem=way.sent.at[slot, octant],
        recv_sem=way.arrived.at[m, octant],
        device_id=neighbour(octant, way.sign, groups_a),
        device_id_type=MESH,
    )


def send_blocks(way, m, groups_a):
    for octant in range(8):
        block_copy(way, m, octant, groups_a).start()


def wait_sent(way, m, groups_a):
    for octant in range(1, 8):
        block_copy(way, m, octant, groups_a).wait_send()


def wait_arrived(way, m, groups_a):
    block_copy(way, m, 0, groups_a).wait()
    for octant in range(1, 8):
        block_copy(way, m, octant, groups_a).wait_recv()


def first_forward(r, sc, m, i):
    w, st = sc, SimpleNamespace()
    stage = r.x_stage.at[m % 2, i]
    sc.pad[:, 0:WS] = r.tokens[i, 0]
    st.x = sc.pad[...].astype(F32)
    sc.xT[...] = sc.pad[...]
    places = r.places
    valid = (
        (places[0:1, :] < r.info[m * WINDOWS + i, 1])
        & (places[1:2, :] < r.info[m * WINDOWS + i, 2])
        & (places[2:3, :] < r.info[m * WINDOWS + i, 3])
    )
    valid = jnp.where(valid, 1.0, 0.0)
    sc.codes[...] = jnp.broadcast_to(valid - 1.0, (128, T)).T
    yield 100
    yield from forward_attention(sc, w, st, jnp.zeros((1, T), F32))
    sc.cot[:, 0:WS] = r.cotangent[i, 0]
    stage[:, CA:] = jnp.concatenate(
        [dot(r.perm[...], sc.cot[...], NT), jnp.zeros((T, CA - C), F32)], axis=1
    ).astype(BF)
    yield 100
    x = st.x + st.branch
    sc.x1[...] = x
    second_norm(sc, w, x)
    yield 150
    for c in range(6):
        rows = slice(64 * c, 64 * c + 64)
        active, slope = gelu_pair(dot(w.upT[rows], sc.n2aug[...]))
        sc.act[rows, :] = active.astype(BF)
        sc.gp[rows, :] = slope.astype(BF)
        yield 100
    x = x + (dot(w.downT[...], sc.act[...]) + wide(w.vec[4]))
    yield 100
    row = lax.broadcasted_iota(jnp.int32, (CA - C, T), 0)
    label = r.info[m * WINDOWS + i, 0].astype(F32)
    extra = jnp.where(row == 0, label, jnp.where(row == 1, valid, 0.0))
    x = jnp.concatenate([x, extra], axis=0).astype(BF)
    stage[:, 0:CA] = dot(r.perm[...], x, NT).astype(BF)
    yield 100


def second_layer(r, sc, m, i, groups_a):
    w, st = sc, SimpleNamespace()
    stage = r.d_stage.at[m % 2, i]
    n = m * WINDOWS + i
    came = r.x_got[n, :, 0:CA]
    x = came.T.astype(F32)
    place, sizes = grid_place(groups_a)
    code_row = []
    for octant in range(8):
        rows = slice(OCT_OFF[octant], OCT_OFF[octant] + OCT_LEN[octant])
        wraps = [
            bit * jnp.where(p == n_ - 1, 1, 0)
            for p, bit, n_ in zip(place, octant_bits(octant), sizes)
        ]
        wrap = (wraps[0] * 4 + wraps[1] * 2 + wraps[2]).astype(F32)
        columns = came[rows].astype(F32)
        code = jnp.where(columns[:, C + 1 : C + 2] > 0.0, columns[:, C : C + 1] * 8.0 + wrap, -1.0)
        sc.codes[rows, :] = jnp.broadcast_to(code, (OCT_LEN[octant], 128))
        code_row.append(jnp.full((1, OCT_LEN[octant]), wrap))
    code_row = jnp.concatenate(code_row, axis=1) + 8.0 * x[C : C + 1]
    keep = x[C + 1 : C + 2]
    x = x[0:C]
    sc.xT[...] = x.astype(BF)
    st.x = x
    yield 150
    yield from forward_attention(sc, w, st, code_row)
    st.d = r.x_got[n, :, CA:].T[0:C].astype(F32) * keep
    dd = st.d.astype(BF)
    x = sc.xT[...].astype(F32) + st.branch.astype(BF).astype(F32)
    z, scale = second_norm(sc, w, x)
    yield 200
    for c in range(6):
        rows = slice(64 * c, 64 * c + 64)
        active, slope = gelu_pair(dot(w.upT[rows], sc.n2aug[...]))
        sc.act[rows, :] = active.astype(BF)
        sc.dh[rows, :] = (dot(w.down[rows], dd) * slope).astype(BF)
        yield 120
    x = x + (dot(w.downT[...], sc.act[...]) + wide(w.vec[4]))
    none = jnp.zeros((CA - C, T), F32)
    stage[:, 0:CA] = jnp.concatenate([x * keep, none], axis=0).T.astype(BF)
    yield 150
    yield from feed_forward_back(sc, w, st, dd, z, scale)
    z, scale = ln_stats(sc.xT[...].astype(F32))
    yield from backward_attention(sc, w, st, z, scale, True)
    stage[:, CA:] = jnp.concatenate([st.d, none], axis=0).T.astype(BF)
    yield 100


def first_backward(r, sc, m, i):
    w, st = sc, SimpleNamespace()
    came = r.d_got[m * WINDOWS + i].T
    came = jnp.concatenate([came[0:C], came[CA : CA + C]], axis=0)
    yield 200
    came = dot(came, r.perm[...])
    r.output[i, 0] = came[0:C, 0:WS].astype(BF)
    st.d = came[C : 2 * C]
    dd = st.d.astype(BF)
    z, scale = ln_stats(sc.x1[...])
    yield 200
    for c in range(3):
        rows = slice(128 * c, 128 * c + 128)
        sc.dh[rows, :] = (dot(w.down[rows], dd) * sc.gp[rows, :].astype(F32)).astype(BF)
        yield 50
    yield from feed_forward_back(sc, w, st, dd, z, scale)
    z, scale = ln_stats(sc.xT[...].astype(F32))
    yield from backward_attention(sc, w, st, z, scale, False)
    r.input_grad[i, 0] = st.d[:, 0:WS]
    yield 50


def layers_kernel(n_vol, n_plane, shard_len, steps, r):
    groups_a = n_plane // 2
    s = pl.program_id(0)
    forth = SimpleNamespace(
        stage=r.x_stage, got=r.x_got, sent=r.x_sent, arrived=r.x_arrived, sign=-1
    )
    back = SimpleNamespace(
        stage=r.d_stage, got=r.d_got, sent=r.d_sent, arrived=r.d_arrived, sign=1
    )

    far = all_peers(n_vol, n_plane)
    reduction = Reduction(r, far, n_vol, n_plane, shard_len)

    @pl.when(s == 0)
    def _():
        peers = far + [
            neighbour(octant, sign, groups_a) for sign in (1, -1) for octant in range(1, 8)
        ]
        greet(peers)
        for n in range(TABLE_SLOTS):
            table_copy(r, n).start()
        vol, plane, core = own_place()
        r.buf[core, plane, vol] = r.shard[...]
        clear_scratch(r)
        await_greetings(peers)
        meanwhile = (lambda: None, lambda: turn_tables(r, 0), lambda: turn_tables(r, 1))
        for copies, work in zip(gather_stages(r, far, n_vol, n_plane), meanwhile):
            for c in copies:
                c.start()
            work()
            for c in copies:
                c.wait()
        prepare(r, n_vol, n_plane, shard_len)

    @pl.when(s < steps)
    def _():
        @pl.when(s >= 2)
        def _():
            wait_sent(forth, s - 2, groups_a)

        windows = of_layer(r, 0, s % 3)
        weave([first_forward(r, sc, s, i) for i, sc in enumerate(windows)], 0)
        send_blocks(forth, s, groups_a)

    @pl.when((s >= 1) & (s <= steps))
    def _():
        m = s - 1
        wait_arrived(forth, m, groups_a)

        @pl.when(m >= 2)
        def _():
            wait_sent(back, m - 2, groups_a)

        windows = of_layer(r, 1, 0)
        weave([second_layer(r, sc, m, i, groups_a) for i, sc in enumerate(windows)], 0)
        send_blocks(back, m, groups_a)

    @pl.when(s == steps)
    def _():
        write_grads(of_layer(r, 1, 0)[0], r.grads.at[1])
        reduction.start_core(1)

    @pl.when(s == steps + 1)
    def _():
        reduction.start_plane(1)

    @pl.when(s >= 2)
    def _():
        m = s - 2
        wait_arrived(back, m, groups_a)
        windows = of_layer(r, 0, m % 3)
        weave([first_backward(r, sc, m, i) for i, sc in enumerate(windows)], 0)

    @pl.when(s == steps + 1)
    def _():
        write_grads(of_layer(r, 0, 0)[0], r.grads.at[0])
        reduction.start_core(0)
        reduction.end_plane(1)
        reduction.start_plane(0)
        for m in range(max(steps - 2, 0), steps):
            wait_sent(forth, m, groups_a)
            wait_sent(back, m, groups_a)
        reduction.end_plane(0)
        reduction.finish()


def shard_rows(device, shard_len):
    return device * shard_len // C, -(-(device + 1) * shard_len // C)


def flat_offset(device, shard_len):
    return device * shard_len % C


def slab_rows(shard_len):
    return -(-((shard_len + C - 2) // C + 1) // 16) * 16


def own_place():
    win = lax.axis_index(WIN)
    return lax.axis_index(VOL), win // 2, win % 2


def all_peers(n_vol, n_plane):
    vol, plane, core = own_place()
    return (
        [((vol + j) % n_vol, plane * 2 + core) for j in range(1, n_vol)]
        + [(vol, (plane + j) % n_plane * 2 + core) for j in range(1, n_plane)]
        + [(vol, plane * 2 + 1 - core)]
    )


def transpose_with(matrix, extra):
    below = jnp.where(lax.broadcasted_iota(jnp.int32, (CA - C, C), 0) == 0, extra, 0.0)
    return jnp.concatenate([matrix, below], axis=0).T


def gather_stages(r, peers, n_vol, n_plane):
    vol, plane, core = own_place()

    def copy(ref, n):
        return pltpu.make_async_remote_copy(
            src_ref=ref,
            dst_ref=ref,
            send_sem=r.g_sent.at[n],
            recv_sem=r.g_arrived.at[n],
            device_id=peers[n],
            device_id_type=MESH,
        )

    return (
        [copy(r.buf.at[core, plane, vol], n) for n in range(n_vol - 1)],
        [copy(r.buf.at[core, plane], n_vol - 1 + n) for n in range(n_plane - 1)],
        [copy(r.buf.at[core], n_vol + n_plane - 2)],
    )


def prepare(r, n_vol, n_plane, shard_len):
    buf = r.buf
    flat = r.grads
    flat[...] = jnp.zeros(flat.shape, F32)
    half = n_vol * n_plane
    for v in range(n_vol):
        for p in range(n_plane):
            for c in range(2):
                device = (v * n_plane + p) * 2 + c
                start, stop = shard_rows(device % half, shard_len)
                flat[device // half, start:stop, :] += buf[c, p, v, 0 : stop - start].astype(F32)
    for layer in range(2):

        def rows(start, count=C, stride=1):
            return flat[layer, pl.ds(start, count, stride), :]

        def vector(n):
            return rows(12 * C + n, 1)

        o = SimpleNamespace(**{n: getattr(r, n).at[layer] for n in WEIGHTS})
        none = jnp.zeros((1, C), F32)
        wq, wk, wv = (rows(n, C, 3) for n in range(3))
        o.q[...] = wq.astype(BF)
        o.kv96[...] = jnp.concatenate([wk, wv], axis=1).astype(BF)
        o.qkvT[0:C, :] = (transpose_with(wq, vector(2)) * 0.25).astype(BF)
        o.qkvT[C : 2 * C, :] = (transpose_with(wk, none) * 0.25).astype(BF)
        o.qkvT[2 * C :, :] = transpose_with(wv, vector(3)).astype(BF)
        row = lax.broadcasted_iota(jnp.int32, (CA - C, CA), 0)
        lane = lax.broadcasted_iota(jnp.int32, (CA - C, CA), 1)
        blank = jnp.zeros((C, CA - C), F32)
        bias_v = jnp.concatenate([vector(3), blank[0:1]], axis=1)
        ones = jnp.where((lane == C) | (lane == C + 1), 1.0, bias_v)
        o.kv[0:C, :] = jnp.concatenate([wk, blank, wv, blank], axis=1).astype(BF)
        o.kv[C:, 0:CA] = jnp.zeros((CA - C, CA), BF)
        o.kv[C:, CA:] = jnp.where(row == 0, ones, 0.0).astype(BF)
        proj = rows(3 * C)
        o.proj[...] = proj.astype(BF)
        o.projT[...] = transpose_with(proj, vector(4)).astype(BF)
        ups = [rows(4 * C + j, C, 4) for j in range(4)]
        o.up[...] = jnp.concatenate(ups, axis=1).astype(BF)
        for j in range(4):
            o.upT[C * j : C * j + C, :] = transpose_with(ups[j], vector(8 + j)).astype(BF)
        down = rows(8 * C, FF)
        o.down[...] = down.astype(BF)
        o.downT[...] = down.T.astype(BF)
        for n, source in enumerate((0, 1, 5, 6, 7)):
            o.vec[n] = jnp.broadcast_to(vector(source), (128, C)).T


class Reduction:
    def __init__(self, r, peers, n_vol, n_plane, shard_len):
        self.r, self.peers, self.shard_len = r, peers, shard_len
        self.n_vol, self.n_plane, self.half = n_vol, n_plane, n_vol // 2
        self.vol, self.plane, self.core = own_place()

    def vols(self, layer):
        return pl.ds(layer * self.half, self.half)

    def copy(self, source, target, peer, n):
        return pltpu.make_async_remote_copy(
            src_ref=source,
            dst_ref=target,
            send_sem=self.r.r_sent.at[n],
            recv_sem=self.r.r_arrived.at[n],
            device_id=self.peers[peer],
            device_id_type=MESH,
        )

    def over_core(self, layer):
        source = self.r.work.at[1 - self.core, :, self.vols(layer)]
        return [self.copy(source, self.r.from_core.at[layer], len(self.peers) - 1, layer)]

    def over_plane(self, layer):
        return [
            self.copy(
                self.r.wire.at[(self.plane + j) % self.n_plane, self.vols(layer)],
                self.r.from_plane.at[layer, j - 1],
                self.n_vol - 2 + j,
                2 + layer * (self.n_plane - 1) + j - 1,
            )
            for j in range(1, self.n_plane)
        ]

    def over_vol(self):
        return [
            self.copy(
                self.r.wire.at[self.plane, (self.vol + j) % self.n_vol],
                self.r.from_vol.at[j - 1],
                j - 1,
                2 * self.n_plane + j - 1,
            )
            for j in range(1, self.n_vol)
        ]

    def start_core(self, layer):
        for v in range(layer * self.half, (layer + 1) * self.half):
            for p in range(self.n_plane):
                for c in range(2):
                    device = (v % self.half * self.n_plane + p) * 2 + c
                    start, stop = shard_rows(device, self.shard_len)
                    self.r.work[c, p, v, 0 : stop - start] = self.r.grads[layer, start:stop, :]
        for c in self.over_core(layer):
            c.start()

    def start_plane(self, layer):
        for c in self.over_core(layer):
            c.wait()
        vols, work = self.vols(layer), self.r.work
        total = work[self.core, :, vols] + self.r.from_core[layer]
        work[self.core, :, vols] = total
        self.r.wire[:, vols] = total.astype(BF)
        for c in self.over_plane(layer):
            c.start()

    def end_plane(self, layer):
        for c in self.over_plane(layer):
            c.wait()
        vols, work = self.vols(layer), self.r.work
        total = work[self.core, self.plane, vols]
        for j in range(self.n_plane - 1):
            total = total + self.r.from_plane[layer, j].astype(F32)
        work[self.core, self.plane, vols] = total
        self.r.wire[self.plane, vols] = total.astype(BF)

    def finish(self):
        for c in self.over_vol():
            c.start()
        for c in self.over_vol():
            c.wait()
        total = self.r.work[self.core, self.plane, self.vol]
        for j in range(self.n_vol - 1):
            total = total + self.r.from_vol[j].astype(F32)
        self.r.total[...] = total


def call(kernel, steps, ins, outs, scratch, semaphores=(), collective_id=None, lag=0):
    def spec(shape, kind, late):
        if kind in (SMEM, HBM):
            return pl.BlockSpec(memory_space=pltpu.SMEM if kind is SMEM else pl.ANY)
        zeros = (0,) * (len(shape) - 1)
        if kind is BY_STEP:

            def index(s):
                return (jnp.clip(s - late, 0, steps - 1),) + zeros

            return pl.BlockSpec((shape[0] // steps,) + tuple(shape[1:]), index)
        return pl.BlockSpec(
            tuple(shape), lambda s: (0,) + zeros, pipeline_mode=None if late else pl.Buffered(1)
        )

    semaphores = dict(semaphores)
    names = tuple(ins) + tuple(outs) + tuple(scratch) + tuple(semaphores)

    def body(*refs):
        kernel(SimpleNamespace(**dict(zip(names, refs))))

    results = pl.pallas_call(
        body,
        grid=(steps + lag,),
        in_specs=[spec(a.shape, kind, 0) for a, kind in ins.values()],
        out_specs=[spec(shape, kind, lag) for shape, _, kind in outs.values()],
        out_shape=[jax.ShapeDtypeStruct(shape, dtype) for shape, dtype, _ in outs.values()],
        scratch_shapes=[pltpu.VMEM(shape, dtype) for shape, dtype in scratch.values()]
        + [pltpu.SemaphoreType.DMA(shape) for shape in semaphores.values()],
        compiler_params=pltpu.CompilerParams(
            vmem_limit_bytes=62 * 2**20,
            collective_id=collective_id,
            has_side_effects=collective_id is not None,
        ),
    )(*[a for a, _ in ins.values()])
    return SimpleNamespace(**dict(zip(outs, results)))


def on_device(
    tokens,
    cotangent,
    position_bias,
    window_volume,
    clip_extent,
    master,
    first_moment,
    second_moment,
):
    n_vol, n_win = lax.axis_size(VOL), lax.axis_size(WIN)
    n_plane = n_win // 2
    count = tokens.shape[0]
    steps = count // WINDOWS
    shard_len = master.shape[0]
    device = lax.axis_index((VOL, WIN))
    slab = slab_rows(shard_len)
    offset = flat_offset(device, shard_len)
    shard = lax.dynamic_update_slice(jnp.zeros((slab * C,), BF), master.astype(BF), (offset,))
    n_peers = n_vol + n_plane - 1
    info = jnp.concatenate((window_volume[:, :, None], clip_extent), axis=2)[:, 0]

    def each(table, *sizes):
        return {n: (sizes + shape, dtype) for n, (shape, dtype) in table.items()}

    def kept(layer, slots):
        shapes = dict(KEPT, e=((ROWS[layer], HEADS * T), BF))
        shapes = dict(shapes, gp=((16, T), BF)) if layer else shapes
        return {name + n: v for name in KEPT_NAMES[layer] for n, v in each(shapes, slots).items()}

    stage, landing = ((2, WINDOWS, T, 2 * CA), BF), ((count, T, 2 * CA), BF)
    layers = call(
        lambda r: layers_kernel(n_vol, n_plane, shard_len, steps, r),
        steps,
        dict(
            tokens=(tokens.transpose(0, 1, 3, 2), BY_STEP),
            cotangent=(cotangent.transpose(0, 1, 3, 2), BY_STEP),
            info=(info, SMEM),
            perm=(jnp.asarray(PERM, BF), WHOLE),
            places=(jnp.asarray(PLACES), WHOLE),
            order=(jnp.asarray(np.stack([np.eye(T, WS), ORDER]), BF), WHOLE),
            table=(position_bias, HBM),
            shard=(shard.reshape(slab, C), WHOLE),
        ),
        dict(
            output=((count, 1, C, WS), BF, BY_STEP),
            input_grad=((count, 1, C, WS), F32, BY_STEP),
            total=((slab, C), F32, WHOLE),
        ),
        dict(
            **each(FWD, WINDOWS),
            **each(BWD, WINDOWS),
            **each(PADS, WINDOWS),
            **each(GRADS, 2),
            **each(BIAS, 2),
            **kept(0, 3),
            **kept(1, 1),
            **each(WEIGHTS, 2),
            page=((TABLE_SLOTS, WS, WS), BF),
            buf=((2, n_plane, n_vol, slab, C), BF),
            grads=((2, BLOCK_ROWS, C), F32),
            work=((2, n_plane, n_vol, slab, C), F32),
            wire=((n_plane, n_vol, slab, C), BF),
            from_core=((2, n_plane, n_vol // 2, slab, C), F32),
            from_plane=((2, n_plane - 1, n_vol // 2, slab, C), BF),
            from_vol=((n_vol - 1, slab, C), BF),
            x_stage=stage,
            d_stage=stage,
            x_got=landing,
            d_got=landing,
        ),
        dict(
            x_sent=(2, 8),
            x_arrived=(steps, 8),
            d_sent=(2, 8),
            d_arrived=(steps, 8),
            g_sent=(n_peers,),
            g_arrived=(n_peers,),
            turned=(TABLE_SLOTS,),
            r_sent=(2 * n_plane + n_vol - 1,),
            r_arrived=(2 * n_plane + n_vol - 1,),
        ),
        collective_id=1,
        lag=2,
    )
    shard_grad = lax.dynamic_slice(layers.total.reshape(-1), (offset,), (shard_len,))
    position = (device * shard_len + jnp.arange(shard_len, dtype=jnp.int32)) % (BLOCK_ROWS * C)
    is_vector = position >= 12 * C * C
    step_rate = jnp.where(is_vector, RATE_VECTOR, RATE_MATRIX)
    weight_decay = jnp.where(is_vector, 0.0, DECAY_MATRIX)
    moment_one = BETA_FIRST * first_moment + (1.0 - BETA_FIRST) * shard_grad
    moment_two = BETA_SECOND * second_moment + (1.0 - BETA_SECOND) * shard_grad * shard_grad
    corrected_one = moment_one / (1.0 - BETA_FIRST**STEP)
    corrected_two = moment_two / (1.0 - BETA_SECOND**STEP)
    normalized = corrected_one / (jnp.sqrt(corrected_two) + ADAM_EPS)
    new_master = master - step_rate * (normalized + weight_decay * master)
    return (
        layers.output.transpose(0, 1, 3, 2),
        layers.input_grad.transpose(0, 1, 3, 2),
        new_master,
        moment_one,
        moment_two,
        new_master.astype(BF),
    )


def solution(mesh):
    placed = (
        P(None, (VOL, WIN), None, None),
        P(None, (VOL, WIN), None, None),
        P(),
        P(None, (VOL, WIN)),
        P(None, (VOL, WIN), None),
        P((VOL, WIN)),
        P((VOL, WIN)),
        P((VOL, WIN)),
    )
    return jax.shard_map(
        on_device,
        mesh=mesh,
        in_specs=placed,
        out_specs=(
            P(None, (VOL, WIN), None, None),
            P(None, (VOL, WIN), None, None),
            P((VOL, WIN)),
            P((VOL, WIN)),
            P((VOL, WIN)),
            P((VOL, WIN)),
        ),
        check_vma=False,
    )
```

```python
from types import SimpleNamespace

import jax
import jax.numpy as jnp
import numpy as np
from jax import lax
from jax.experimental import pallas as pl
from jax.experimental.pallas import tpu as pltpu
from jax.sharding import PartitionSpec as P

C = 96
HEADS = 6
HEAD_DIM = 16
FF = 384
SIDE = 7
SHIFT = 3
WS = 343
STEP = 6
T = 384
WINDOWS = 2
CHUNK = 64
LAG = 150
TABLE_SLOTS = 3
ROWS = (352, T)
CA = 128
BLOCK_ROWS = 1164

NORM_EPS = 1e-05
MASK_FILL = -1000000000.0
BETA_FIRST = 0.5
BETA_SECOND = 0.5
ADAM_EPS = 1e-08
RATE_MATRIX = 0.1
RATE_VECTOR = 0.4
DECAY_MATRIX = 0.05

BF = jnp.bfloat16
F32 = jnp.float32
NN = (((1,), (0,)), ((), ()))
NT = (((1,), (1,)), ((), ()))
BY_STEP, WHOLE, SMEM, HBM = range(4)
MESH = pl.DeviceIdType.MESH
VOL, WIN = "vol", "win"
KEPT_NAMES = ("a0", "a1"), ("b0", "b1")


def octant_bits(octant):
    return (octant >> 2 & 1, octant >> 1 & 1, octant & 1)


OCT_SIZE = []
OCT_LEN = []
OCT_OFF = []
for _octant in range(8):
    _size = 1
    for _bit in octant_bits(_octant):
        _size *= SHIFT if _bit else SIDE - SHIFT
    OCT_OFF.append(sum(OCT_LEN))
    OCT_SIZE.append(_size)
    OCT_LEN.append(-(-_size // 16) * 16)


def slot_tables():
    perm = np.zeros((T, T), np.float32)
    order = np.zeros((T, WS), np.float32)
    places = np.full((8, T), 99, np.int32)
    for octant in range(8):
        bits = octant_bits(octant)
        lens = [SHIFT if bit else SIDE - SHIFT for bit in bits]
        for i in range(lens[0]):
            for j in range(lens[1]):
                for k in range(lens[2]):
                    source = [v if bit else v + SHIFT for v, bit in zip((i, j, k), bits)]
                    own = [v + bit * (SIDE - SHIFT) for v, bit in zip((i, j, k), bits)]
                    q = OCT_OFF[octant] + (i * lens[1] + j) * lens[2] + k
                    t = (source[0] * SIDE + source[1]) * SIDE + source[2]
                    perm[q, t] = 1
                    order[q, (own[0] * SIDE + own[1]) * SIDE + own[2]] = 1
                    places[:3, t] = source
    return perm, order, places


PERM, ORDER, PLACES = slot_tables()


def dot(a, b, dims=NN):
    return lax.dot_general(a, b, dims, preferred_element_type=F32)


def wide(column):
    return jnp.concatenate([column] * (T // 128), axis=1)


def ln_stats(x):
    centred = x - jnp.mean(x, axis=0, keepdims=True)
    scale = lax.rsqrt(jnp.mean(centred * centred, axis=0, keepdims=True) + NORM_EPS)
    return centred * scale, scale


def norm_back(e, z, scale, gain):
    eg = e * gain
    return scale * (
        eg - jnp.mean(eg, axis=0, keepdims=True) - z * jnp.mean(eg * z, axis=0, keepdims=True)
    )


def gelu_pair(h):
    base = 1.0 + (0.3275911 * 0.7071067811865476) * jnp.abs(h)
    t = pl.reciprocal(base, approx=True)
    t = t * (2.0 - base * t)
    poly = t * (
        0.5 * 0.254829592
        + t
        * (
            0.5 * -0.284496736
            + t * (0.5 * 1.421413741 + t * (0.5 * -1.453152027 + t * (0.5 * 1.061405429)))
        )
    )
    bell = jnp.exp(-0.5 * (h * h))
    tail = poly * bell
    phi = jnp.where(h < 0.0, tail, 1.0 - tail)
    return h * phi, phi + h * bell * 0.3989422804014327


def ones_row(shape, row=0):
    return jnp.where(lax.broadcasted_iota(jnp.int32, shape, 0) == row, 1.0, 0.0)


def weave(tasks, lag):
    clocks = [lag * n for n in range(len(tasks))]
    while tasks:
        n = clocks.index(min(clocks))
        cost = next(tasks[n], None)
        if cost is None:
            tasks, clocks = (x[:n] + x[n + 1 :] for x in (tasks, clocks))
        else:
            clocks[n] += cost


def clear_scratch(r):
    zeros = jnp.zeros((CA, HEADS * T), BF)
    for i in range(WINDOWS):
        r.qb[i] = zeros
        r.dab[i] = zeros
        r.rb[i] = jnp.zeros((2, 2 * C, 2 * T), BF)
        r.pad[i] = jnp.zeros((C, T), BF)
        r.cot[i] = jnp.zeros((C, T), BF)
        for h in range(HEADS):
            r.vt[i, h, 16:32, :] = ones_row((16, T)).astype(BF)
    for name, (shape, dtype) in GRADS.items():
        getattr(r, name)[...] = jnp.zeros((2,) + shape, dtype)


def table_copy(r, n):
    slot = n % TABLE_SLOTS
    return pltpu.make_async_copy(
        r.table.at[n // HEADS, n % HEADS], r.page.at[slot], r.turned.at[slot]
    )


def turn_tables(r, layer):
    for n in range(HEADS * layer, HEADS * layer + HEADS):
        table_copy(r, n).wait()
        half = dot(r.order[layer], r.page[n % TABLE_SLOTS], NT).astype(BF)
        if n + TABLE_SLOTS < 2 * HEADS:
            table_copy(r, n + TABLE_SLOTS).start()
        r.bias[layer, n % HEADS] = dot(half, r.order[layer], NT)


def set_queries(sc, queries):
    for h in range(HEADS):
        sc.qb[16 * h : 16 * h + 16, T * h : T * h + T] = queries[16 * h : 16 * h + 16, :]


def forward_attention(sc, w, st, code_row):
    z, _ = ln_stats(st.x)
    sc.n1aug[C:CA, :] = ones_row((CA - C, T)).astype(BF)
    sc.attaug[C:CA, :] = ones_row((CA - C, T)).astype(BF)
    sc.n1aug[0:C, :] = (z * wide(w.vec[0]) + wide(w.vec[1])).astype(BF)
    yield 150
    kv = dot(sc.n1aug[...].T, w.kv[...]).astype(BF)
    sc.kn[...] = kv[:, 0:CA]
    sc.vn[...] = kv[:, CA:]
    yield 200
    qkv = dot(w.qkvT[...], sc.n1aug[...])
    queries = qkv[0:C].astype(BF)
    set_queries(sc, queries)
    sc.qT[...] = queries
    sc.kT[...] = qkv[C : 2 * C].astype(BF)
    values = qkv[2 * C :].astype(BF)
    for h in range(HEADS):
        sc.vt[h, 0:16, :] = values[16 * h : 16 * h + 16, :]
    yield 150
    eye = lax.broadcasted_iota(jnp.int32, (128, 128), 0) == lax.broadcasted_iota(
        jnp.int32, (128, 128), 1
    )
    tops = [None] * HEADS

    def scores(h, c):
        rows = slice(CHUNK * c, min(CHUNK * c + CHUNK, sc.rows))
        count = rows.stop - rows.start
        x_all = dot(sc.kn[rows], sc.qb[:, T * h : T * h + T])
        codes = sc.codes[rows]
        parts = []
        for j in range(3):
            lanes = slice(128 * j, 128 * j + 128)
            allowed = codes == code_row[:, lanes]
            if j == rows.start // 128:
                allowed = allowed | eye[rows.start % 128 : rows.start % 128 + count]
            part = jnp.where(allowed, x_all[:, lanes] + sc.bias[h, rows, lanes], MASK_FILL)
            sc.s[rows, lanes] = part
            parts.append(jnp.max(part.reshape(count // 8, 8, 128), axis=0))
        top = jnp.concatenate(parts, axis=1)
        tops[h] = top if tops[h] is None else jnp.maximum(tops[h], top)

    def raise_(h, c):
        rows = slice(CHUNK * c, min(CHUNK * c + CHUNK, sc.rows))
        sc.e[rows, T * h : T * h + T] = jnp.exp(sc.s[rows] - tops[h]).astype(BF)

    def attend(h):
        out = dot(sc.vt[h, :, 0 : sc.rows], sc.e[:, T * h : T * h + T])
        inverse = 1.0 / out[16:17]
        part = out[0:16] * inverse
        sc.att[16 * h : 16 * h + 16, :] = part
        sc.inv[h : h + 1, :] = inverse
        sc.attaug[16 * h : 16 * h + 16, :] = part.astype(BF)

    for h in range(HEADS + 2):
        for c in range(T // CHUNK):
            if 0 <= h - 1 < HEADS:
                raise_(h - 1, c)
            if h < HEADS:
                scores(h, c)
            if c == 0 and 0 <= h - 2 < HEADS:
                attend(h - 2)
            yield 35
        if h < HEADS:
            tops[h] = jnp.max(tops[h], axis=0, keepdims=True)
    st.branch = dot(w.projT[...], sc.attaug[...])
    yield 100


def backward_attention(sc, w, st, z, scale, shifted):
    d_mid = st.d
    db = d_mid.astype(BF)
    d_att = dot(w.proj[...], db).astype(BF).astype(F32)
    sc.gproj[...] += dot(sc.attaug[...], db, NT)
    yield 150
    row = lax.broadcasted_iota(jnp.int32, (16, T), 0)
    for h in range(HEADS):
        part = (d_att[16 * h : 16 * h + 16] * sc.inv[h : h + 1, :]).astype(BF)
        cols = slice(T * h, T * h + T)
        sc.dab[16 * h : 16 * h + 16, cols] = part
        inner = -jnp.sum(
            part.astype(F32) * sc.att[16 * h : 16 * h + 16, :], axis=0, keepdims=True
        )
        high = inner.astype(BF).astype(F32)
        low = inner - high
        sc.dab[C : C + 16, cols] = jnp.where(
            row == 0, high, jnp.where(row == 1, low, 0.0)
        ).astype(BF)
    yield 100
    total = None
    none = jnp.zeros((16, T), BF)

    def soft(h):
        cols = slice(T * h, T * h + T)
        pull = dot(sc.vn[0 : sc.rows], sc.dab[:, cols])
        sc.ds[h % 2, 0 : sc.rows] = (pull * sc.e[:, cols].astype(F32)).astype(BF)

    def place_rows(h):
        rb = sc.rb.at[h % 2]
        last = (h - 2) % HEADS
        rb[16 * last : 16 * last + 16, T:] = none
        rb[C + 16 * last : C + 16 * last + 16, 0:T] = none
        rb[16 * h : 16 * h + 16, T:] = sc.qT[16 * h : 16 * h + 16, :]
        rb[C + 16 * h : C + 16 * h + 16, 0:T] = sc.dab[
            16 * h : 16 * h + 16, T * h : T * h + T
        ]

    def to_queries(h):
        sc.dq[16 * h : 16 * h + 16, :] = dot(
            sc.kT[16 * h : 16 * h + 16, 0 : sc.rows], sc.ds[h % 2, 0 : sc.rows]
        ).astype(BF)

    for h in range(HEADS + 1):
        if h < HEADS:
            place_rows(h)
            soft(h)
            yield 120
        if h > 0:
            to_queries(h - 1)
            yield 60
            both = jnp.concatenate(
                [sc.e[:, T * (h - 1) : T * h], sc.ds[(h - 1) % 2, 0 : sc.rows]], axis=1
            )
            term = dot(both, sc.rb[(h - 1) % 2], NT)
            total = term if total is None else total + term
            yield 180
    dkv = total.astype(BF)
    if sc.rows < T:
        dkv = jnp.concatenate([dkv, jnp.zeros((T - sc.rows, 2 * C), BF)], axis=0)
    dq = sc.dq[...]
    dn = dot(w.q[...], dq) + dot(w.kv96[...], dkv, NT)
    yield 120
    sc.gkv[...] += dot(sc.n1aug[...], dkv)
    sc.gq[...] += dot(dq, sc.n1aug[...], NT)
    yield 150
    if shifted:
        dn = dn.astype(BF).astype(F32)
    sc.gvec[0] += dn * z
    sc.gvec[1] += dn
    st.d = d_mid + norm_back(dn, z, scale, wide(w.vec[0]))
    yield 150


def feed_forward_back(sc, w, st, dd, z, scale):
    dn = dot(w.up[...], sc.dh[...])
    yield 120
    sc.gdown[...] += dot(sc.act[...], dd, NT)
    yield 120
    sc.gup[...] += dot(sc.dh[...], sc.n2aug[...], NT)
    yield 120
    sc.gvec[4] += dd.astype(F32)
    sc.gvec[2] += dn * z
    sc.gvec[3] += dn
    st.d = st.d + norm_back(dn, z, scale, wide(w.vec[2]))
    yield 150


def write_grads(sc, out):
    gq = sc.gq[...].T
    gkv = sc.gkv[...]
    gup = sc.gup[...].T
    out[pl.ds(0, C, 3), :] = gq[0:C]
    out[pl.ds(1, C, 3), :] = gkv[0:C, 0:C]
    out[pl.ds(2, C, 3), :] = gkv[0:C, C : 2 * C]
    out[3 * C : 4 * C, :] = sc.gproj[0:C, :]
    for j in range(4):
        out[pl.ds(4 * C + j, C, 4), :] = gup[0:C, C * j : C * j + C]
    out[8 * C : 12 * C, :] = sc.gdown[...]
    sums = [jnp.sum(sc.gvec[n].T, axis=0, keepdims=True) for n in range(5)]
    rows = [
        sums[0],
        sums[1],
        gq[C : C + 1],
        gkv[C : C + 1, C : 2 * C],
        sc.gproj[C : C + 1, :],
        sums[2],
        sums[3],
        sums[4],
    ] + [gup[C : C + 1, C * j : C * j + C] for j in range(4)]
    for n, value in enumerate(rows):
        out[12 * C + n : 12 * C + n + 1, :] = value


FWD = dict(
    qb=((CA, HEADS * T), BF),
    vt=((HEADS, 32, T), BF),
    kn=((T, CA), BF),
    codes=((T, 128), F32),
    s=((T, T), F32),
)
BIAS = dict(bias=((HEADS, T, T), F32))
KEPT = dict(
    qT=((C, T), BF),
    kT=((C, T), BF),
    vn=((T, CA), BF),
    e=((T, HEADS * T), BF),
    att=((C, T), F32),
    inv=((8, T), F32),
    attaug=((CA, T), BF),
    n1aug=((CA, T), BF),
    n2aug=((CA, T), BF),
    act=((FF, T), BF),
    gp=((FF, T), BF),
    xT=((C, T), BF),
    x1=((C, T), F32),
)
GRADS = dict(
    gq=((C, CA), F32),
    gkv=((CA, 2 * C), F32),
    gproj=((CA, C), F32),
    gup=((FF, CA), F32),
    gdown=((FF, C), F32),
    gvec=((5, C, T), F32),
)
BWD = dict(
    dab=((CA, HEADS * T), BF),
    rb=((2, 2 * C, 2 * T), BF),
    ds=((2, T, T), BF),
    dq=((C, T), BF),
    dh=((FF, T), BF),
)


PADS = dict(pad=((C, T), BF), cot=((C, T), BF))
WEIGHTS = dict(
    qkvT=((3 * C, CA), BF),
    kv=((CA, 2 * CA), BF),
    projT=((C, CA), BF),
    proj=((C, C), BF),
    upT=((FF, CA), BF),
    up=((C, FF), BF),
    downT=((C, FF), BF),
    down=((FF, C), BF),
    q=((C, C), BF),
    kv96=((C, 2 * C), BF),
    vec=((5, C, 128), F32),
)


def of_layer(r, layer, slot):
    shared = {n: getattr(r, n).at[layer] for n in (*WEIGHTS, *GRADS, *BIAS)}
    return [
        SimpleNamespace(
            rows=ROWS[layer],
            **shared,
            **{n: getattr(r, n).at[i] for n in (*FWD, *BWD, *PADS)},
            **{n: getattr(r, KEPT_NAMES[layer][i] + n).at[slot] for n in KEPT},
        )
        for i in range(WINDOWS)
    ]


def second_norm(sc, w, x):
    z, scale = ln_stats(x)
    sc.n2aug[C:CA, :] = ones_row((CA - C, T)).astype(BF)
    sc.n2aug[0:C, :] = (z * wide(w.vec[2]) + wide(w.vec[3])).astype(BF)
    return z, scale


def grid_place(groups_a):
    win = lax.axis_index(WIN)
    return (win // 4, win // 2 % 2, win % 2), (groups_a, 2, 2)


def neighbour(octant, sign, groups_a):
    place, sizes = grid_place(groups_a)
    a, b, c = (
        (p + sign * bit + n) % n for p, bit, n in zip(place, octant_bits(octant), sizes)
    )
    return lax.axis_index(VOL), (a * 2 + b) * 2 + c


def greet(peers):
    barrier = pltpu.get_barrier_semaphore()
    for peer in peers:
        pl.semaphore_signal(barrier, inc=1, device_id=peer, device_id_type=MESH)


def await_greetings(peers):
    pl.semaphore_wait(pltpu.get_barrier_semaphore(), len(peers))


def block_copy(way, m, octant, groups_a):
    rows = pl.ds(OCT_OFF[octant], OCT_LEN[octant])
    slot = m % 2
    source = way.stage.at[slot, :, rows]
    target = way.got.at[pl.ds(m * WINDOWS, WINDOWS), rows]
    if octant == 0:
        return pltpu.make_async_copy(source, target, way.arrived.at[m, 0])
    return pltpu.make_async_remote_copy(
        src_ref=source,
        dst_ref=target,
        send_sem=way.sent.at[slot, octant],
        recv_sem=way.arrived.at[m, octant],
        device_id=neighbour(octant, way.sign, groups_a),
        device_id_type=MESH,
    )


def send_blocks(way, m, groups_a):
    for octant in range(8):
        block_copy(way, m, octant, groups_a).start()


def wait_sent(way, m, groups_a):
    for octant in range(1, 8):
        block_copy(way, m, octant, groups_a).wait_send()


def wait_arrived(way, m, groups_a):
    block_copy(way, m, 0, groups_a).wait()
    for octant in range(1, 8):
        block_copy(way, m, octant, groups_a).wait_recv()


def first_forward(r, sc, m, i):
    w, st = sc, SimpleNamespace()
    stage = r.x_stage.at[m % 2, i]
    sc.pad[:, 0:WS] = r.tokens[i, 0]
    st.x = sc.pad[...].astype(F32)
    sc.xT[...] = sc.pad[...]
    places = r.places
    valid = (
        (places[0:1, :] < r.extent[0, 0, m * WINDOWS + i])
        & (places[1:2, :] < r.extent[1, 0, m * WINDOWS + i])
        & (places[2:3, :] < r.extent[2, 0, m * WINDOWS + i])
    )
    valid = jnp.where(valid, 1.0, 0.0)
    sc.codes[...] = jnp.broadcast_to(valid - 1.0, (128, T)).T
    yield 100
    yield from forward_attention(sc, w, st, jnp.zeros((1, T), F32))
    sc.cot[:, 0:WS] = r.cotangent[i, 0]
    stage[:, CA:] = jnp.concatenate(
        [dot(r.perm[...], sc.cot[...], NT), jnp.zeros((T, CA - C), F32)], axis=1
    ).astype(BF)
    yield 100
    x = st.x + st.branch
    sc.x1[...] = x
    second_norm(sc, w, x)
    yield 150
    for c in range(6):
        rows = slice(64 * c, 64 * c + 64)
        active, slope = gelu_pair(dot(w.upT[rows], sc.n2aug[...]))
        sc.act[rows, :] = active.astype(BF)
        sc.gp[rows, :] = slope.astype(BF)
        yield 100
    x = x + (dot(w.downT[...], sc.act[...]) + wide(w.vec[4]))
    yield 100
    row = lax.broadcasted_iota(jnp.int32, (CA - C, T), 0)
    label = r.volume[0, m * WINDOWS + i].astype(F32)
    extra = jnp.where(row == 0, label, jnp.where(row == 1, valid, 0.0))
    x = jnp.concatenate([x, extra], axis=0).astype(BF)
    stage[:, 0:CA] = dot(r.perm[...], x, NT).astype(BF)
    yield 100


def second_layer(r, sc, m, i, groups_a):
    w, st = sc, SimpleNamespace()
    stage = r.d_stage.at[m % 2, i]
    n = m * WINDOWS + i
    came = r.x_got[n, :, 0:CA]
    x = came.T.astype(F32)
    place, sizes = grid_place(groups_a)
    code_row = []
    for octant in range(8):
        rows = slice(OCT_OFF[octant], OCT_OFF[octant] + OCT_LEN[octant])
        wraps = [
            bit * jnp.where(p == n_ - 1, 1, 0)
            for p, bit, n_ in zip(place, octant_bits(octant), sizes)
        ]
        wrap = (wraps[0] * 4 + wraps[1] * 2 + wraps[2]).astype(F32)
        columns = came[rows].astype(F32)
        code = jnp.where(columns[:, C + 1 : C + 2] > 0.0, columns[:, C : C + 1] * 8.0 + wrap, -1.0)
        sc.codes[rows, :] = jnp.broadcast_to(code, (OCT_LEN[octant], 128))
        code_row.append(jnp.full((1, OCT_LEN[octant]), wrap))
    code_row = jnp.concatenate(code_row, axis=1) + 8.0 * x[C : C + 1]
    keep = x[C + 1 : C + 2]
    x = x[0:C]
    sc.xT[...] = x.astype(BF)
    st.x = x
    yield 150
    yield from forward_attention(sc, w, st, code_row)
    st.d = r.x_got[n, :, CA:].T[0:C].astype(F32) * keep
    dd = st.d.astype(BF)
    x = sc.xT[...].astype(F32) + st.branch.astype(BF).astype(F32)
    z, scale = second_norm(sc, w, x)
    yield 200
    for c in range(6):
        rows = slice(64 * c, 64 * c + 64)
        active, slope = gelu_pair(dot(w.upT[rows], sc.n2aug[...]))
        sc.act[rows, :] = active.astype(BF)
        sc.dh[rows, :] = (dot(w.down[rows], dd) * slope).astype(BF)
        yield 120
    x = x + (dot(w.downT[...], sc.act[...]) + wide(w.vec[4]))
    none = jnp.zeros((CA - C, T), F32)
    stage[:, 0:CA] = jnp.concatenate([x * keep, none], axis=0).T.astype(BF)
    yield 150
    yield from feed_forward_back(sc, w, st, dd, z, scale)
    z, scale = ln_stats(sc.xT[...].astype(F32))
    yield from backward_attention(sc, w, st, z, scale, True)
    stage[:, CA:] = jnp.concatenate([st.d, none], axis=0).T.astype(BF)
    yield 100


def first_backward(r, sc, m, i):
    w, st = sc, SimpleNamespace()
    came = r.d_got[m * WINDOWS + i].T
    came = jnp.concatenate([came[0:C], came[CA : CA + C]], axis=0)
    yield 200
    came = dot(came, r.perm[...])
    r.output[i, 0] = came[0:C, 0:WS].astype(BF)
    st.d = came[C : 2 * C]
    dd = st.d.astype(BF)
    z, scale = ln_stats(sc.x1[...])
    yield 200
    for c in range(3):
        rows = slice(128 * c, 128 * c + 128)
        sc.dh[rows, :] = (dot(w.down[rows], dd) * sc.gp[rows, :].astype(F32)).astype(BF)
        yield 50
    yield from feed_forward_back(sc, w, st, dd, z, scale)
    z, scale = ln_stats(sc.xT[...].astype(F32))
    yield from backward_attention(sc, w, st, z, scale, False)
    r.input_grad[i, 0] = st.d[:, 0:WS]
    yield 50


def layers_kernel(n_vol, n_plane, shard_len, steps, r):
    groups_a = n_plane // 2
    s = pl.program_id(0)
    forth = SimpleNamespace(
        stage=r.x_stage, got=r.x_got, sent=r.x_sent, arrived=r.x_arrived, sign=-1
    )
    back = SimpleNamespace(
        stage=r.d_stage, got=r.d_got, sent=r.d_sent, arrived=r.d_arrived, sign=1
    )

    far = all_peers(n_vol, n_plane)
    reduction = Reduction(r, far, n_vol, n_plane, shard_len)

    @pl.when(s == 0)
    def _():
        peers = far + [
            neighbour(octant, sign, groups_a) for sign in (1, -1) for octant in range(1, 8)
        ]
        greet(peers)
        for n in range(TABLE_SLOTS):
            table_copy(r, n).start()
        vol, plane, core = own_place()
        r.buf[core, plane, vol] = r.shard[...]
        clear_scratch(r)
        await_greetings(peers)
        meanwhile = (lambda: None, lambda: turn_tables(r, 0), lambda: turn_tables(r, 1))
        for copies, work in zip(gather_stages(r, far, n_vol, n_plane), meanwhile):
            for c in copies:
                c.start()
            work()
            for c in copies:
                c.wait()
        prepare(r, n_vol, n_plane, shard_len)

    @pl.when(s < steps)
    def _():
        @pl.when(s >= 2)
        def _():
            wait_sent(forth, s - 2, groups_a)

        windows = of_layer(r, 0, s % 3)
        weave([first_forward(r, sc, s, i) for i, sc in enumerate(windows)], LAG)
        send_blocks(forth, s, groups_a)

    @pl.when((s >= 1) & (s <= steps))
    def _():
        m = s - 1
        wait_arrived(forth, m, groups_a)

        @pl.when(m >= 2)
        def _():
            wait_sent(back, m - 2, groups_a)

        windows = of_layer(r, 1, 0)
        weave([second_layer(r, sc, m, i, groups_a) for i, sc in enumerate(windows)], LAG)
        send_blocks(back, m, groups_a)

    @pl.when(s == steps)
    def _():
        write_grads(of_layer(r, 1, 0)[0], r.grads.at[1])
        reduction.start_core(1)

    @pl.when(s == steps + 1)
    def _():
        reduction.start_plane(1)

    @pl.when(s >= 2)
    def _():
        m = s - 2
        wait_arrived(back, m, groups_a)
        windows = of_layer(r, 0, m % 3)
        weave([first_backward(r, sc, m, i) for i, sc in enumerate(windows)], LAG)

    @pl.when(s == steps + 1)
    def _():
        write_grads(of_layer(r, 0, 0)[0], r.grads.at[0])
        reduction.start_core(0)
        reduction.end_plane(1)
        reduction.start_plane(0)
        for m in range(max(steps - 2, 0), steps):
            wait_sent(forth, m, groups_a)
            wait_sent(back, m, groups_a)
        reduction.end_plane(0)
        reduction.finish()


def shard_rows(device, shard_len):
    return device * shard_len // C, -(-(device + 1) * shard_len // C)


def flat_offset(device, shard_len):
    return device * shard_len % C


def slab_rows(shard_len):
    return -(-((shard_len + C - 2) // C + 1) // 16) * 16


def own_place():
    win = lax.axis_index(WIN)
    return lax.axis_index(VOL), win // 2, win % 2


def all_peers(n_vol, n_plane):
    vol, plane, core = own_place()
    return (
        [((vol + j) % n_vol, plane * 2 + core) for j in range(1, n_vol)]
        + [(vol, (plane + j) % n_plane * 2 + core) for j in range(1, n_plane)]
        + [(vol, plane * 2 + 1 - core)]
    )


def transpose_with(matrix, extra):
    below = jnp.where(lax.broadcasted_iota(jnp.int32, (CA - C, C), 0) == 0, extra, 0.0)
    return jnp.concatenate([matrix, below], axis=0).T


def gather_stages(r, peers, n_vol, n_plane):
    vol, plane, core = own_place()

    def copy(ref, n):
        return pltpu.make_async_remote_copy(
            src_ref=ref,
            dst_ref=ref,
            send_sem=r.g_sent.at[n],
            recv_sem=r.g_arrived.at[n],
            device_id=peers[n],
            device_id_type=MESH,
        )

    return (
        [copy(r.buf.at[core, plane, vol], n) for n in range(n_vol - 1)],
        [copy(r.buf.at[core, plane], n_vol - 1 + n) for n in range(n_plane - 1)],
        [copy(r.buf.at[core], n_vol + n_plane - 2)],
    )


def prepare(r, n_vol, n_plane, shard_len):
    buf = r.buf
    flat = r.grads
    flat[...] = jnp.zeros(flat.shape, F32)
    half = n_vol * n_plane
    for v in range(n_vol):
        for p in range(n_plane):
            for c in range(2):
                device = (v * n_plane + p) * 2 + c
                start, stop = shard_rows(device % half, shard_len)
                flat[device // half, start:stop, :] += buf[c, p, v, 0 : stop - start].astype(F32)
    for layer in range(2):

        def rows(start, count=C, stride=1):
            return flat[layer, pl.ds(start, count, stride), :]

        def vector(n):
            return rows(12 * C + n, 1)

        o = SimpleNamespace(**{n: getattr(r, n).at[layer] for n in WEIGHTS})
        none = jnp.zeros((1, C), F32)
        wq, wk, wv = (rows(n, C, 3) for n in range(3))
        o.q[...] = wq.astype(BF)
        o.kv96[...] = jnp.concatenate([wk, wv], axis=1).astype(BF)
        o.qkvT[0:C, :] = (transpose_with(wq, vector(2)) * 0.25).astype(BF)
        o.qkvT[C : 2 * C, :] = (transpose_with(wk, none) * 0.25).astype(BF)
        o.qkvT[2 * C :, :] = transpose_with(wv, vector(3)).astype(BF)
        row = lax.broadcasted_iota(jnp.int32, (CA - C, CA), 0)
        lane = lax.broadcasted_iota(jnp.int32, (CA - C, CA), 1)
        blank = jnp.zeros((C, CA - C), F32)
        bias_v = jnp.concatenate([vector(3), blank[0:1]], axis=1)
        ones = jnp.where((lane == C) | (lane == C + 1), 1.0, bias_v)
        o.kv[0:C, :] = jnp.concatenate([wk, blank, wv, blank], axis=1).astype(BF)
        o.kv[C:, 0:CA] = jnp.zeros((CA - C, CA), BF)
        o.kv[C:, CA:] = jnp.where(row == 0, ones, 0.0).astype(BF)
        proj = rows(3 * C)
        o.proj[...] = proj.astype(BF)
        o.projT[...] = transpose_with(proj, vector(4)).astype(BF)
        ups = [rows(4 * C + j, C, 4) for j in range(4)]
        o.up[...] = jnp.concatenate(ups, axis=1).astype(BF)
        for j in range(4):
            o.upT[C * j : C * j + C, :] = transpose_with(ups[j], vector(8 + j)).astype(BF)
        down = rows(8 * C, FF)
        o.down[...] = down.astype(BF)
        o.downT[...] = down.T.astype(BF)
        for n, source in enumerate((0, 1, 5, 6, 7)):
            o.vec[n] = jnp.broadcast_to(vector(source), (128, C)).T


class Reduction:
    def __init__(self, r, peers, n_vol, n_plane, shard_len):
        self.r, self.peers, self.shard_len = r, peers, shard_len
        self.n_vol, self.n_plane, self.half = n_vol, n_plane, n_vol // 2
        self.vol, self.plane, self.core = own_place()

    def vols(self, layer):
        return pl.ds(layer * self.half, self.half)

    def copy(self, source, target, peer, n):
        return pltpu.make_async_remote_copy(
            src_ref=source,
            dst_ref=target,
            send_sem=self.r.r_sent.at[n],
            recv_sem=self.r.r_arrived.at[n],
            device_id=self.peers[peer],
            device_id_type=MESH,
        )

    def over_core(self, layer):
        source = self.r.work.at[1 - self.core, :, self.vols(layer)]
        return [self.copy(source, self.r.from_core.at[layer], len(self.peers) - 1, layer)]

    def over_plane(self, layer):
        return [
            self.copy(
                self.r.wire.at[(self.plane + j) % self.n_plane, self.vols(layer)],
                self.r.from_plane.at[layer, j - 1],
                self.n_vol - 2 + j,
                2 + layer * (self.n_plane - 1) + j - 1,
            )
            for j in range(1, self.n_plane)
        ]

    def over_vol(self):
        return [
            self.copy(
                self.r.wire.at[self.plane, (self.vol + j) % self.n_vol],
                self.r.from_vol.at[j - 1],
                j - 1,
                2 * self.n_plane + j - 1,
            )
            for j in range(1, self.n_vol)
        ]

    def start_core(self, layer):
        for v in range(layer * self.half, (layer + 1) * self.half):
            for p in range(self.n_plane):
                for c in range(2):
                    device = (v % self.half * self.n_plane + p) * 2 + c
                    start, stop = shard_rows(device, self.shard_len)
                    self.r.work[c, p, v, 0 : stop - start] = self.r.grads[layer, start:stop, :]
        for c in self.over_core(layer):
            c.start()

    def start_plane(self, layer):
        for c in self.over_core(layer):
            c.wait()
        vols, work = self.vols(layer), self.r.work
        total = work[self.core, :, vols] + self.r.from_core[layer]
        work[self.core, :, vols] = total
        self.r.wire[:, vols] = total.astype(BF)
        for c in self.over_plane(layer):
            c.start()

    def end_plane(self, layer):
        for c in self.over_plane(layer):
            c.wait()
        vols, work = self.vols(layer), self.r.work
        total = work[self.core, self.plane, vols]
        for j in range(self.n_plane - 1):
            total = total + self.r.from_plane[layer, j].astype(F32)
        work[self.core, self.plane, vols] = total
        self.r.wire[self.plane, vols] = total.astype(BF)

    def finish(self):
        for c in self.over_vol():
            c.start()
        for c in self.over_vol():
            c.wait()
        total = self.r.work[self.core, self.plane, self.vol]
        for j in range(self.n_vol - 1):
            total = total + self.r.from_vol[j].astype(F32)
        self.r.total[...] = total


def call(kernel, steps, ins, outs, scratch, semaphores=(), collective_id=None, lag=0):
    def spec(shape, kind, late):
        if kind in (SMEM, HBM):
            return pl.BlockSpec(memory_space=pltpu.SMEM if kind is SMEM else pl.ANY)
        zeros = (0,) * (len(shape) - 1)
        if kind is BY_STEP:

            def index(s):
                return (jnp.clip(s - late, 0, steps - 1),) + zeros

            return pl.BlockSpec((shape[0] // steps,) + tuple(shape[1:]), index)
        return pl.BlockSpec(
            tuple(shape), lambda s: (0,) + zeros, pipeline_mode=None if late else pl.Buffered(1)
        )

    semaphores = dict(semaphores)
    names = tuple(ins) + tuple(outs) + tuple(scratch) + tuple(semaphores)

    def body(*refs):
        kernel(SimpleNamespace(**dict(zip(names, refs))))

    results = pl.pallas_call(
        body,
        grid=(steps + lag,),
        in_specs=[spec(a.shape, kind, 0) for a, kind in ins.values()],
        out_specs=[spec(shape, kind, lag) for shape, _, kind in outs.values()],
        out_shape=[jax.ShapeDtypeStruct(shape, dtype) for shape, dtype, _ in outs.values()],
        scratch_shapes=[pltpu.VMEM(shape, dtype) for shape, dtype in scratch.values()]
        + [pltpu.SemaphoreType.DMA(shape) for shape in semaphores.values()],
        compiler_params=pltpu.CompilerParams(
            vmem_limit_bytes=62 * 2**20,
            collective_id=collective_id,
            has_side_effects=collective_id is not None,
        ),
    )(*[a for a, _ in ins.values()])
    return SimpleNamespace(**dict(zip(outs, results)))


def on_device(
    tokens,
    cotangent,
    position_bias,
    window_volume,
    clip_extent,
    master,
    first_moment,
    second_moment,
):
    n_vol, n_win = lax.axis_size(VOL), lax.axis_size(WIN)
    n_plane = n_win // 2
    count = tokens.shape[0]
    steps = count // WINDOWS
    shard_len = master.shape[0]
    device = lax.axis_index((VOL, WIN))
    slab = slab_rows(shard_len)
    offset = flat_offset(device, shard_len)
    shard = lax.dynamic_update_slice(jnp.zeros((slab * C,), BF), master.astype(BF), (offset,))
    n_peers = n_vol + n_plane - 1

    def each(table, *sizes):
        return {n: (sizes + shape, dtype) for n, (shape, dtype) in table.items()}

    def kept(layer, slots):
        shapes = dict(KEPT, e=((ROWS[layer], HEADS * T), BF))
        shapes = dict(shapes, gp=((16, T), BF)) if layer else shapes
        return {name + n: v for name in KEPT_NAMES[layer] for n, v in each(shapes, slots).items()}

    stage, landing = ((2, WINDOWS, T, 2 * CA), BF), ((count, T, 2 * CA), BF)
    layers = call(
        lambda r: layers_kernel(n_vol, n_plane, shard_len, steps, r),
        steps,
        dict(
            tokens=(tokens.transpose(0, 1, 3, 2), BY_STEP),
            cotangent=(cotangent.transpose(0, 1, 3, 2), BY_STEP),
            volume=(window_volume.T, SMEM),
            extent=(clip_extent.transpose(2, 1, 0), SMEM),
            perm=(jnp.asarray(PERM, BF), WHOLE),
            places=(jnp.asarray(PLACES), WHOLE),
            order=(jnp.asarray(np.stack([np.eye(T, WS), ORDER]), BF), WHOLE),
            table=(position_bias, HBM),
            shard=(shard.reshape(slab, C), WHOLE),
        ),
        dict(
            output=((count, 1, C, WS), BF, BY_STEP),
            input_grad=((count, 1, C, WS), F32, BY_STEP),
            total=((slab, C), F32, WHOLE),
        ),
        dict(
            **each(FWD, WINDOWS),
            **each(BWD, WINDOWS),
            **each(PADS, WINDOWS),
            **each(GRADS, 2),
            **each(BIAS, 2),
            **kept(0, 3),
            **kept(1, 1),
            **each(WEIGHTS, 2),
            page=((TABLE_SLOTS, WS, WS), BF),
            buf=((2, n_plane, n_vol, slab, C), BF),
            grads=((2, BLOCK_ROWS, C), F32),
            work=((2, n_plane, n_vol, slab, C), F32),
            wire=((n_plane, n_vol, slab, C), BF),
            from_core=((2, n_plane, n_vol // 2, slab, C), F32),
            from_plane=((2, n_plane - 1, n_vol // 2, slab, C), BF),
            from_vol=((n_vol - 1, slab, C), BF),
            x_stage=stage,
            d_stage=stage,
            x_got=landing,
            d_got=landing,
        ),
        dict(
            x_sent=(2, 8),
            x_arrived=(steps, 8),
            d_sent=(2, 8),
            d_arrived=(steps, 8),
            g_sent=(n_peers,),
            g_arrived=(n_peers,),
            turned=(TABLE_SLOTS,),
            r_sent=(2 * n_plane + n_vol - 1,),
            r_arrived=(2 * n_plane + n_vol - 1,),
        ),
        collective_id=1,
        lag=2,
    )
    shard_grad = lax.dynamic_slice(layers.total.reshape(-1), (offset,), (shard_len,))
    position = (device * shard_len + jnp.arange(shard_len, dtype=jnp.int32)) % (BLOCK_ROWS * C)
    is_vector = position >= 12 * C * C
    step_rate = jnp.where(is_vector, RATE_VECTOR, RATE_MATRIX)
    weight_decay = jnp.where(is_vector, 0.0, DECAY_MATRIX)
    moment_one = BETA_FIRST * first_moment + (1.0 - BETA_FIRST) * shard_grad
    moment_two = BETA_SECOND * second_moment + (1.0 - BETA_SECOND) * shard_grad * shard_grad
    corrected_one = moment_one / (1.0 - BETA_FIRST**STEP)
    corrected_two = moment_two / (1.0 - BETA_SECOND**STEP)
    normalized = corrected_one / (jnp.sqrt(corrected_two) + ADAM_EPS)
    new_master = master - step_rate * (normalized + weight_decay * master)
    return (
        layers.output.transpose(0, 1, 3, 2),
        layers.input_grad.transpose(0, 1, 3, 2),
        new_master,
        moment_one,
        moment_two,
        new_master.astype(BF),
    )


def solution(mesh):
    placed = (
        P(None, (VOL, WIN), None, None),
        P(None, (VOL, WIN), None, None),
        P(),
        P(None, (VOL, WIN)),
        P(None, (VOL, WIN), None),
        P((VOL, WIN)),
        P((VOL, WIN)),
        P((VOL, WIN)),
    )
    return jax.shard_map(
        on_device,
        mesh=mesh,
        in_specs=placed,
        out_specs=(
            P(None, (VOL, WIN), None, None),
            P(None, (VOL, WIN), None, None),
            P((VOL, WIN)),
            P((VOL, WIN)),
            P((VOL, WIN)),
            P((VOL, WIN)),
        ),
        check_vma=False,
    )
```

```python
from types import SimpleNamespace

import jax
import jax.numpy as jnp
import numpy as np
from jax import lax
from jax.experimental import pallas as pl
from jax.experimental.pallas import tpu as pltpu
from jax.sharding import PartitionSpec as P

C = 96
HEADS = 6
HEAD_DIM = 16
FF = 384
SIDE = 7
SHIFT = 3
WS = 343
STEP = 6
T = 384
WINDOWS = 2
CHUNK = 64
LAG = 150
TABLE_SLOTS = 3
ROWS = (352, T)
CA = 128
BLOCK_ROWS = 1164

NORM_EPS = 1e-05
MASK_FILL = -1000000000.0
BETA_FIRST = 0.5
BETA_SECOND = 0.5
ADAM_EPS = 1e-08
RATE_MATRIX = 0.1
RATE_VECTOR = 0.4
DECAY_MATRIX = 0.05

BF = jnp.bfloat16
F32 = jnp.float32
NN = (((1,), (0,)), ((), ()))
NT = (((1,), (1,)), ((), ()))
BY_STEP, WHOLE, SMEM, HBM = range(4)
MESH = pl.DeviceIdType.MESH
VOL, WIN = "vol", "win"
KEPT_NAMES = ("a0", "a1"), ("b0", "b1")


def octant_bits(octant):
    return (octant >> 2 & 1, octant >> 1 & 1, octant & 1)


OCT_SIZE = []
OCT_LEN = []
OCT_OFF = []
for _octant in range(8):
    _size = 1
    for _bit in octant_bits(_octant):
        _size *= SHIFT if _bit else SIDE - SHIFT
    OCT_OFF.append(sum(OCT_LEN))
    OCT_SIZE.append(_size)
    OCT_LEN.append(-(-_size // 16) * 16)


def slot_tables():
    perm = np.zeros((T, T), np.float32)
    order = np.zeros((T, WS), np.float32)
    places = np.full((8, T), 99, np.int32)
    for octant in range(8):
        bits = octant_bits(octant)
        lens = [SHIFT if bit else SIDE - SHIFT for bit in bits]
        for i in range(lens[0]):
            for j in range(lens[1]):
                for k in range(lens[2]):
                    source = [v if bit else v + SHIFT for v, bit in zip((i, j, k), bits)]
                    own = [v + bit * (SIDE - SHIFT) for v, bit in zip((i, j, k), bits)]
                    q = OCT_OFF[octant] + (i * lens[1] + j) * lens[2] + k
                    t = (source[0] * SIDE + source[1]) * SIDE + source[2]
                    perm[q, t] = 1
                    order[q, (own[0] * SIDE + own[1]) * SIDE + own[2]] = 1
                    places[:3, t] = source
    return perm, order, places


PERM, ORDER, PLACES = slot_tables()


def dot(a, b, dims=NN):
    return lax.dot_general(a, b, dims, preferred_element_type=F32)


def wide(column):
    return jnp.concatenate([column] * (T // 128), axis=1)


def ln_stats(x):
    centred = x - jnp.mean(x, axis=0, keepdims=True)
    scale = lax.rsqrt(jnp.mean(centred * centred, axis=0, keepdims=True) + NORM_EPS)
    return centred * scale, scale


def norm_back(e, z, scale, gain):
    eg = e * gain
    return scale * (
        eg - jnp.mean(eg, axis=0, keepdims=True) - z * jnp.mean(eg * z, axis=0, keepdims=True)
    )


def gelu_pair(h):
    base = 1.0 + (0.3275911 * 0.7071067811865476) * jnp.abs(h)
    t = pl.reciprocal(base, approx=True)
    t = t * (2.0 - base * t)
    poly = t * (
        0.5 * 0.254829592
        + t
        * (
            0.5 * -0.284496736
            + t * (0.5 * 1.421413741 + t * (0.5 * -1.453152027 + t * (0.5 * 1.061405429)))
        )
    )
    bell = jnp.exp(-0.5 * (h * h))
    tail = poly * bell
    phi = jnp.where(h < 0.0, tail, 1.0 - tail)
    return h * phi, phi + h * bell * 0.3989422804014327


def ones_row(shape, row=0):
    return jnp.where(lax.broadcasted_iota(jnp.int32, shape, 0) == row, 1.0, 0.0)


def weave(tasks, lag):
    clocks = [lag * n for n in range(len(tasks))]
    while tasks:
        n = clocks.index(min(clocks))
        cost = next(tasks[n], None)
        if cost is None:
            tasks, clocks = (x[:n] + x[n + 1 :] for x in (tasks, clocks))
        else:
            clocks[n] += cost


def clear_scratch(r):
    zeros = jnp.zeros((CA, HEADS * T), BF)
    for i in range(WINDOWS):
        r.qb[i] = zeros
        r.dab[i] = zeros
        r.rb[i] = jnp.zeros((2, 2 * C, 2 * T), BF)
        r.pad[i] = jnp.zeros((C, T), BF)
        r.cot[i] = jnp.zeros((C, T), BF)
        for h in range(HEADS):
            r.vt[i, h, 16:32, :] = ones_row((16, T)).astype(BF)
    for name, (shape, dtype) in GRADS.items():
        getattr(r, name)[...] = jnp.zeros((2,) + shape, dtype)


def table_copy(r, n):
    slot = n % TABLE_SLOTS
    return pltpu.make_async_copy(
        r.table.at[n // HEADS, n % HEADS], r.page.at[slot], r.turned.at[slot]
    )


def turn_tables(r, layer):
    for n in range(HEADS * layer, HEADS * layer + HEADS):
        table_copy(r, n).wait()
        half = dot(r.order[layer], r.page[n % TABLE_SLOTS], NT).astype(BF)
        if n + TABLE_SLOTS < 2 * HEADS:
            table_copy(r, n + TABLE_SLOTS).start()
        r.bias[layer, n % HEADS] = dot(half, r.order[layer], NT)


def set_queries(sc, queries):
    for h in range(HEADS):
        sc.qb[16 * h : 16 * h + 16, T * h : T * h + T] = queries[16 * h : 16 * h + 16, :]


def forward_attention(sc, w, st, code_row):
    z, _ = ln_stats(st.x)
    sc.n1aug[C:CA, :] = ones_row((CA - C, T)).astype(BF)
    sc.attaug[C:CA, :] = ones_row((CA - C, T)).astype(BF)
    sc.n1aug[0:C, :] = (z * wide(w.vec[0]) + wide(w.vec[1])).astype(BF)
    yield 150
    kv = dot(sc.n1aug[...].T, w.kv[...]).astype(BF)
    sc.kn[...] = kv[:, 0:CA]
    sc.vn[...] = kv[:, CA:]
    yield 200
    qkv = dot(w.qkvT[...], sc.n1aug[...])
    queries = qkv[0:C].astype(BF)
    set_queries(sc, queries)
    sc.qT[...] = queries
    sc.kT[...] = qkv[C : 2 * C].astype(BF)
    values = qkv[2 * C :].astype(BF)
    for h in range(HEADS):
        sc.vt[h, 0:16, :] = values[16 * h : 16 * h + 16, :]
    yield 150
    eye = lax.broadcasted_iota(jnp.int32, (128, 128), 0) == lax.broadcasted_iota(
        jnp.int32, (128, 128), 1
    )
    tops = [None] * HEADS

    def scores(h, c):
        rows = slice(CHUNK * c, min(CHUNK * c + CHUNK, sc.rows))
        count = rows.stop - rows.start
        x_all = dot(sc.kn[rows], sc.qb[:, T * h : T * h + T])
        codes = sc.codes[rows]
        parts = []
        for j in range(3):
            lanes = slice(128 * j, 128 * j + 128)
            allowed = codes == code_row[:, lanes]
            if j == rows.start // 128:
                allowed = allowed | eye[rows.start % 128 : rows.start % 128 + count]
            part = jnp.where(allowed, x_all[:, lanes] + sc.bias[h, rows, lanes], MASK_FILL)
            sc.s[rows, lanes] = part
            parts.append(jnp.max(part.reshape(count // 8, 8, 128), axis=0))
        top = jnp.concatenate(parts, axis=1)
        tops[h] = top if tops[h] is None else jnp.maximum(tops[h], top)

    def raise_(h, c):
        rows = slice(CHUNK * c, min(CHUNK * c + CHUNK, sc.rows))
        sc.e[rows, T * h : T * h + T] = jnp.exp(sc.s[rows] - tops[h]).astype(BF)

    def attend(h):
        out = dot(sc.vt[h, :, 0 : sc.rows], sc.e[:, T * h : T * h + T])
        inverse = 1.0 / out[16:17]
        part = out[0:16] * inverse
        sc.att[16 * h : 16 * h + 16, :] = part
        sc.inv[h : h + 1, :] = inverse
        sc.attaug[16 * h : 16 * h + 16, :] = part.astype(BF)

    for h in range(HEADS + 2):
        for c in range(T // CHUNK):
            if 0 <= h - 1 < HEADS:
                raise_(h - 1, c)
            if h < HEADS:
                scores(h, c)
            if c == 3 and 0 <= h - 2 < HEADS:
                attend(h - 2)
            yield 35
        if h < HEADS:
            tops[h] = jnp.max(tops[h], axis=0, keepdims=True)
    st.branch = dot(w.projT[...], sc.attaug[...])
    yield 100


def backward_attention(sc, w, st, z, scale, shifted):
    d_mid = st.d
    db = d_mid.astype(BF)
    d_att = dot(w.proj[...], db).astype(BF).astype(F32)
    sc.gproj[...] += dot(sc.attaug[...], db, NT)
    yield 150
    row = lax.broadcasted_iota(jnp.int32, (16, T), 0)
    for h in range(HEADS):
        part = (d_att[16 * h : 16 * h + 16] * sc.inv[h : h + 1, :]).astype(BF)
        cols = slice(T * h, T * h + T)
        sc.dab[16 * h : 16 * h + 16, cols] = part
        inner = -jnp.sum(
            part.astype(F32) * sc.att[16 * h : 16 * h + 16, :], axis=0, keepdims=True
        )
        high = inner.astype(BF).astype(F32)
        low = inner - high
        sc.dab[C : C + 16, cols] = jnp.where(
            row == 0, high, jnp.where(row == 1, low, 0.0)
        ).astype(BF)
    yield 100
    total = None
    none = jnp.zeros((16, T), BF)

    def soft(h):
        cols = slice(T * h, T * h + T)
        pull = dot(sc.vn[0 : sc.rows], sc.dab[:, cols])
        sc.ds[h % 2, 0 : sc.rows] = (pull * sc.e[:, cols].astype(F32)).astype(BF)

    def place_rows(h):
        rb = sc.rb.at[h % 2]
        last = (h - 2) % HEADS
        rb[16 * last : 16 * last + 16, T:] = none
        rb[C + 16 * last : C + 16 * last + 16, 0:T] = none
        rb[16 * h : 16 * h + 16, T:] = sc.qT[16 * h : 16 * h + 16, :]
        rb[C + 16 * h : C + 16 * h + 16, 0:T] = sc.dab[
            16 * h : 16 * h + 16, T * h : T * h + T
        ]

    def to_queries(h):
        sc.dq[16 * h : 16 * h + 16, :] = dot(
            sc.kT[16 * h : 16 * h + 16, 0 : sc.rows], sc.ds[h % 2, 0 : sc.rows]
        ).astype(BF)

    for h in range(HEADS + 1):
        if h < HEADS:
            place_rows(h)
            soft(h)
            yield 120
        if h > 0:
            to_queries(h - 1)
            yield 60
            both = jnp.concatenate(
                [sc.e[:, T * (h - 1) : T * h], sc.ds[(h - 1) % 2, 0 : sc.rows]], axis=1
            )
            term = dot(both, sc.rb[(h - 1) % 2], NT)
            total = term if total is None else total + term
            yield 180
    dkv = total.astype(BF)
    if sc.rows < T:
        dkv = jnp.concatenate([dkv, jnp.zeros((T - sc.rows, 2 * C), BF)], axis=0)
    dq = sc.dq[...]
    dn = dot(w.q[...], dq) + dot(w.kv96[...], dkv, NT)
    yield 120
    sc.gkv[...] += dot(sc.n1aug[...], dkv)
    sc.gq[...] += dot(dq, sc.n1aug[...], NT)
    yield 150
    if shifted:
        dn = dn.astype(BF).astype(F32)
    sc.gvec[0] += dn * z
    sc.gvec[1] += dn
    st.d = d_mid + norm_back(dn, z, scale, wide(w.vec[0]))
    yield 150


def feed_forward_back(sc, w, st, dd, z, scale):
    dn = dot(w.up[...], sc.dh[...])
    yield 120
    sc.gdown[...] += dot(sc.act[...], dd, NT)
    yield 120
    sc.gup[...] += dot(sc.dh[...], sc.n2aug[...], NT)
    yield 120
    sc.gvec[4] += dd.astype(F32)
    sc.gvec[2] += dn * z
    sc.gvec[3] += dn
    st.d = st.d + norm_back(dn, z, scale, wide(w.vec[2]))
    yield 150


def write_grads(sc, out):
    gq = sc.gq[...].T
    gkv = sc.gkv[...]
    gup = sc.gup[...].T
    out[pl.ds(0, C, 3), :] = gq[0:C]
    out[pl.ds(1, C, 3), :] = gkv[0:C, 0:C]
    out[pl.ds(2, C, 3), :] = gkv[0:C, C : 2 * C]
    out[3 * C : 4 * C, :] = sc.gproj[0:C, :]
    for j in range(4):
        out[pl.ds(4 * C + j, C, 4), :] = gup[0:C, C * j : C * j + C]
    out[8 * C : 12 * C, :] = sc.gdown[...]
    sums = [jnp.sum(sc.gvec[n].T, axis=0, keepdims=True) for n in range(5)]
    rows = [
        sums[0],
        sums[1],
        gq[C : C + 1],
        gkv[C : C + 1, C : 2 * C],
        sc.gproj[C : C + 1, :],
        sums[2],
        sums[3],
        sums[4],
    ] + [gup[C : C + 1, C * j : C * j + C] for j in range(4)]
    for n, value in enumerate(rows):
        out[12 * C + n : 12 * C + n + 1, :] = value


FWD = dict(
    qb=((CA, HEADS * T), BF),
    vt=((HEADS, 32, T), BF),
    kn=((T, CA), BF),
    codes=((T, 128), F32),
    s=((T, T), F32),
)
BIAS = dict(bias=((HEADS, T, T), F32))
KEPT = dict(
    qT=((C, T), BF),
    kT=((C, T), BF),
    vn=((T, CA), BF),
    e=((T, HEADS * T), BF),
    att=((C, T), F32),
    inv=((8, T), F32),
    attaug=((CA, T), BF),
    n1aug=((CA, T), BF),
    n2aug=((CA, T), BF),
    act=((FF, T), BF),
    gp=((FF, T), BF),
    xT=((C, T), BF),
    x1=((C, T), F32),
)
GRADS = dict(
    gq=((C, CA), F32),
    gkv=((CA, 2 * C), F32),
    gproj=((CA, C), F32),
    gup=((FF, CA), F32),
    gdown=((FF, C), F32),
    gvec=((5, C, T), F32),
)
BWD = dict(
    dab=((CA, HEADS * T), BF),
    rb=((2, 2 * C, 2 * T), BF),
    ds=((2, T, T), BF),
    dq=((C, T), BF),
    dh=((FF, T), BF),
)


PADS = dict(pad=((C, T), BF), cot=((C, T), BF))
WEIGHTS = dict(
    qkvT=((3 * C, CA), BF),
    kv=((CA, 2 * CA), BF),
    projT=((C, CA), BF),
    proj=((C, C), BF),
    upT=((FF, CA), BF),
    up=((C, FF), BF),
    downT=((C, FF), BF),
    down=((FF, C), BF),
    q=((C, C), BF),
    kv96=((C, 2 * C), BF),
    vec=((5, C, 128), F32),
)


def of_layer(r, layer, slot):
    shared = {n: getattr(r, n).at[layer] for n in (*WEIGHTS, *GRADS, *BIAS)}
    return [
        SimpleNamespace(
            rows=ROWS[layer],
            **shared,
            **{n: getattr(r, n).at[i] for n in (*FWD, *BWD, *PADS)},
            **{n: getattr(r, KEPT_NAMES[layer][i] + n).at[slot] for n in KEPT},
        )
        for i in range(WINDOWS)
    ]


def second_norm(sc, w, x):
    z, scale = ln_stats(x)
    sc.n2aug[C:CA, :] = ones_row((CA - C, T)).astype(BF)
    sc.n2aug[0:C, :] = (z * wide(w.vec[2]) + wide(w.vec[3])).astype(BF)
    return z, scale


def grid_place(groups_a):
    win = lax.axis_index(WIN)
    return (win // 4, win // 2 % 2, win % 2), (groups_a, 2, 2)


def neighbour(octant, sign, groups_a):
    place, sizes = grid_place(groups_a)
    a, b, c = (
        (p + sign * bit + n) % n for p, bit, n in zip(place, octant_bits(octant), sizes)
    )
    return lax.axis_index(VOL), (a * 2 + b) * 2 + c


def greet(peers):
    barrier = pltpu.get_barrier_semaphore()
    for peer in peers:
        pl.semaphore_signal(barrier, inc=1, device_id=peer, device_id_type=MESH)


def await_greetings(peers):
    pl.semaphore_wait(pltpu.get_barrier_semaphore(), len(peers))


def block_copy(way, m, octant, groups_a):
    rows = pl.ds(OCT_OFF[octant], OCT_LEN[octant])
    slot = m % 2
    source = way.stage.at[slot, :, rows]
    target = way.got.at[pl.ds(m * WINDOWS, WINDOWS), rows]
    if octant == 0:
        return pltpu.make_async_copy(source, target, way.arrived.at[m, 0])
    return pltpu.make_async_remote_copy(
        src_ref=source,
        dst_ref=target,
        send_sem=way.sent.at[slot, octant],
        recv_sem=way.arrived.at[m, octant],
        device_id=neighbour(octant, way.sign, groups_a),
        device_id_type=MESH,
    )


def send_blocks(way, m, groups_a):
    for octant in range(8):
        block_copy(way, m, octant, groups_a).start()


def wait_sent(way, m, groups_a):
    for octant in range(1, 8):
        block_copy(way, m, octant, groups_a).wait_send()


def wait_arrived(way, m, groups_a):
    block_copy(way, m, 0, groups_a).wait()
    for octant in range(1, 8):
        block_copy(way, m, octant, groups_a).wait_recv()


def first_forward(r, sc, m, i):
    w, st = sc, SimpleNamespace()
    stage = r.x_stage.at[m % 2, i]
    sc.pad[:, 0:WS] = r.tokens[i, 0]
    st.x = sc.pad[...].astype(F32)
    sc.xT[...] = sc.pad[...]
    places = r.places
    valid = (
        (places[0:1, :] < r.extent[0, 0, m * WINDOWS + i])
        & (places[1:2, :] < r.extent[1, 0, m * WINDOWS + i])
        & (places[2:3, :] < r.extent[2, 0, m * WINDOWS + i])
    )
    valid = jnp.where(valid, 1.0, 0.0)
    sc.codes[...] = jnp.broadcast_to(valid - 1.0, (128, T)).T
    yield 100
    yield from forward_attention(sc, w, st, jnp.zeros((1, T), F32))
    sc.cot[:, 0:WS] = r.cotangent[i, 0]
    stage[:, CA:] = jnp.concatenate(
        [dot(r.perm[...], sc.cot[...], NT), jnp.zeros((T, CA - C), F32)], axis=1
    ).astype(BF)
    yield 100
    x = st.x + st.branch
    sc.x1[...] = x
    second_norm(sc, w, x)
    yield 150
    for c in range(6):
        rows = slice(64 * c, 64 * c + 64)
        active, slope = gelu_pair(dot(w.upT[rows], sc.n2aug[...]))
        sc.act[rows, :] = active.astype(BF)
        sc.gp[rows, :] = slope.astype(BF)
        yield 100
    x = x + (dot(w.downT[...], sc.act[...]) + wide(w.vec[4]))
    yield 100
    row = lax.broadcasted_iota(jnp.int32, (CA - C, T), 0)
    label = r.volume[0, m * WINDOWS + i].astype(F32)
    extra = jnp.where(row == 0, label, jnp.where(row == 1, valid, 0.0))
    x = jnp.concatenate([x, extra], axis=0).astype(BF)
    stage[:, 0:CA] = dot(r.perm[...], x, NT).astype(BF)
    yield 100


def second_layer(r, sc, m, i, groups_a):
    w, st = sc, SimpleNamespace()
    stage = r.d_stage.at[m % 2, i]
    n = m * WINDOWS + i
    came = r.x_got[n, :, 0:CA]
    x = came.T.astype(F32)
    place, sizes = grid_place(groups_a)
    code_row = []
    for octant in range(8):
        rows = slice(OCT_OFF[octant], OCT_OFF[octant] + OCT_LEN[octant])
        wraps = [
            bit * jnp.where(p == n_ - 1, 1, 0)
            for p, bit, n_ in zip(place, octant_bits(octant), sizes)
        ]
        wrap = (wraps[0] * 4 + wraps[1] * 2 + wraps[2]).astype(F32)
        columns = came[rows].astype(F32)
        code = jnp.where(columns[:, C + 1 : C + 2] > 0.0, columns[:, C : C + 1] * 8.0 + wrap, -1.0)
        sc.codes[rows, :] = jnp.broadcast_to(code, (OCT_LEN[octant], 128))
        code_row.append(jnp.full((1, OCT_LEN[octant]), wrap))
    code_row = jnp.concatenate(code_row, axis=1) + 8.0 * x[C : C + 1]
    keep = x[C + 1 : C + 2]
    x = x[0:C]
    sc.xT[...] = x.astype(BF)
    st.x = x
    yield 150
    yield from forward_attention(sc, w, st, code_row)
    st.d = r.x_got[n, :, CA:].T[0:C].astype(F32) * keep
    dd = st.d.astype(BF)
    x = sc.xT[...].astype(F32) + st.branch.astype(BF).astype(F32)
    z, scale = second_norm(sc, w, x)
    yield 200
    for c in range(6):
        rows = slice(64 * c, 64 * c + 64)
        active, slope = gelu_pair(dot(w.upT[rows], sc.n2aug[...]))
        sc.act[rows, :] = active.astype(BF)
        sc.dh[rows, :] = (dot(w.down[rows], dd) * slope).astype(BF)
        yield 120
    x = x + (dot(w.downT[...], sc.act[...]) + wide(w.vec[4]))
    none = jnp.zeros((CA - C, T), F32)
    stage[:, 0:CA] = jnp.concatenate([x * keep, none], axis=0).T.astype(BF)
    yield 150
    yield from feed_forward_back(sc, w, st, dd, z, scale)
    z, scale = ln_stats(sc.xT[...].astype(F32))
    yield from backward_attention(sc, w, st, z, scale, True)
    stage[:, CA:] = jnp.concatenate([st.d, none], axis=0).T.astype(BF)
    yield 100


def first_backward(r, sc, m, i):
    w, st = sc, SimpleNamespace()
    came = r.d_got[m * WINDOWS + i].T
    came = jnp.concatenate([came[0:C], came[CA : CA + C]], axis=0)
    yield 200
    came = dot(came, r.perm[...])
    r.output[i, 0] = came[0:C, 0:WS].astype(BF)
    st.d = came[C : 2 * C]
    dd = st.d.astype(BF)
    z, scale = ln_stats(sc.x1[...])
    yield 200
    for c in range(3):
        rows = slice(128 * c, 128 * c + 128)
        sc.dh[rows, :] = (dot(w.down[rows], dd) * sc.gp[rows, :].astype(F32)).astype(BF)
        yield 50
    yield from feed_forward_back(sc, w, st, dd, z, scale)
    z, scale = ln_stats(sc.xT[...].astype(F32))
    yield from backward_attention(sc, w, st, z, scale, False)
    r.input_grad[i, 0] = st.d[:, 0:WS]
    yield 50


def layers_kernel(n_vol, n_plane, shard_len, steps, r):
    groups_a = n_plane // 2
    s = pl.program_id(0)
    forth = SimpleNamespace(
        stage=r.x_stage, got=r.x_got, sent=r.x_sent, arrived=r.x_arrived, sign=-1
    )
    back = SimpleNamespace(
        stage=r.d_stage, got=r.d_got, sent=r.d_sent, arrived=r.d_arrived, sign=1
    )

    far = all_peers(n_vol, n_plane)
    reduction = Reduction(r, far, n_vol, n_plane, shard_len)

    @pl.when(s == 0)
    def _():
        peers = far + [
            neighbour(octant, sign, groups_a) for sign in (1, -1) for octant in range(1, 8)
        ]
        greet(peers)
        for n in range(TABLE_SLOTS):
            table_copy(r, n).start()
        vol, plane, core = own_place()
        r.buf[core, plane, vol] = r.shard[...].astype(BF)
        clear_scratch(r)
        await_greetings(peers)
        meanwhile = (lambda: turn_tables(r, 0), lambda: turn_tables(r, 1), lambda: None)
        for copies, work in zip(gather_stages(r, far, n_vol, n_plane), meanwhile):
            for c in copies:
                c.start()
            work()
            for c in copies:
                c.wait()
        prepare(r, n_vol, n_plane, shard_len)

    @pl.when(s < steps)
    def _():
        @pl.when(s >= 2)
        def _():
            wait_sent(forth, s - 2, groups_a)

        windows = of_layer(r, 0, s % 3)
        weave([first_forward(r, sc, s, i) for i, sc in enumerate(windows)], LAG)
        send_blocks(forth, s, groups_a)

    @pl.when((s >= 1) & (s <= steps))
    def _():
        m = s - 1
        wait_arrived(forth, m, groups_a)

        @pl.when(m >= 2)
        def _():
            wait_sent(back, m - 2, groups_a)

        windows = of_layer(r, 1, 0)
        weave([second_layer(r, sc, m, i, groups_a) for i, sc in enumerate(windows)], LAG)
        send_blocks(back, m, groups_a)

    @pl.when(s == steps)
    def _():
        write_grads(of_layer(r, 1, 0)[0], r.grads.at[1])
        reduction.start_core(1)

    @pl.when(s == steps + 1)
    def _():
        reduction.start_plane(1)

    @pl.when(s >= 2)
    def _():
        m = s - 2
        wait_arrived(back, m, groups_a)
        windows = of_layer(r, 0, m % 3)
        weave([first_backward(r, sc, m, i) for i, sc in enumerate(windows)], LAG)

    @pl.when(s == steps + 1)
    def _():
        write_grads(of_layer(r, 0, 0)[0], r.grads.at[0])
        reduction.start_core(0)
        reduction.end_plane(1)
        reduction.start_plane(0)
        for m in range(max(steps - 2, 0), steps):
            wait_sent(forth, m, groups_a)
            wait_sent(back, m, groups_a)
        reduction.end_plane(0)
        reduction.finish()


def shard_rows(device, shard_len):
    return device * shard_len // C, -(-(device + 1) * shard_len // C)


def flat_offset(device, shard_len):
    return device * shard_len % C


def slab_rows(shard_len):
    return -(-((shard_len + C - 2) // C + 1) // 16) * 16


def own_place():
    win = lax.axis_index(WIN)
    return lax.axis_index(VOL), win // 2, win % 2


def all_peers(n_vol, n_plane):
    vol, plane, core = own_place()
    return (
        [((vol + j) % n_vol, plane * 2 + core) for j in range(1, n_vol)]
        + [(vol, (plane + j) % n_plane * 2 + core) for j in range(1, n_plane)]
        + [(vol, plane * 2 + 1 - core)]
    )


def transpose_with(matrix, extra):
    below = jnp.where(lax.broadcasted_iota(jnp.int32, (CA - C, C), 0) == 0, extra, 0.0)
    return jnp.concatenate([matrix, below], axis=0).T


def gather_stages(r, peers, n_vol, n_plane):
    vol, plane, core = own_place()

    def copy(ref, n):
        return pltpu.make_async_remote_copy(
            src_ref=ref,
            dst_ref=ref,
            send_sem=r.g_sent.at[n],
            recv_sem=r.g_arrived.at[n],
            device_id=peers[n],
            device_id_type=MESH,
        )

    return (
        [copy(r.buf.at[core, plane, vol], n) for n in range(n_vol - 1)],
        [copy(r.buf.at[core, plane], n_vol - 1 + n) for n in range(n_plane - 1)],
        [copy(r.buf.at[core], n_vol + n_plane - 2)],
    )


def prepare(r, n_vol, n_plane, shard_len):
    buf = r.buf
    flat = r.grads
    flat[...] = jnp.zeros(flat.shape, F32)
    half = n_vol * n_plane
    for v in range(n_vol):
        for p in range(n_plane):
            for c in range(2):
                device = (v * n_plane + p) * 2 + c
                start, stop = shard_rows(device % half, shard_len)
                flat[device // half, start:stop, :] += buf[c, p, v, 0 : stop - start].astype(F32)
    for layer in range(2):

        def rows(start, count=C, stride=1):
            return flat[layer, pl.ds(start, count, stride), :]

        def vector(n):
            return rows(12 * C + n, 1)

        o = SimpleNamespace(**{n: getattr(r, n).at[layer] for n in WEIGHTS})
        none = jnp.zeros((1, C), F32)
        wq, wk, wv = (rows(n, C, 3) for n in range(3))
        o.q[...] = wq.astype(BF)
        o.kv96[...] = jnp.concatenate([wk, wv], axis=1).astype(BF)
        o.qkvT[0:C, :] = (transpose_with(wq, vector(2)) * 0.25).astype(BF)
        o.qkvT[C : 2 * C, :] = (transpose_with(wk, none) * 0.25).astype(BF)
        o.qkvT[2 * C :, :] = transpose_with(wv, vector(3)).astype(BF)
        row = lax.broadcasted_iota(jnp.int32, (CA - C, CA), 0)
        lane = lax.broadcasted_iota(jnp.int32, (CA - C, CA), 1)
        blank = jnp.zeros((C, CA - C), F32)
        bias_v = jnp.concatenate([vector(3), blank[0:1]], axis=1)
        ones = jnp.where((lane == C) | (lane == C + 1), 1.0, bias_v)
        o.kv[0:C, :] = jnp.concatenate([wk, blank, wv, blank], axis=1).astype(BF)
        o.kv[C:, 0:CA] = jnp.zeros((CA - C, CA), BF)
        o.kv[C:, CA:] = jnp.where(row == 0, ones, 0.0).astype(BF)
        proj = rows(3 * C)
        o.proj[...] = proj.astype(BF)
        o.projT[...] = transpose_with(proj, vector(4)).astype(BF)
        ups = [rows(4 * C + j, C, 4) for j in range(4)]
        o.up[...] = jnp.concatenate(ups, axis=1).astype(BF)
        for j in range(4):
            o.upT[C * j : C * j + C, :] = transpose_with(ups[j], vector(8 + j)).astype(BF)
        down = rows(8 * C, FF)
        o.down[...] = down.astype(BF)
        o.downT[...] = down.T.astype(BF)
        for n, source in enumerate((0, 1, 5, 6, 7)):
            o.vec[n] = jnp.broadcast_to(vector(source), (128, C)).T


class Reduction:
    def __init__(self, r, peers, n_vol, n_plane, shard_len):
        self.r, self.peers, self.shard_len = r, peers, shard_len
        self.n_vol, self.n_plane, self.half = n_vol, n_plane, n_vol // 2
        self.vol, self.plane, self.core = own_place()

    def vols(self, layer):
        return pl.ds(layer * self.half, self.half)

    def copy(self, source, target, peer, n):
        return pltpu.make_async_remote_copy(
            src_ref=source,
            dst_ref=target,
            send_sem=self.r.r_sent.at[n],
            recv_sem=self.r.r_arrived.at[n],
            device_id=self.peers[peer],
            device_id_type=MESH,
        )

    def over_core(self, layer):
        source = self.r.work.at[1 - self.core, :, self.vols(layer)]
        return [self.copy(source, self.r.from_core.at[layer], len(self.peers) - 1, layer)]

    def over_plane(self, layer):
        return [
            self.copy(
                self.r.wire.at[(self.plane + j) % self.n_plane, self.vols(layer)],
                self.r.from_plane.at[layer, j - 1],
                self.n_vol - 2 + j,
                2 + layer * (self.n_plane - 1) + j - 1,
            )
            for j in range(1, self.n_plane)
        ]

    def over_vol(self):
        return [
            self.copy(
                self.r.wire.at[self.plane, (self.vol + j) % self.n_vol],
                self.r.from_vol.at[j - 1],
                j - 1,
                2 * self.n_plane + j - 1,
            )
            for j in range(1, self.n_vol)
        ]

    def start_core(self, layer):
        for v in range(layer * self.half, (layer + 1) * self.half):
            for p in range(self.n_plane):
                for c in range(2):
                    device = (v % self.half * self.n_plane + p) * 2 + c
                    start, stop = shard_rows(device, self.shard_len)
                    self.r.work[c, p, v, 0 : stop - start] = self.r.grads[layer, start:stop, :]
        for c in self.over_core(layer):
            c.start()

    def start_plane(self, layer):
        for c in self.over_core(layer):
            c.wait()
        vols, work = self.vols(layer), self.r.work
        total = work[self.core, :, vols] + self.r.from_core[layer]
        work[self.core, :, vols] = total
        self.r.wire[:, vols] = total.astype(BF)
        for c in self.over_plane(layer):
            c.start()

    def end_plane(self, layer):
        for c in self.over_plane(layer):
            c.wait()
        vols, work = self.vols(layer), self.r.work
        total = work[self.core, self.plane, vols]
        for j in range(self.n_plane - 1):
            total = total + self.r.from_plane[layer, j].astype(F32)
        work[self.core, self.plane, vols] = total
        self.r.wire[self.plane, vols] = total.astype(BF)

    def finish(self):
        for c in self.over_vol():
            c.start()
        for c in self.over_vol():
            c.wait()
        total = self.r.work[self.core, self.plane, self.vol]
        for j in range(self.n_vol - 1):
            total = total + self.r.from_vol[j].astype(F32)
        self.r.total[...] = total


def call(kernel, steps, ins, outs, scratch, semaphores=(), collective_id=None, lag=0):
    def spec(shape, kind, late):
        if kind in (SMEM, HBM):
            return pl.BlockSpec(memory_space=pltpu.SMEM if kind is SMEM else pl.ANY)
        zeros = (0,) * (len(shape) - 1)
        if kind is BY_STEP:

            def index(s):
                return (jnp.clip(s - late, 0, steps - 1),) + zeros

            return pl.BlockSpec((shape[0] // steps,) + tuple(shape[1:]), index)
        return pl.BlockSpec(
            tuple(shape), lambda s: (0,) + zeros, pipeline_mode=None if late else pl.Buffered(1)
        )

    semaphores = dict(semaphores)
    names = tuple(ins) + tuple(outs) + tuple(scratch) + tuple(semaphores)

    def body(*refs):
        kernel(SimpleNamespace(**dict(zip(names, refs))))

    results = pl.pallas_call(
        body,
        grid=(steps + lag,),
        in_specs=[spec(a.shape, kind, 0) for a, kind in ins.values()],
        out_specs=[spec(shape, kind, lag) for shape, _, kind in outs.values()],
        out_shape=[jax.ShapeDtypeStruct(shape, dtype) for shape, dtype, _ in outs.values()],
        scratch_shapes=[pltpu.VMEM(shape, dtype) for shape, dtype in scratch.values()]
        + [pltpu.SemaphoreType.DMA(shape) for shape in semaphores.values()],
        compiler_params=pltpu.CompilerParams(
            vmem_limit_bytes=62 * 2**20,
            collective_id=collective_id,
            has_side_effects=collective_id is not None,
        ),
    )(*[a for a, _ in ins.values()])
    return SimpleNamespace(**dict(zip(outs, results)))


def on_device(
    tokens,
    cotangent,
    position_bias,
    window_volume,
    clip_extent,
    master,
    first_moment,
    second_moment,
):
    n_vol, n_win = lax.axis_size(VOL), lax.axis_size(WIN)
    n_plane = n_win // 2
    count = tokens.shape[0]
    steps = count // WINDOWS
    shard_len = master.shape[0]
    device = lax.axis_index((VOL, WIN))
    slab = slab_rows(shard_len)
    offset = flat_offset(device, shard_len)
    shard = lax.dynamic_update_slice(jnp.zeros((slab * C,), F32), master, (offset,))
    n_peers = n_vol + n_plane - 1

    def each(table, *sizes):
        return {n: (sizes + shape, dtype) for n, (shape, dtype) in table.items()}

    def kept(layer, slots):
        shapes = dict(KEPT, e=((ROWS[layer], HEADS * T), BF))
        shapes = dict(shapes, gp=((16, T), BF)) if layer else shapes
        return {name + n: v for name in KEPT_NAMES[layer] for n, v in each(shapes, slots).items()}

    stage, landing = ((2, WINDOWS, T, 2 * CA), BF), ((count, T, 2 * CA), BF)
    layers = call(
        lambda r: layers_kernel(n_vol, n_plane, shard_len, steps, r),
        steps,
        dict(
            tokens=(tokens.transpose(0, 1, 3, 2), BY_STEP),
            cotangent=(cotangent.transpose(0, 1, 3, 2), BY_STEP),
            volume=(window_volume.T, SMEM),
            extent=(clip_extent.transpose(2, 1, 0), SMEM),
            perm=(jnp.asarray(PERM, BF), WHOLE),
            places=(jnp.asarray(PLACES), WHOLE),
            order=(jnp.asarray(np.stack([np.eye(T, WS), ORDER]), BF), WHOLE),
            table=(position_bias, HBM),
            shard=(shard.reshape(slab, C), WHOLE),
        ),
        dict(
            output=((count, 1, C, WS), BF, BY_STEP),
            input_grad=((count, 1, C, WS), F32, BY_STEP),
            total=((slab, C), F32, WHOLE),
        ),
        dict(
            **each(FWD, WINDOWS),
            **each(BWD, WINDOWS),
            **each(PADS, WINDOWS),
            **each(GRADS, 2),
            **each(BIAS, 2),
            **kept(0, 3),
            **kept(1, 1),
            **each(WEIGHTS, 2),
            page=((TABLE_SLOTS, WS, WS), BF),
            buf=((2, n_plane, n_vol, slab, C), BF),
            grads=((2, BLOCK_ROWS, C), F32),
            work=((2, n_plane, n_vol, slab, C), F32),
            wire=((n_plane, n_vol, slab, C), BF),
            from_core=((2, n_plane, n_vol // 2, slab, C), F32),
            from_plane=((2, n_plane - 1, n_vol // 2, slab, C), BF),
            from_vol=((n_vol - 1, slab, C), BF),
            x_stage=stage,
            d_stage=stage,
            x_got=landing,
            d_got=landing,
        ),
        dict(
            x_sent=(2, 8),
            x_arrived=(steps, 8),
            d_sent=(2, 8),
            d_arrived=(steps, 8),
            g_sent=(n_peers,),
            g_arrived=(n_peers,),
            turned=(TABLE_SLOTS,),
            r_sent=(2 * n_plane + n_vol - 1,),
            r_arrived=(2 * n_plane + n_vol - 1,),
        ),
        collective_id=1,
        lag=2,
    )
    shard_grad = lax.dynamic_slice(layers.total.reshape(-1), (offset,), (shard_len,))
    position = (device * shard_len + jnp.arange(shard_len, dtype=jnp.int32)) % (BLOCK_ROWS * C)
    is_vector = position >= 12 * C * C
    step_rate = jnp.where(is_vector, RATE_VECTOR, RATE_MATRIX)
    weight_decay = jnp.where(is_vector, 0.0, DECAY_MATRIX)
    moment_one = BETA_FIRST * first_moment + (1.0 - BETA_FIRST) * shard_grad
    moment_two = BETA_SECOND * second_moment + (1.0 - BETA_SECOND) * shard_grad * shard_grad
    corrected_one = moment_one / (1.0 - BETA_FIRST**STEP)
    corrected_two = moment_two / (1.0 - BETA_SECOND**STEP)
    normalized = corrected_one / (jnp.sqrt(corrected_two) + ADAM_EPS)
    new_master = master - step_rate * (normalized + weight_decay * master)
    return (
        layers.output.transpose(0, 1, 3, 2),
        layers.input_grad.transpose(0, 1, 3, 2),
        new_master,
        moment_one,
        moment_two,
        new_master.astype(BF),
    )


def solution(mesh):
    placed = (
        P(None, (VOL, WIN), None, None),
        P(None, (VOL, WIN), None, None),
        P(),
        P(None, (VOL, WIN)),
        P(None, (VOL, WIN), None),
        P((VOL, WIN)),
        P((VOL, WIN)),
        P((VOL, WIN)),
    )
    return jax.shard_map(
        on_device,
        mesh=mesh,
        in_specs=placed,
        out_specs=(
            P(None, (VOL, WIN), None, None),
            P(None, (VOL, WIN), None, None),
            P((VOL, WIN)),
            P((VOL, WIN)),
            P((VOL, WIN)),
            P((VOL, WIN)),
        ),
        check_vma=False,
    )
```

```python
from types import SimpleNamespace

import jax
import jax.numpy as jnp
import numpy as np
from jax import lax
from jax.experimental import pallas as pl
from jax.experimental.pallas import tpu as pltpu
from jax.sharding import PartitionSpec as P

C = 96
HEADS = 6
HEAD_DIM = 16
FF = 384
SIDE = 7
SHIFT = 3
WS = 343
STEP = 6
T = 384
WINDOWS = 2
CHUNK = 64
LAG = 150
TABLE_SLOTS = 3
ROWS = (352, T)
CA = 128
BLOCK_ROWS = 1164

NORM_EPS = 1e-05
MASK_FILL = -1000000000.0
BETA_FIRST = 0.5
BETA_SECOND = 0.5
ADAM_EPS = 1e-08
RATE_MATRIX = 0.1
RATE_VECTOR = 0.4
DECAY_MATRIX = 0.05

BF = jnp.bfloat16
F32 = jnp.float32
NN = (((1,), (0,)), ((), ()))
NT = (((1,), (1,)), ((), ()))
BY_STEP, WHOLE, SMEM, HBM = range(4)
MESH = pl.DeviceIdType.MESH
VOL, WIN = "vol", "win"
KEPT_NAMES = ("a0", "a1"), ("b0", "b1")


def octant_bits(octant):
    return (octant >> 2 & 1, octant >> 1 & 1, octant & 1)


OCT_SIZE = []
OCT_LEN = []
OCT_OFF = []
for _octant in range(8):
    _size = 1
    for _bit in octant_bits(_octant):
        _size *= SHIFT if _bit else SIDE - SHIFT
    OCT_OFF.append(sum(OCT_LEN))
    OCT_SIZE.append(_size)
    OCT_LEN.append(-(-_size // 16) * 16)


def slot_tables():
    perm = np.zeros((T, T), np.float32)
    order = np.zeros((T, WS), np.float32)
    places = np.full((8, T), 99, np.int32)
    for octant in range(8):
        bits = octant_bits(octant)
        lens = [SHIFT if bit else SIDE - SHIFT for bit in bits]
        for i in range(lens[0]):
            for j in range(lens[1]):
                for k in range(lens[2]):
                    source = [v if bit else v + SHIFT for v, bit in zip((i, j, k), bits)]
                    own = [v + bit * (SIDE - SHIFT) for v, bit in zip((i, j, k), bits)]
                    q = OCT_OFF[octant] + (i * lens[1] + j) * lens[2] + k
                    t = (source[0] * SIDE + source[1]) * SIDE + source[2]
                    perm[q, t] = 1
                    order[q, (own[0] * SIDE + own[1]) * SIDE + own[2]] = 1
                    places[:3, t] = source
    return perm, order, places


PERM, ORDER, PLACES = slot_tables()


def dot(a, b, dims=NN):
    return lax.dot_general(a, b, dims, preferred_element_type=F32)


def wide(column):
    return jnp.concatenate([column] * (T // 128), axis=1)


def ln_stats(x):
    centred = x - jnp.mean(x, axis=0, keepdims=True)
    scale = lax.rsqrt(jnp.mean(centred * centred, axis=0, keepdims=True) + NORM_EPS)
    return centred * scale, scale


def norm_back(e, z, scale, gain):
    eg = e * gain
    return scale * (
        eg - jnp.mean(eg, axis=0, keepdims=True) - z * jnp.mean(eg * z, axis=0, keepdims=True)
    )


def gelu_pair(h):
    base = 1.0 + (0.3275911 * 0.7071067811865476) * jnp.abs(h)
    t = pl.reciprocal(base, approx=True)
    t = t * (2.0 - base * t)
    poly = t * (
        0.5 * 0.254829592
        + t
        * (
            0.5 * -0.284496736
            + t * (0.5 * 1.421413741 + t * (0.5 * -1.453152027 + t * (0.5 * 1.061405429)))
        )
    )
    bell = jnp.exp(-0.5 * (h * h))
    tail = poly * bell
    phi = jnp.where(h < 0.0, tail, 1.0 - tail)
    return h * phi, phi + h * bell * 0.3989422804014327


def ones_row(shape, row=0):
    return jnp.where(lax.broadcasted_iota(jnp.int32, shape, 0) == row, 1.0, 0.0)


def weave(tasks, lag):
    clocks = [lag * n for n in range(len(tasks))]
    while tasks:
        n = clocks.index(min(clocks))
        cost = next(tasks[n], None)
        if cost is None:
            tasks, clocks = (x[:n] + x[n + 1 :] for x in (tasks, clocks))
        else:
            clocks[n] += cost


def clear_scratch(r):
    zeros = jnp.zeros((CA, HEADS * T), BF)
    for i in range(WINDOWS):
        r.qb[i] = zeros
        r.dab[i] = zeros
        r.rb[i] = jnp.zeros((2, 2 * C, 2 * T), BF)
        r.pad[i] = jnp.zeros((C, T), BF)
        r.cot[i] = jnp.zeros((C, T), BF)
        for h in range(HEADS):
            r.vt[i, h, 16:32, :] = ones_row((16, T)).astype(BF)
    for name, (shape, dtype) in GRADS.items():
        getattr(r, name)[...] = jnp.zeros((2,) + shape, dtype)


def table_copy(r, n):
    slot = n % TABLE_SLOTS
    return pltpu.make_async_copy(
        r.table.at[n // HEADS, n % HEADS], r.page.at[slot], r.turned.at[slot]
    )


def turn_tables(r, layer):
    for n in range(HEADS * layer, HEADS * layer + HEADS):
        table_copy(r, n).wait()
        half = dot(r.order[layer], r.page[n % TABLE_SLOTS], NT).astype(BF)
        if n + TABLE_SLOTS < 2 * HEADS:
            table_copy(r, n + TABLE_SLOTS).start()
        r.bias[layer, n % HEADS] = dot(half, r.order[layer], NT)


def set_queries(sc, queries):
    for h in range(HEADS):
        sc.qb[16 * h : 16 * h + 16, T * h : T * h + T] = queries[16 * h : 16 * h + 16, :]


def forward_attention(sc, w, st, code_row):
    z, _ = ln_stats(st.x)
    sc.n1aug[C:CA, :] = ones_row((CA - C, T)).astype(BF)
    sc.attaug[C:CA, :] = ones_row((CA - C, T)).astype(BF)
    sc.n1aug[0:C, :] = (z * wide(w.vec[0]) + wide(w.vec[1])).astype(BF)
    yield 150
    kv = dot(sc.n1aug[...].T, w.kv[...]).astype(BF)
    sc.kn[...] = kv[:, 0:CA]
    sc.vn[...] = kv[:, CA:]
    yield 200
    qkv = dot(w.qkvT[...], sc.n1aug[...])
    queries = qkv[0:C].astype(BF)
    set_queries(sc, queries)
    sc.qT[...] = queries
    sc.kT[...] = qkv[C : 2 * C].astype(BF)
    values = qkv[2 * C :].astype(BF)
    for h in range(HEADS):
        sc.vt[h, 0:16, :] = values[16 * h : 16 * h + 16, :]
    yield 150
    eye = lax.broadcasted_iota(jnp.int32, (128, 128), 0) == lax.broadcasted_iota(
        jnp.int32, (128, 128), 1
    )
    tops = [None] * HEADS

    def scores(h, c):
        rows = slice(CHUNK * c, min(CHUNK * c + CHUNK, sc.rows))
        count = rows.stop - rows.start
        x_all = dot(sc.kn[rows], sc.qb[:, T * h : T * h + T])
        codes = sc.codes[rows]
        parts = []
        for j in range(3):
            lanes = slice(128 * j, 128 * j + 128)
            allowed = codes == code_row[:, lanes]
            if j == rows.start // 128:
                allowed = allowed | eye[rows.start % 128 : rows.start % 128 + count]
            part = jnp.where(allowed, x_all[:, lanes] + sc.bias[h, rows, lanes], MASK_FILL)
            sc.s[rows, lanes] = part
            parts.append(jnp.max(part.reshape(count // 8, 8, 128), axis=0))
        top = jnp.concatenate(parts, axis=1)
        tops[h] = top if tops[h] is None else jnp.maximum(tops[h], top)

    def raise_(h, c):
        rows = slice(CHUNK * c, min(CHUNK * c + CHUNK, sc.rows))
        sc.e[rows, T * h : T * h + T] = jnp.exp(sc.s[rows] - tops[h]).astype(BF)

    def attend(h):
        out = dot(sc.vt[h, :, 0 : sc.rows], sc.e[:, T * h : T * h + T])
        inverse = 1.0 / out[16:17]
        part = out[0:16] * inverse
        sc.att[16 * h : 16 * h + 16, :] = part
        sc.inv[h : h + 1, :] = inverse
        sc.attaug[16 * h : 16 * h + 16, :] = part.astype(BF)

    for h in range(HEADS + 2):
        for c in range(T // CHUNK):
            if 0 <= h - 1 < HEADS:
                raise_(h - 1, c)
            if h < HEADS:
                scores(h, c)
            if c == 3 and 0 <= h - 2 < HEADS:
                attend(h - 2)
            yield 35
        if h < HEADS:
            tops[h] = jnp.max(tops[h], axis=0, keepdims=True)
    st.branch = dot(w.projT[...], sc.attaug[...])
    yield 100


def backward_attention(sc, w, st, z, scale, shifted):
    d_mid = st.d
    db = d_mid.astype(BF)
    d_att = dot(w.proj[...], db).astype(BF).astype(F32)
    sc.gproj[...] += dot(sc.attaug[...], db, NT)
    yield 150
    row = lax.broadcasted_iota(jnp.int32, (16, T), 0)
    for h in range(HEADS):
        part = (d_att[16 * h : 16 * h + 16] * sc.inv[h : h + 1, :]).astype(BF)
        cols = slice(T * h, T * h + T)
        sc.dab[16 * h : 16 * h + 16, cols] = part
        inner = -jnp.sum(
            part.astype(F32) * sc.att[16 * h : 16 * h + 16, :], axis=0, keepdims=True
        )
        high = inner.astype(BF).astype(F32)
        low = inner - high
        sc.dab[C : C + 16, cols] = jnp.where(
            row == 0, high, jnp.where(row == 1, low, 0.0)
        ).astype(BF)
    yield 100
    total = None
    none = jnp.zeros((16, T), BF)

    def soft(h):
        cols = slice(T * h, T * h + T)
        pull = dot(sc.vn[0 : sc.rows], sc.dab[:, cols])
        sc.ds[h % 2, 0 : sc.rows] = (pull * sc.e[:, cols].astype(F32)).astype(BF)

    def place_rows(h):
        rb = sc.rb.at[h % 2]
        last = (h - 2) % HEADS
        rb[16 * last : 16 * last + 16, T:] = none
        rb[C + 16 * last : C + 16 * last + 16, 0:T] = none
        rb[16 * h : 16 * h + 16, T:] = sc.qT[16 * h : 16 * h + 16, :]
        rb[C + 16 * h : C + 16 * h + 16, 0:T] = sc.dab[
            16 * h : 16 * h + 16, T * h : T * h + T
        ]

    def to_queries(h):
        sc.dq[16 * h : 16 * h + 16, :] = dot(
            sc.kT[16 * h : 16 * h + 16, 0 : sc.rows], sc.ds[h % 2, 0 : sc.rows]
        ).astype(BF)

    for h in range(HEADS + 1):
        if h < HEADS:
            place_rows(h)
            soft(h)
            yield 120
        if h > 0:
            to_queries(h - 1)
            yield 60
            both = jnp.concatenate(
                [sc.e[:, T * (h - 1) : T * h], sc.ds[(h - 1) % 2, 0 : sc.rows]], axis=1
            )
            term = dot(both, sc.rb[(h - 1) % 2], NT)
            total = term if total is None else total + term
            yield 180
    dkv = total.astype(BF)
    if sc.rows < T:
        dkv = jnp.concatenate([dkv, jnp.zeros((T - sc.rows, 2 * C), BF)], axis=0)
    dq = sc.dq[...]
    dn = dot(w.q[...], dq) + dot(w.kv96[...], dkv, NT)
    yield 120
    sc.gkv[...] += dot(sc.n1aug[...], dkv)
    sc.gq[...] += dot(dq, sc.n1aug[...], NT)
    yield 150
    if shifted:
        dn = dn.astype(BF).astype(F32)
    sc.gvec[0] += dn * z
    sc.gvec[1] += dn
    st.d = d_mid + norm_back(dn, z, scale, wide(w.vec[0]))
    yield 150


def feed_forward_back(sc, w, st, dd, z, scale):
    dn = dot(w.up[...], sc.dh[...])
    yield 120
    sc.gdown[...] += dot(sc.act[...], dd, NT)
    yield 120
    sc.gup[...] += dot(sc.dh[...], sc.n2aug[...], NT)
    yield 120
    sc.gvec[4] += dd.astype(F32)
    sc.gvec[2] += dn * z
    sc.gvec[3] += dn
    st.d = st.d + norm_back(dn, z, scale, wide(w.vec[2]))
    yield 150


def write_grads(sc, out):
    gq = sc.gq[...].T
    gkv = sc.gkv[...]
    gup = sc.gup[...].T
    out[pl.ds(0, C, 3), :] = gq[0:C]
    out[pl.ds(1, C, 3), :] = gkv[0:C, 0:C]
    out[pl.ds(2, C, 3), :] = gkv[0:C, C : 2 * C]
    out[3 * C : 4 * C, :] = sc.gproj[0:C, :]
    for j in range(4):
        out[pl.ds(4 * C + j, C, 4), :] = gup[0:C, C * j : C * j + C]
    out[8 * C : 12 * C, :] = sc.gdown[...]
    sums = [jnp.sum(sc.gvec[n].T, axis=0, keepdims=True) for n in range(5)]
    rows = [
        sums[0],
        sums[1],
        gq[C : C + 1],
        gkv[C : C + 1, C : 2 * C],
        sc.gproj[C : C + 1, :],
        sums[2],
        sums[3],
        sums[4],
    ] + [gup[C : C + 1, C * j : C * j + C] for j in range(4)]
    for n, value in enumerate(rows):
        out[12 * C + n : 12 * C + n + 1, :] = value


FWD = dict(
    qb=((CA, HEADS * T), BF),
    vt=((HEADS, 32, T), BF),
    kn=((T, CA), BF),
    codes=((T, 128), F32),
    s=((T, T), F32),
)
BIAS = dict(bias=((HEADS, T, T), F32))
KEPT = dict(
    qT=((C, T), BF),
    kT=((C, T), BF),
    vn=((T, CA), BF),
    e=((T, HEADS * T), BF),
    att=((C, T), F32),
    inv=((8, T), F32),
    attaug=((CA, T), BF),
    n1aug=((CA, T), BF),
    n2aug=((CA, T), BF),
    act=((FF, T), BF),
    gp=((FF, T), BF),
    xT=((C, T), BF),
    x1=((C, T), F32),
)
GRADS = dict(
    gq=((C, CA), F32),
    gkv=((CA, 2 * C), F32),
    gproj=((CA, C), F32),
    gup=((FF, CA), F32),
    gdown=((FF, C), F32),
    gvec=((5, C, T), F32),
)
BWD = dict(
    dab=((CA, HEADS * T), BF),
    rb=((2, 2 * C, 2 * T), BF),
    ds=((2, T, T), BF),
    dq=((C, T), BF),
    dh=((FF, T), BF),
)


PADS = dict(pad=((C, T), BF), cot=((C, T), BF))
WEIGHTS = dict(
    qkvT=((3 * C, CA), BF),
    kv=((CA, 2 * CA), BF),
    projT=((C, CA), BF),
    proj=((C, C), BF),
    upT=((FF, CA), BF),
    up=((C, FF), BF),
    downT=((C, FF), BF),
    down=((FF, C), BF),
    q=((C, C), BF),
    kv96=((C, 2 * C), BF),
    vec=((5, C, 128), F32),
)


def of_layer(r, layer, slot):
    shared = {n: getattr(r, n).at[layer] for n in (*WEIGHTS, *GRADS, *BIAS)}
    return [
        SimpleNamespace(
            rows=ROWS[layer],
            **shared,
            **{n: getattr(r, n).at[i] for n in (*FWD, *BWD, *PADS)},
            **{n: getattr(r, KEPT_NAMES[layer][i] + n).at[slot] for n in KEPT},
        )
        for i in range(WINDOWS)
    ]


def second_norm(sc, w, x):
    z, scale = ln_stats(x)
    sc.n2aug[C:CA, :] = ones_row((CA - C, T)).astype(BF)
    sc.n2aug[0:C, :] = (z * wide(w.vec[2]) + wide(w.vec[3])).astype(BF)
    return z, scale


def grid_place(groups_a):
    win = lax.axis_index(WIN)
    return (win // 4, win // 2 % 2, win % 2), (groups_a, 2, 2)


def neighbour(octant, sign, groups_a):
    place, sizes = grid_place(groups_a)
    a, b, c = (
        (p + sign * bit + n) % n for p, bit, n in zip(place, octant_bits(octant), sizes)
    )
    return lax.axis_index(VOL), (a * 2 + b) * 2 + c


def greet(peers):
    barrier = pltpu.get_barrier_semaphore()
    for peer in peers:
        pl.semaphore_signal(barrier, inc=1, device_id=peer, device_id_type=MESH)


def await_greetings(peers):
    pl.semaphore_wait(pltpu.get_barrier_semaphore(), len(peers))


def block_copy(way, m, octant, groups_a):
    rows = pl.ds(OCT_OFF[octant], OCT_LEN[octant])
    slot = m % 2
    source = way.stage.at[slot, :, rows]
    target = way.got.at[pl.ds(m * WINDOWS, WINDOWS), rows]
    if octant == 0:
        return pltpu.make_async_copy(source, target, way.arrived.at[m, 0])
    return pltpu.make_async_remote_copy(
        src_ref=source,
        dst_ref=target,
        send_sem=way.sent.at[slot, octant],
        recv_sem=way.arrived.at[m, octant],
        device_id=neighbour(octant, way.sign, groups_a),
        device_id_type=MESH,
    )


def send_blocks(way, m, groups_a):
    for octant in range(8):
        block_copy(way, m, octant, groups_a).start()


def wait_sent(way, m, groups_a):
    for octant in range(1, 8):
        block_copy(way, m, octant, groups_a).wait_send()


def wait_arrived(way, m, groups_a):
    block_copy(way, m, 0, groups_a).wait()
    for octant in range(1, 8):
        block_copy(way, m, octant, groups_a).wait_recv()


def first_forward(r, sc, m, i):
    w, st = sc, SimpleNamespace()
    stage = r.x_stage.at[m % 2, i]
    sc.pad[:, 0:WS] = r.tokens[i, 0]
    st.x = sc.pad[...].astype(F32)
    sc.xT[...] = sc.pad[...]
    places = r.places
    valid = (
        (places[0:1, :] < r.extent[0, 0, m * WINDOWS + i])
        & (places[1:2, :] < r.extent[1, 0, m * WINDOWS + i])
        & (places[2:3, :] < r.extent[2, 0, m * WINDOWS + i])
    )
    valid = jnp.where(valid, 1.0, 0.0)
    sc.codes[...] = jnp.broadcast_to(valid - 1.0, (128, T)).T
    yield 100
    yield from forward_attention(sc, w, st, jnp.zeros((1, T), F32))
    sc.cot[:, 0:WS] = r.cotangent[i, 0]
    stage[:, CA:] = jnp.concatenate(
        [dot(r.perm[...], sc.cot[...], NT), jnp.zeros((T, CA - C), F32)], axis=1
    ).astype(BF)
    yield 100
    x = st.x + st.branch
    sc.x1[...] = x
    second_norm(sc, w, x)
    yield 150
    for c in range(6):
        rows = slice(64 * c, 64 * c + 64)
        active, slope = gelu_pair(dot(w.upT[rows], sc.n2aug[...]))
        sc.act[rows, :] = active.astype(BF)
        sc.gp[rows, :] = slope.astype(BF)
        yield 100
    x = x + (dot(w.downT[...], sc.act[...]) + wide(w.vec[4]))
    yield 100
    row = lax.broadcasted_iota(jnp.int32, (CA - C, T), 0)
    label = r.volume[0, m * WINDOWS + i].astype(F32)
    extra = jnp.where(row == 0, label, jnp.where(row == 1, valid, 0.0))
    x = jnp.concatenate([x, extra], axis=0).astype(BF)
    stage[:, 0:CA] = dot(r.perm[...], x, NT).astype(BF)
    yield 100


def second_layer(r, sc, m, i, groups_a):
    w, st = sc, SimpleNamespace()
    stage = r.d_stage.at[m % 2, i]
    n = m * WINDOWS + i
    came = r.x_got[n, :, 0:CA]
    x = came.T.astype(F32)
    place, sizes = grid_place(groups_a)
    code_row = []
    for octant in range(8):
        rows = slice(OCT_OFF[octant], OCT_OFF[octant] + OCT_LEN[octant])
        wraps = [
            bit * jnp.where(p == n_ - 1, 1, 0)
            for p, bit, n_ in zip(place, octant_bits(octant), sizes)
        ]
        wrap = (wraps[0] * 4 + wraps[1] * 2 + wraps[2]).astype(F32)
        columns = came[rows].astype(F32)
        code = jnp.where(columns[:, C + 1 : C + 2] > 0.0, columns[:, C : C + 1] * 8.0 + wrap, -1.0)
        sc.codes[rows, :] = jnp.broadcast_to(code, (OCT_LEN[octant], 128))
        code_row.append(jnp.full((1, OCT_LEN[octant]), wrap))
    code_row = jnp.concatenate(code_row, axis=1) + 8.0 * x[C : C + 1]
    keep = x[C + 1 : C + 2]
    x = x[0:C]
    sc.xT[...] = x.astype(BF)
    st.x = x
    yield 150
    yield from forward_attention(sc, w, st, code_row)
    st.d = r.x_got[n, :, CA:].T[0:C].astype(F32) * keep
    dd = st.d.astype(BF)
    x = sc.xT[...].astype(F32) + st.branch.astype(BF).astype(F32)
    z, scale = second_norm(sc, w, x)
    yield 200
    for c in range(6):
        rows = slice(64 * c, 64 * c + 64)
        active, slope = gelu_pair(dot(w.upT[rows], sc.n2aug[...]))
        sc.act[rows, :] = active.astype(BF)
        sc.dh[rows, :] = (dot(w.down[rows], dd) * slope).astype(BF)
        yield 120
    x = x + (dot(w.downT[...], sc.act[...]) + wide(w.vec[4]))
    none = jnp.zeros((CA - C, T), F32)
    stage[:, 0:CA] = jnp.concatenate([x * keep, none], axis=0).T.astype(BF)
    yield 150
    yield from feed_forward_back(sc, w, st, dd, z, scale)
    z, scale = ln_stats(sc.xT[...].astype(F32))
    yield from backward_attention(sc, w, st, z, scale, True)
    stage[:, CA:] = jnp.concatenate([st.d, none], axis=0).T.astype(BF)
    yield 100


def first_backward(r, sc, m, i):
    w, st = sc, SimpleNamespace()
    came = r.d_got[m * WINDOWS + i].T
    came = jnp.concatenate([came[0:C], came[CA : CA + C]], axis=0)
    yield 200
    came = dot(came, r.perm[...])
    r.output[i, 0] = came[0:C, 0:WS].astype(BF)
    st.d = came[C : 2 * C]
    dd = st.d.astype(BF)
    z, scale = ln_stats(sc.x1[...])
    yield 200
    for c in range(3):
        rows = slice(128 * c, 128 * c + 128)
        sc.dh[rows, :] = (dot(w.down[rows], dd) * sc.gp[rows, :].astype(F32)).astype(BF)
        yield 50
    yield from feed_forward_back(sc, w, st, dd, z, scale)
    z, scale = ln_stats(sc.xT[...].astype(F32))
    yield from backward_attention(sc, w, st, z, scale, False)
    r.input_grad[i, 0] = st.d[:, 0:WS]
    yield 50


def layers_kernel(n_vol, n_plane, shard_len, steps, r):
    groups_a = n_plane // 2
    s = pl.program_id(0)
    forth = SimpleNamespace(
        stage=r.x_stage, got=r.x_got, sent=r.x_sent, arrived=r.x_arrived, sign=-1
    )
    back = SimpleNamespace(
        stage=r.d_stage, got=r.d_got, sent=r.d_sent, arrived=r.d_arrived, sign=1
    )

    far = all_peers(n_vol, n_plane)
    reduction = Reduction(r, far, n_vol, n_plane, shard_len)

    @pl.when(s == 0)
    def _():
        peers = far + [
            neighbour(octant, sign, groups_a) for sign in (1, -1) for octant in range(1, 8)
        ]
        greet(peers)
        for n in range(TABLE_SLOTS):
            table_copy(r, n).start()
        vol, plane, core = own_place()
        r.buf[core, plane, vol] = r.shard[...].astype(BF)
        clear_scratch(r)
        await_greetings(peers)
        meanwhile = (lambda: turn_tables(r, 0), lambda: turn_tables(r, 1), lambda: None)
        for copies, work in zip(gather_stages(r, far, n_vol, n_plane), meanwhile):
            for c in copies:
                c.start()
            work()
            for c in copies:
                c.wait()
        prepare(r, n_vol, n_plane, shard_len)

    @pl.when(s < steps)
    def _():
        @pl.when(s >= 2)
        def _():
            wait_sent(forth, s - 2, groups_a)

        windows = of_layer(r, 0, s % 3)
        weave([first_forward(r, sc, s, i) for i, sc in enumerate(windows)], LAG)
        send_blocks(forth, s, groups_a)

    @pl.when((s >= 1) & (s <= steps))
    def _():
        m = s - 1
        wait_arrived(forth, m, groups_a)

        @pl.when(m >= 2)
        def _():
            wait_sent(back, m - 2, groups_a)

        windows = of_layer(r, 1, 0)
        weave([second_layer(r, sc, m, i, groups_a) for i, sc in enumerate(windows)], LAG)
        send_blocks(back, m, groups_a)

    @pl.when(s == steps)
    def _():
        write_grads(of_layer(r, 1, 0)[0], r.grads.at[1])
        reduction.start_core(1)

    @pl.when(s == steps + 1)
    def _():
        reduction.start_plane(1)

    @pl.when(s >= 2)
    def _():
        m = s - 2
        wait_arrived(back, m, groups_a)
        windows = of_layer(r, 0, m % 3)
        weave([first_backward(r, sc, m, i) for i, sc in enumerate(windows)], LAG)

    @pl.when(s == steps + 1)
    def _():
        write_grads(of_layer(r, 0, 0)[0], r.grads.at[0])
        reduction.start_core(0)
        reduction.end_plane(1)
        reduction.start_vol(1)
        reduction.start_plane(0)
        for m in range(max(steps - 2, 0), steps):
            wait_sent(forth, m, groups_a)
            wait_sent(back, m, groups_a)
        reduction.end_plane(0)
        reduction.start_vol(0)
        reduction.finish()


def shard_rows(device, shard_len):
    return device * shard_len // C, -(-(device + 1) * shard_len // C)


def flat_offset(device, shard_len):
    return device * shard_len % C


def slab_rows(shard_len):
    return -(-((shard_len + C - 2) // C + 1) // 16) * 16


def own_place():
    win = lax.axis_index(WIN)
    return lax.axis_index(VOL), win // 2, win % 2


def all_peers(n_vol, n_plane):
    vol, plane, core = own_place()
    return (
        [((vol + j) % n_vol, plane * 2 + core) for j in range(1, n_vol)]
        + [(vol, (plane + j) % n_plane * 2 + core) for j in range(1, n_plane)]
        + [(vol, plane * 2 + 1 - core)]
    )


def transpose_with(matrix, extra):
    below = jnp.where(lax.broadcasted_iota(jnp.int32, (CA - C, C), 0) == 0, extra, 0.0)
    return jnp.concatenate([matrix, below], axis=0).T


def gather_stages(r, peers, n_vol, n_plane):
    vol, plane, core = own_place()

    def copy(ref, n):
        return pltpu.make_async_remote_copy(
            src_ref=ref,
            dst_ref=ref,
            send_sem=r.g_sent.at[n],
            recv_sem=r.g_arrived.at[n],
            device_id=peers[n],
            device_id_type=MESH,
        )

    return (
        [copy(r.buf.at[core, plane, vol], n) for n in range(n_vol - 1)],
        [copy(r.buf.at[core, plane], n_vol - 1 + n) for n in range(n_plane - 1)],
        [copy(r.buf.at[core], n_vol + n_plane - 2)],
    )


def prepare(r, n_vol, n_plane, shard_len):
    buf = r.buf
    flat = r.grads
    flat[...] = jnp.zeros(flat.shape, F32)
    half = n_vol * n_plane
    for v in range(n_vol):
        for p in range(n_plane):
            for c in range(2):
                device = (v * n_plane + p) * 2 + c
                start, stop = shard_rows(device % half, shard_len)
                flat[device // half, start:stop, :] += buf[c, p, v, 0 : stop - start].astype(F32)
    for layer in range(2):

        def rows(start, count=C, stride=1):
            return flat[layer, pl.ds(start, count, stride), :]

        def vector(n):
            return rows(12 * C + n, 1)

        o = SimpleNamespace(**{n: getattr(r, n).at[layer] for n in WEIGHTS})
        none = jnp.zeros((1, C), F32)
        wq, wk, wv = (rows(n, C, 3) for n in range(3))
        o.q[...] = wq.astype(BF)
        o.kv96[...] = jnp.concatenate([wk, wv], axis=1).astype(BF)
        o.qkvT[0:C, :] = (transpose_with(wq, vector(2)) * 0.25).astype(BF)
        o.qkvT[C : 2 * C, :] = (transpose_with(wk, none) * 0.25).astype(BF)
        o.qkvT[2 * C :, :] = transpose_with(wv, vector(3)).astype(BF)
        row = lax.broadcasted_iota(jnp.int32, (CA - C, CA), 0)
        lane = lax.broadcasted_iota(jnp.int32, (CA - C, CA), 1)
        blank = jnp.zeros((C, CA - C), F32)
        bias_v = jnp.concatenate([vector(3), blank[0:1]], axis=1)
        ones = jnp.where((lane == C) | (lane == C + 1), 1.0, bias_v)
        o.kv[0:C, :] = jnp.concatenate([wk, blank, wv, blank], axis=1).astype(BF)
        o.kv[C:, 0:CA] = jnp.zeros((CA - C, CA), BF)
        o.kv[C:, CA:] = jnp.where(row == 0, ones, 0.0).astype(BF)
        proj = rows(3 * C)
        o.proj[...] = proj.astype(BF)
        o.projT[...] = transpose_with(proj, vector(4)).astype(BF)
        ups = [rows(4 * C + j, C, 4) for j in range(4)]
        o.up[...] = jnp.concatenate(ups, axis=1).astype(BF)
        for j in range(4):
            o.upT[C * j : C * j + C, :] = transpose_with(ups[j], vector(8 + j)).astype(BF)
        down = rows(8 * C, FF)
        o.down[...] = down.astype(BF)
        o.downT[...] = down.T.astype(BF)
        for n, source in enumerate((0, 1, 5, 6, 7)):
            o.vec[n] = jnp.broadcast_to(vector(source), (128, C)).T


class Reduction:
    def __init__(self, r, peers, n_vol, n_plane, shard_len):
        self.r, self.peers, self.shard_len = r, peers, shard_len
        self.n_vol, self.n_plane, self.half = n_vol, n_plane, n_vol // 2
        self.vol, self.plane, self.core = own_place()

    def vols(self, layer):
        return pl.ds(layer * self.half, self.half)

    def copy(self, source, target, peer, n):
        return pltpu.make_async_remote_copy(
            src_ref=source,
            dst_ref=target,
            send_sem=self.r.r_sent.at[n],
            recv_sem=self.r.r_arrived.at[n],
            device_id=self.peers[peer],
            device_id_type=MESH,
        )

    def over_core(self, layer):
        source = self.r.work.at[1 - self.core, :, self.vols(layer)]
        return [self.copy(source, self.r.from_core.at[layer], len(self.peers) - 1, layer)]

    def over_plane(self, layer):
        return [
            self.copy(
                self.r.wire.at[(self.plane + j) % self.n_plane, self.vols(layer)],
                self.r.from_plane.at[layer, j - 1],
                self.n_vol - 2 + j,
                2 + layer * (self.n_plane - 1) + j - 1,
            )
            for j in range(1, self.n_plane)
        ]

    def over_vol(self):
        return [
            self.copy(
                self.r.wire.at[self.plane, (self.vol + j) % self.n_vol],
                self.r.from_vol.at[j - 1],
                j - 1,
                2 * self.n_plane + j - 1,
            )
            for j in range(1, self.n_vol)
        ]

    def start_core(self, layer):
        for v in range(layer * self.half, (layer + 1) * self.half):
            for p in range(self.n_plane):
                for c in range(2):
                    device = (v % self.half * self.n_plane + p) * 2 + c
                    start, stop = shard_rows(device, self.shard_len)
                    self.r.work[c, p, v, 0 : stop - start] = self.r.grads[layer, start:stop, :]
        for c in self.over_core(layer):
            c.start()

    def start_plane(self, layer):
        for c in self.over_core(layer):
            c.wait()
        vols, work = self.vols(layer), self.r.work
        total = work[self.core, :, vols] + self.r.from_core[layer]
        work[self.core, :, vols] = total
        self.r.wire[:, vols] = total.astype(BF)
        for c in self.over_plane(layer):
            c.start()

    def end_plane(self, layer):
        for c in self.over_plane(layer):
            c.wait()
        vols, work = self.vols(layer), self.r.work
        total = work[self.core, self.plane, vols]
        for j in range(self.n_plane - 1):
            total = total + self.r.from_plane[layer, j].astype(F32)
        work[self.core, self.plane, vols] = total
        self.r.wire[self.plane, vols] = total.astype(BF)

    def start_vol(self, layer):
        for j, c in enumerate(self.over_vol(), 1):
            target = (self.vol + j) % self.n_vol

            @pl.when(target // self.half == layer)
            def _():
                c.start()

    def finish(self):
        for c in self.over_vol():
            c.wait()
        total = self.r.work[self.core, self.plane, self.vol]
        for j in range(self.n_vol - 1):
            total = total + self.r.from_vol[j].astype(F32)
        self.r.total[...] = total


def call(kernel, steps, ins, outs, scratch, semaphores=(), collective_id=None, lag=0):
    def spec(shape, kind, late):
        if kind in (SMEM, HBM):
            return pl.BlockSpec(memory_space=pltpu.SMEM if kind is SMEM else pl.ANY)
        zeros = (0,) * (len(shape) - 1)
        if kind is BY_STEP:

            def index(s):
                return (jnp.clip(s - late, 0, steps - 1),) + zeros

            return pl.BlockSpec((shape[0] // steps,) + tuple(shape[1:]), index)
        return pl.BlockSpec(
            tuple(shape), lambda s: (0,) + zeros, pipeline_mode=None if late else pl.Buffered(1)
        )

    semaphores = dict(semaphores)
    names = tuple(ins) + tuple(outs) + tuple(scratch) + tuple(semaphores)

    def body(*refs):
        kernel(SimpleNamespace(**dict(zip(names, refs))))

    results = pl.pallas_call(
        body,
        grid=(steps + lag,),
        in_specs=[spec(a.shape, kind, 0) for a, kind in ins.values()],
        out_specs=[spec(shape, kind, lag) for shape, _, kind in outs.values()],
        out_shape=[jax.ShapeDtypeStruct(shape, dtype) for shape, dtype, _ in outs.values()],
        scratch_shapes=[pltpu.VMEM(shape, dtype) for shape, dtype in scratch.values()]
        + [pltpu.SemaphoreType.DMA(shape) for shape in semaphores.values()],
        compiler_params=pltpu.CompilerParams(
            vmem_limit_bytes=62 * 2**20,
            collective_id=collective_id,
            has_side_effects=collective_id is not None,
        ),
    )(*[a for a, _ in ins.values()])
    return SimpleNamespace(**dict(zip(outs, results)))


def on_device(
    tokens,
    cotangent,
    position_bias,
    window_volume,
    clip_extent,
    master,
    first_moment,
    second_moment,
):
    n_vol, n_win = lax.axis_size(VOL), lax.axis_size(WIN)
    n_plane = n_win // 2
    count = tokens.shape[0]
    steps = count // WINDOWS
    shard_len = master.shape[0]
    device = lax.axis_index((VOL, WIN))
    slab = slab_rows(shard_len)
    offset = flat_offset(device, shard_len)
    shard = lax.dynamic_update_slice(jnp.zeros((slab * C,), F32), master, (offset,))
    n_peers = n_vol + n_plane - 1

    def each(table, *sizes):
        return {n: (sizes + shape, dtype) for n, (shape, dtype) in table.items()}

    def kept(layer, slots):
        shapes = dict(KEPT, e=((ROWS[layer], HEADS * T), BF))
        shapes = dict(shapes, gp=((16, T), BF)) if layer else shapes
        return {name + n: v for name in KEPT_NAMES[layer] for n, v in each(shapes, slots).items()}

    stage, landing = ((2, WINDOWS, T, 2 * CA), BF), ((count, T, 2 * CA), BF)
    layers = call(
        lambda r: layers_kernel(n_vol, n_plane, shard_len, steps, r),
        steps,
        dict(
            tokens=(tokens.transpose(0, 1, 3, 2), BY_STEP),
            cotangent=(cotangent.transpose(0, 1, 3, 2), BY_STEP),
            volume=(window_volume.T, SMEM),
            extent=(clip_extent.transpose(2, 1, 0), SMEM),
            perm=(jnp.asarray(PERM, BF), WHOLE),
            places=(jnp.asarray(PLACES), WHOLE),
            order=(jnp.asarray(np.stack([np.eye(T, WS), ORDER]), BF), WHOLE),
            table=(position_bias, HBM),
            shard=(shard.reshape(slab, C), WHOLE),
        ),
        dict(
            output=((count, 1, C, WS), BF, BY_STEP),
            input_grad=((count, 1, C, WS), F32, BY_STEP),
            total=((slab, C), F32, WHOLE),
        ),
        dict(
            **each(FWD, WINDOWS),
            **each(BWD, WINDOWS),
            **each(PADS, WINDOWS),
            **each(GRADS, 2),
            **each(BIAS, 2),
            **kept(0, 3),
            **kept(1, 1),
            **each(WEIGHTS, 2),
            page=((TABLE_SLOTS, WS, WS), BF),
            buf=((2, n_plane, n_vol, slab, C), BF),
            grads=((2, BLOCK_ROWS, C), F32),
            work=((2, n_plane, n_vol, slab, C), F32),
            wire=((n_plane, n_vol, slab, C), BF),
            from_core=((2, n_plane, n_vol // 2, slab, C), F32),
            from_plane=((2, n_plane - 1, n_vol // 2, slab, C), BF),
            from_vol=((n_vol - 1, slab, C), BF),
            x_stage=stage,
            d_stage=stage,
            x_got=landing,
            d_got=landing,
        ),
        dict(
            x_sent=(2, 8),
            x_arrived=(steps, 8),
            d_sent=(2, 8),
            d_arrived=(steps, 8),
            g_sent=(n_peers,),
            g_arrived=(n_peers,),
            turned=(TABLE_SLOTS,),
            r_sent=(2 * n_plane + n_vol - 1,),
            r_arrived=(2 * n_plane + n_vol - 1,),
        ),
        collective_id=1,
        lag=2,
    )
    shard_grad = lax.dynamic_slice(layers.total.reshape(-1), (offset,), (shard_len,))
    position = (device * shard_len + jnp.arange(shard_len, dtype=jnp.int32)) % (BLOCK_ROWS * C)
    is_vector = position >= 12 * C * C
    step_rate = jnp.where(is_vector, RATE_VECTOR, RATE_MATRIX)
    weight_decay = jnp.where(is_vector, 0.0, DECAY_MATRIX)
    moment_one = BETA_FIRST * first_moment + (1.0 - BETA_FIRST) * shard_grad
    moment_two = BETA_SECOND * second_moment + (1.0 - BETA_SECOND) * shard_grad * shard_grad
    corrected_one = moment_one / (1.0 - BETA_FIRST**STEP)
    corrected_two = moment_two / (1.0 - BETA_SECOND**STEP)
    normalized = corrected_one / (jnp.sqrt(corrected_two) + ADAM_EPS)
    new_master = master - step_rate * (normalized + weight_decay * master)
    return (
        layers.output.transpose(0, 1, 3, 2),
        layers.input_grad.transpose(0, 1, 3, 2),
        new_master,
        moment_one,
        moment_two,
        new_master.astype(BF),
    )


def solution(mesh):
    placed = (
        P(None, (VOL, WIN), None, None),
        P(None, (VOL, WIN), None, None),
        P(),
        P(None, (VOL, WIN)),
        P(None, (VOL, WIN), None),
        P((VOL, WIN)),
        P((VOL, WIN)),
        P((VOL, WIN)),
    )
    return jax.shard_map(
        on_device,
        mesh=mesh,
        in_specs=placed,
        out_specs=(
            P(None, (VOL, WIN), None, None),
            P(None, (VOL, WIN), None, None),
            P((VOL, WIN)),
            P((VOL, WIN)),
            P((VOL, WIN)),
            P((VOL, WIN)),
        ),
        check_vma=False,
    )
```
